256 devices in a mesh: strip: 16 (over x, y_lo, core), vec: 16 (over y_hi, z).
Axes of the slice: x: 4, y: 4 (y_hi: 2, y_lo: 2; y = y_hi * 2 + y_lo), z: 8, core: 2. Of those that a mesh axis runs over, the one named last changes fastest.
Arguments:
- start_vectors: float32 [64, 512, 1024], P('vec', 'strip'), may hold values from -40 to 40
- potential: int32 [512, 1024], P('strip'), may hold values from 0 to 15
- bounds: int32 [4], replicated, may hold values from -96 to 96, as said below
Outputs:
- ortho_basis: float32 [64, 512, 1024], P('vec', 'strip')
- ritz_matrix: float32 [64, 64], replicated
The draws below stay inside these ranges and needn't reach their ends.
Inputs may be any that keep to these rules, and one draw needn't show every extreme that they name: bounds[0] and bounds[1] enclose the spectrum of H: bounds[0] is at most -84 and bounds[1] at least 84; bounds[0] < bounds[2] < bounds[3] < bounds[1].
All inputs are finite; a program needn't handle non-finite values.
Results may differ from the reference program's by a relative error of at most 0.00021.
Values sent between devices are 32-bit elements; how exact they have to be, the bound alone decides.
A program may use at most 64 MiB of HBM per device.

```python
import math
import jax
import jax.numpy as jnp
from jax import lax

NVEC = 64
ROWS_DEV = 32
LY = 1024
DEGREE = 32
POT_LEVELS = 16
LX = 512
SITES = 524288


def draw_start_vectors(key, part):
    first_key = jax.random.fold_in(jax.random.fold_in(key, 11), 0)
    base = jax.random.truncated_normal(first_key, -4.0, 4.0, (NVEC, LX, LY), jnp.float32)
    mixed = base + 0.5 * jnp.roll(base, -1, 0) + 0.3 * jnp.roll(base, -7, 0)
    row_scale = 3.0 ** (jnp.arange(LX).astype(jnp.float32) / max(LX - 1, 1))
    return (mixed * row_scale[None, :, None]).astype(jnp.float32)


def draw_bounds(key, part):
    base_key = jax.random.fold_in(key, 23)
    keys = jax.random.split(base_key, 4)
    enclose_lo = jax.random.randint(keys[0], (), -96, -83)
    enclose_hi = jax.random.randint(keys[1], (), 84, 97)
    window_lo = jax.random.randint(keys[2], (), -40, -8)
    window_hi = window_lo + jax.random.randint(keys[3], (), 16, 49)
    return jnp.stack([enclose_lo, enclose_hi, window_lo, window_hi]).astype(jnp.int32)


def plant(entries, rng, least, high):
    longest = entries.shape.index(max(entries.shape))
    spots = []
    for shift in (0, 1):
        where = [jax.random.randint(jax.random.fold_in(rng, axis), (), 0, length) for axis, length in enumerate(entries.shape)]
        where[longest] = (where[longest] + shift) % entries.shape[longest]
        spots.append(tuple(where))
    return entries.at[spots[0]].set(least).at[spots[1]].set(high)


def setup_inputs(seed: int = 0) -> dict:
    arg_keys = jax.random.split(jax.random.key(seed), 4)
    return {
        "start_vectors": draw_start_vectors(jax.random.fold_in(arg_keys[3], 71), 0),
        "potential": plant(jax.random.randint(arg_keys[1], (LX, LY), 0, POT_LEVELS), jax.random.fold_in(arg_keys[1], 1), 0, POT_LEVELS - 1).astype(jnp.int32),
        "bounds": draw_bounds(jax.random.fold_in(arg_keys[3], 71), 0),
    }


grid_unit = 0.0625
disorder = 2.0

def filter_terms(bounds):
    edges = bounds.astype(jnp.float32) * grid_unit
    center = (edges[0] + edges[1]) * 0.5
    spread = (edges[1] - edges[0]) * 0.5
    theta_lo = jnp.arccos((edges[2] - center) / spread)
    theta_hi = jnp.arccos((edges[3] - center) / spread)
    orders = jnp.arange(1, DEGREE + 1).astype(jnp.float32)
    others = 2.0 * (jnp.sin(orders * theta_lo) - jnp.sin(orders * theta_hi)) / (orders * math.pi)
    first = jnp.reshape((theta_lo - theta_hi) / math.pi, (1,))
    return (jnp.concatenate([first, others]), center, spread)

def hamiltonian(field, pot_field):
    beside = jnp.roll(field, 1, 1) + jnp.roll(field, -1, 1) + jnp.roll(field, 1, 2) + jnp.roll(field, -1, 2)
    return pot_field[None] * field - beside

def reference(start_vectors, potential, bounds):
    pot_field = disorder * (potential.astype(jnp.float32) / (POT_LEVELS - 1) - 0.5)
    coeffs, center, spread = filter_terms(bounds)

    def scaled(field):
        return (hamiltonian(field, pot_field) - center * field) / spread
    before = start_vectors
    current = scaled(start_vectors)
    filtered = coeffs[0] * before + coeffs[1] * current

    def advance(counter, carry):
        before, current, filtered = carry
        after = 2.0 * scaled(current) - before
        filtered = filtered + coeffs[counter + 1] * after
        return (current, after, filtered)
    before, current, filtered = lax.fori_loop(1, DEGREE, advance, (before, current, filtered))
    applied = hamiltonian(filtered, pot_field)
    y_rows = filtered.reshape(NVEC, -1)
    hy_rows = applied.reshape(NVEC, -1)
    gram_sum = jnp.dot(y_rows.astype(jnp.float32), y_rows.T.astype(jnp.float32), precision=lax.Precision.HIGHEST, preferred_element_type=jnp.float32)
    cross_sum = jnp.dot(y_rows.astype(jnp.float32), hy_rows.T.astype(jnp.float32), precision=lax.Precision.HIGHEST, preferred_element_type=jnp.float32)
    lower_factor = jnp.linalg.cholesky(gram_sum)
    ortho = jax.scipy.linalg.solve_triangular(lower_factor, y_rows, lower=True)
    ortho_basis = (math.sqrt(SITES) * ortho).reshape(NVEC, LX, LY)
    half_done = jax.scipy.linalg.solve_triangular(lower_factor, cross_sum, lower=True)
    ritz_matrix = float(ROWS_DEV) * jax.scipy.linalg.solve_triangular(lower_factor, half_done.T, lower=True)
    return (ortho_basis, ritz_matrix)
```

```python
import math

import jax
import jax.numpy as jnp
from jax import lax
from jax.experimental import pallas as pl
from jax.experimental.pallas import tpu as pltpu
from jax.sharding import PartitionSpec as P

DEGREE = 32
POT_LEVELS = 16
NQ = 4
ROWS = 32
NV = 16
NS = 16
NVEC = NQ * NV
PIECE = ROWS // NV
SUB = 8
CHUNKS = PIECE * SUB
HALO = CHUNKS + SUB
FIELD = (2 * ROWS + ROWS + 1) * SUB
OWN = ROWS * SUB
SITES = NS * ROWS * 1024

grid_unit = 0.0625
disorder = 2.0
F32 = jnp.float32
BF16 = jnp.bfloat16


def filter_terms(bounds):
    edges = bounds.astype(F32) * grid_unit
    center = (edges[0] + edges[1]) * 0.5
    spread = (edges[1] - edges[0]) * 0.5
    theta_lo = jnp.arccos((edges[2] - center) / spread)
    theta_hi = jnp.arccos((edges[3] - center) / spread)
    orders = jnp.arange(1, DEGREE + 1).astype(F32)
    others = 2.0 * (jnp.sin(orders * theta_lo) - jnp.sin(orders * theta_hi)) / (orders * math.pi)
    first = jnp.reshape((theta_lo - theta_hi) / math.pi, (1,))
    return jnp.concatenate([first, others, jnp.stack([2.0 / spread, center])])


def remote(src, dst, send, recv, **where):
    return pltpu.make_async_remote_copy(
        src_ref=src, dst_ref=dst, send_sem=send, recv_sem=recv,
        device_id=where, device_id_type=pl.DeviceIdType.MESH,
    )


def wait_bytes(ref, sem):
    pltpu.make_async_copy(ref, ref, sem).wait()


def split(value):
    high = value.astype(BF16)
    return high, (value - high.astype(F32)).astype(BF16)


def kernel(
    co, x_ref, pot_ref, out_ref, ritz_ref,
    even, odd, filt, diag, pot_own, slab, ops, gm, scattered, summed, total, ortho, fields,
    pot_send, pot_recv, ghost_send, ghost_recv, vec_send, vec_recv, small_send, small_recv, back_send, back_recv,
):
    s = lax.axis_index("strip")
    v = lax.axis_index("vec")

    barrier = pltpu.get_barrier_semaphore()

    def greet(j, carry):
        pl.semaphore_signal(barrier, inc=1, device_id={"vec": lax.rem(v + j, NV)}, device_id_type=pl.DeviceIdType.MESH)
        pl.semaphore_signal(barrier, inc=1, device_id={"strip": lax.rem(s + j, NS)}, device_id_type=pl.DeviceIdType.MESH)
        return carry

    lax.fori_loop(1, NV, greet, 0)

    scale = co[33]
    center = co[34]
    for r in range(ROWS // 8):
        for t in range(SUB):
            level = pot_ref[8 * r:8 * r + 8, 128 * t:128 * t + 128].astype(F32)
            field = disorder * (level / (POT_LEVELS - 1) - 0.5)
            pot_own[pl.ds(64 * r + t, 8, stride=8), :] = field
            diag[pl.ds(OWN + 64 * r + t, 8, stride=8), :] = (field - center) * scale

    for q in range(NQ):
        for r in range(ROWS // 8):
            for t in range(SUB):
                tile = x_ref[q, 8 * r:8 * r + 8, 128 * t:128 * t + 128]
                even[q, pl.ds(OWN + 64 * r + t, 8, stride=8), :] = 0.5 * tile

    pl.semaphore_wait(barrier, NV + NS - 2)

    up = lax.rem(s + NS - 1, NS)
    down = lax.rem(s + 1, NS)
    up2 = lax.rem(s + NS - 2, NS)

    def pot_copies():
        mine = diag.at[pl.ds(OWN, OWN)]
        return (
            remote(mine, diag.at[pl.ds(2 * OWN, OWN)], pot_send.at[0], pot_recv.at[0], strip=up),
            remote(mine, diag.at[pl.ds(0, OWN)], pot_send.at[1], pot_recv.at[1], strip=down),
        )

    def ghost_copies(q):
        mine = even.at[q, pl.ds(OWN, OWN)]
        return (
            remote(mine, even.at[q, pl.ds(2 * OWN, OWN)], ghost_send.at[q, 0], ghost_recv.at[q, 0], strip=up),
            remote(mine, even.at[q, pl.ds(0, OWN)], ghost_send.at[q, 1], ghost_recv.at[q, 1], strip=down),
            remote(
                even.at[q, pl.ds(OWN, SUB)], even.at[q, pl.ds(3 * OWN, SUB)],
                ghost_send.at[q, 2], ghost_recv.at[q, 2], strip=up2,
            ),
        )

    for copy in pot_copies():
        copy.start()

    def start_ghosts(q, carry):
        for copy in ghost_copies(q):
            copy.start()
        return carry

    lax.fori_loop(0, NQ, start_ghosts, 0)

    lane = lax.broadcasted_iota(jnp.int32, (1, 8, 128), 2)
    first_lane = lane == 0
    last_lane = lane == 127

    def update(q, step, low, high, double, c_now, c_next, accumulate):
        now, then = ((even, odd), (odd, even))[step]
        rows = high - low
        shape = (rows, 8, 128)
        above = now[q, (low - 1) * 8:(high - 1) * 8].reshape(shape)
        mid = now[q, low * 8:high * 8].reshape(shape)
        below = now[q, (low + 1) * 8:(high + 1) * 8].reshape(shape)
        ahead = pltpu.roll(mid, 1, 2)
        behind = pltpu.roll(mid, 127, 2)
        beside = jnp.where(first_lane, pltpu.roll(ahead, 1, 1), ahead) + jnp.where(
            last_lane, pltpu.roll(behind, 7, 1), behind
        )
        before = then[q, low * 8:high * 8].reshape(shape)
        if step == 1:
            before = before * double
        after = (diag[low * 8:high * 8].reshape(shape) * mid - before) - scale * ((above + below) + beside)
        then[q, low * 8:high * 8] = after.reshape(rows * 8, 128)
        if accumulate:
            place = slice((low - ROWS) * 8, (high - ROWS) * 8)
            term = (c_now * mid + c_next * after).reshape(rows * 8, 128)
            filt[q, place] = filt[q, place] + term

    def vec_copy(q, j):
        peer = lax.rem(v + j, NV)
        return remote(
            filt.at[q, pl.ds(peer * CHUNKS, HALO)], slab.at[pl.ds((v * NQ + q) * HALO, HALO)],
            vec_send.at[q], vec_recv.at[q], vec=peer,
        )

    for copy in pot_copies():
        copy.wait()

    def one_vector(q, carry):
        for copy in ghost_copies(q):
            copy.wait()
        odd[q] = jnp.zeros((FIELD, 128), F32)
        filt[q] = (2.0 * co[0]) * even[q, OWN:2 * OWN + SUB]
        for block in range(4):
            low, high = 8 * block + 1, 96 - 8 * block

            def pair(i, inner, block=block, low=low, high=high):
                k = 8 * block + 2 * i + 1
                double = jnp.where(k == 1, 2.0, 1.0).astype(F32)
                for step in range(2):
                    update(q, step, low, ROWS, double, 0.0, 0.0, False)
                    update(q, step, ROWS, 2 * ROWS + 1, double, co[k], co[k + 1], step == 1)
                    update(q, step, 2 * ROWS + 1, high, double, 0.0, 0.0, False)
                return inner

            lax.fori_loop(0, 4, pair, 0)
        slab[pl.ds((v * NQ + q) * HALO, HALO)] = filt[q, pl.ds(v * CHUNKS, HALO)]

        def send(j, inner):
            vec_copy(q, j).start()
            return inner

        lax.fori_loop(1, NV, send, 0)
        return carry

    lax.fori_loop(0, NQ, one_vector, 0)
    for q in range(NQ):
        wait_bytes(slab.at[pl.ds(0, (NV - 1) * HALO)], vec_recv.at[q])

    lane2 = lax.broadcasted_iota(jnp.int32, (16, 128), 1)
    pot_slab = pot_own[pl.ds(v * CHUNKS, CHUNKS)] * 0.5

    for g in range(NVEC // 16):
        def chunk(n, g=g):
            base = 16 * g * HALO + n
            return jnp.concatenate(
                [slab[pl.ds(base, 8, stride=HALO), :], slab[pl.ds(base + 8 * HALO, 8, stride=HALO), :]], axis=0
            )

        y = [chunk(n) for n in range(HALO)]
        turned = [pltpu.roll(y[n], 127, 1) for n in range(CHUNKS)]
        for n in range(CHUNKS):
            follow = n // SUB * SUB + (n + 1) % SUB
            right = jnp.where(lane2 == 127, turned[follow], turned[n])
            z = pot_slab[n:n + 1] * y[n] - (right + y[n + SUB])
            for part, value in enumerate(split(y[n]) + split(z)):
                ops[64 * part + 16 * g:64 * part + 16 * g + 16, 128 * n:128 * n + 128] = value
    prod = lax.dot_general(
        ops[...], ops[0:128, :], (((1,), (1,)), ((), ())), preferred_element_type=F32
    )
    gm[0:64] = prod[0:64] + prod[64:128]
    gm[64:128] = prod[128:192] + prod[192:256]

    def to_all(stage, count, axis, me, source, target):
        def send(j, carry):
            peer = lax.rem(me + j, count)
            remote(source(peer), target, small_send.at[stage], small_recv.at[stage], **{axis: peer}).start()
            return carry

        lax.fori_loop(1, count, send, 0)

    mine_v = pl.ds(v * 8, 8)
    mine_s = pl.ds(s * 8, 8)
    scattered[mine_v] = gm[mine_v]
    to_all(0, NV, "vec", v, lambda peer: gm.at[pl.ds(peer * 8, 8)], scattered.at[mine_v])
    wait_bytes(scattered.at[pl.ds(0, 8 * (NV - 1))], small_recv.at[0])
    summed[mine_s] = jnp.sum(scattered[...].reshape(NV, 8, 128), axis=0)
    to_all(1, NS, "strip", s, lambda peer: summed.at[mine_s], summed.at[mine_s])
    wait_bytes(summed.at[pl.ds(0, 8 * (NS - 1))], small_recv.at[1])
    total[mine_v] = jnp.sum(summed[...].reshape(NS, 8, 128), axis=0)
    to_all(2, NV, "vec", v, lambda peer: total.at[mine_v], total.at[mine_v])
    wait_bytes(total.at[pl.ds(0, 8 * (NV - 1))], small_recv.at[2])

    rows64 = lax.broadcasted_iota(jnp.int32, (64, 128), 0)
    lanes64 = lax.broadcasted_iota(jnp.int32, (64, 128), 1)
    gram = total[0:64]
    gram = gram + pltpu.roll(gram, 64, 1)
    aug = jnp.where(lanes64 < 64, gram, jnp.where(lanes64 - 64 == rows64, 1.0, 0.0))
    for k in range(NVEC):
        column = aug[:, k:k + 1] / aug[k:k + 1, k:k + 1]
        factor = jnp.where(rows64 > k, jnp.broadcast_to(column, (64, 128)), 0.0)
        aug = aug - factor * aug[k:k + 1, :]
    pivots = jnp.sum(jnp.where(rows64 == lanes64, aug, 0.0), axis=1, keepdims=True)
    inverse = (pltpu.roll(aug, 64, 1) * lax.rsqrt(pivots))[:, 0:64]

    high, low = split(math.sqrt(SITES) * inverse)
    left = jnp.concatenate(
        [jnp.concatenate([high, high], axis=1), jnp.concatenate([low, low], axis=1)], axis=0
    )
    product = jnp.dot(left, ops[0:128, :], preferred_element_type=F32)
    for n in range(CHUNKS):
        value = product[0:64, 128 * n:128 * n + 128] + product[64:128, 128 * n:128 * n + 128]
        for g in range(8):
            ortho[pl.ds(n + 8 * g * CHUNKS, 8, stride=CHUNKS), :] = value[8 * g:8 * g + 8]

    def back_copy(j, q):
        peer = lax.rem(v + j, NV)
        return remote(
            ortho.at[pl.ds((peer * NQ + q) * CHUNKS, CHUNKS)], fields.at[q, pl.ds(v * CHUNKS, CHUNKS)],
            back_send.at[0], back_recv.at[0], vec=peer,
        )

    def send_back(j, carry):
        for q in range(NQ):
            back_copy(j, q).start()
        return carry

    lax.fori_loop(1, NV, send_back, 0)
    for q in range(NQ):
        fields[q, pl.ds(v * CHUNKS, CHUNKS)] = ortho[pl.ds((v * NQ + q) * CHUNKS, CHUNKS)]

    cross = total[64:128, 0:64] + total[64:128, 64:128]
    cross = cross + cross.T
    half = jnp.dot(inverse, cross, precision=lax.Precision.HIGHEST, preferred_element_type=F32)
    ritz_ref[...] = float(ROWS) * lax.dot_general(
        inverse, half, (((1,), (1,)), ((), ())), precision=lax.Precision.HIGHEST, preferred_element_type=F32
    )

    wait_bytes(ortho.at[pl.ds(0, (NV - 1) * NQ * CHUNKS)], back_recv.at[0])
    for q in range(NQ):
        for r in range(ROWS // 8):
            for t in range(SUB):
                out_ref[q, 8 * r:8 * r + 8, 128 * t:128 * t + 128] = fields[q, pl.ds(64 * r + t, 8, stride=8), :]

    wait_bytes(ortho.at[pl.ds(0, (NV - 1) * NQ * CHUNKS)], back_send.at[0])
    for stage in range(3):
        wait_bytes(total.at[pl.ds(0, 8 * (NV - 1))], small_send.at[stage])
    for q in range(NQ):
        wait_bytes(slab.at[pl.ds(0, (NV - 1) * HALO)], vec_send.at[q])


def shards(start_vectors, potential, bounds):
    terms = filter_terms(bounds)
    vmem = pl.BlockSpec(memory_space=pltpu.VMEM)
    dma = pltpu.SemaphoreType.DMA
    return pl.pallas_call(
        kernel,
        out_shape=(
            jax.ShapeDtypeStruct((NQ, ROWS, 1024), F32),
            jax.ShapeDtypeStruct((NVEC, NVEC), F32),
        ),
        in_specs=[pl.BlockSpec(memory_space=pltpu.SMEM), vmem, vmem],
        out_specs=(vmem, vmem),
        scratch_shapes=[
            pltpu.VMEM((NQ, FIELD, 128), F32),
            pltpu.VMEM((NQ, FIELD, 128), F32),
            pltpu.VMEM((NQ, OWN + SUB, 128), F32),
            pltpu.VMEM((FIELD, 128), F32),
            pltpu.VMEM((OWN, 128), F32),
            pltpu.VMEM((NVEC * HALO, 128), F32),
            pltpu.VMEM((256, CHUNKS * 128), BF16),
            pltpu.VMEM((128, 128), F32),
            pltpu.VMEM((128, 128), F32),
            pltpu.VMEM((128, 128), F32),
            pltpu.VMEM((128, 128), F32),
            pltpu.VMEM((NVEC * CHUNKS, 128), F32),
            pltpu.VMEM((NQ, OWN, 128), F32),
            dma((2,)), dma((2,)), dma((NQ, 3)), dma((NQ, 3)), dma((NQ,)), dma((NQ,)),
            dma((3,)), dma((3,)), dma((1,)), dma((1,)),
        ],
        compiler_params=pltpu.CompilerParams(
            collective_id=0, has_side_effects=True, vmem_limit_bytes=40 << 20
        ),
        name="filter_ritz",
    )(terms, start_vectors, potential)


def solution(mesh):
    in_specs = (P("vec", "strip", None), P("strip", None), P())
    out_specs = (P("vec", "strip", None), P())
    return jax.shard_map(shards, mesh=mesh, in_specs=in_specs, out_specs=out_specs, check_vma=False)
```

```python
import math

import jax
import jax.numpy as jnp
from jax import lax
from jax.experimental import pallas as pl
from jax.experimental.pallas import tpu as pltpu
from jax.sharding import PartitionSpec as P

DEGREE = 32
POT_LEVELS = 16
NQ = 4
ROWS = 32
NV = 16
NS = 16
NVEC = NQ * NV
PIECE = ROWS // NV
SUB = 8
CHUNKS = PIECE * SUB
HALO = CHUNKS + SUB
FIELD = (3 * ROWS + 1) * SUB
PAIRS = 3 * ROWS // 2 + 1
NA = 8
NB = 32
OWN = ROWS * SUB
HALF_PI = math.pi / 2
SITES = NS * ROWS * 1024

grid_unit = 0.0625
disorder = 2.0
F32 = jnp.float32
BF16 = jnp.bfloat16


def remote(src, dst, send, recv, **where):
    return pltpu.make_async_remote_copy(
        src_ref=src, dst_ref=dst, send_sem=send, recv_sem=recv,
        device_id=where, device_id_type=pl.DeviceIdType.MESH,
    )


def wait_bytes(ref, sem):
    pltpu.make_async_copy(ref, ref, sem).wait()


def split(value):
    high = value.astype(BF16)
    return high, (value - high.astype(F32)).astype(BF16)


def arccos(x):
    size = jnp.abs(x)
    large = size > 0.5
    square = jnp.where(large, 0.5 * (1.0 - size), x * x)
    base = jnp.where(large, jnp.sqrt(square), size)
    poly = 4.2163199048e-2 * square + 2.4181311049e-2
    poly = poly * square + 4.5470025998e-2
    poly = poly * square + 7.4953002686e-2
    poly = poly * square + 1.6666752422e-1
    arcsin = base + base * square * poly
    positive = jnp.where(large, 2.0 * arcsin, HALF_PI - arcsin)
    return jnp.where(x < 0.0, math.pi - positive, positive)


def place(s):
    return 4 * (s % 2) + s // 2


def turn_blocks(tiles):
    tiles = list(tiles)
    block = lax.broadcasted_iota(jnp.int32, tiles[0].shape, 1) // 16
    for bit in (1, 2, 4):
        clear = (block & bit) == 0
        for i in range(8):
            if i & bit == 0:
                one, two = tiles[i], tiles[i + bit]
                tiles[i] = jnp.where(clear, one, pltpu.roll(two, 16 * bit, 1))
                tiles[i + bit] = jnp.where(clear, pltpu.roll(one, 128 - 16 * bit, 1), two)
    return tiles


def to_classes(tiles):
    lane = lax.broadcasted_iota(jnp.int32, tiles[0].shape, 1)
    index = 8 * (lane % 16) + lane // 16
    return turn_blocks([jnp.take_along_axis(tile, index, axis=1) for tile in tiles])


def from_classes(tiles):
    lane = lax.broadcasted_iota(jnp.int32, tiles[0].shape, 1)
    index = 16 * (lane % 8) + lane // 8
    return [jnp.take_along_axis(tile, index, axis=1) for tile in turn_blocks(tiles)]


def kernel(
    bounds_ref, x_hbm, pot_hbm, out_ref, ritz_ref,
    x_ref, pot_ref, coef, start, even, odd, filt, filtered, diag_rows, diag, pot_own, slab, ops, apply_ops,
    gm, scattered, summed, total, ortho, fields,
    in_sem, pot_send, pot_recv, ghost_send, ghost_recv, vec_send, vec_recv, small_send, small_recv,
    back_send, back_recv,
):
    s = lax.axis_index("strip")
    v = lax.axis_index("vec")
    y_lo = s // 2 % 2
    along = s // 4 * 2 + s % 2
    across = y_lo * NV + v
    flipped = s + 2 - 4 * y_lo

    barrier = pltpu.get_barrier_semaphore()

    def greet(j, carry):
        peer = lax.rem(v + j, NV)
        for where in ({"strip": s, "vec": peer}, {"strip": flipped, "vec": peer}, {"strip": lax.rem(s + j, NS), "vec": v}):
            pl.semaphore_signal(barrier, inc=1, device_id=where, device_id_type=pl.DeviceIdType.MESH)
        return carry

    pot_in = pltpu.make_async_copy(pot_hbm, pot_ref, in_sem.at[0])
    x_in = pltpu.make_async_copy(x_hbm, x_ref, in_sem.at[1])
    pot_in.start()
    x_in.start()
    lax.fori_loop(1, NV, greet, 0)

    def splat(i):
        return jnp.full((8, 128), bounds_ref[i], jnp.int32).astype(F32) * grid_unit

    edges = [splat(i) for i in range(4)]
    center = (edges[0] + edges[1]) * 0.5
    spread = (edges[1] - edges[0]) * 0.5
    scale = 2.0 / spread

    pot_in.wait()
    for r in range(ROWS // 8):
        tiles = []
        for t in range(SUB):
            level = pot_ref[8 * r:8 * r + 8, 128 * t:128 * t + 128].astype(F32)
            tiles.append(disorder * (level / (POT_LEVELS - 1) - 0.5))
        for c, field in enumerate(to_classes(tiles)):
            pot_own[pl.ds(64 * r + place(c), 8, stride=8), :] = field
            diag_rows[pl.ds(OWN + 64 * r + place(c), 8, stride=8), :] = (field - center) * scale

    x_in.wait()

    def classes_of(q, carry):
        for r in range(ROWS // 8):
            tiles = [0.5 * x_ref[q, 8 * r:8 * r + 8, 128 * t:128 * t + 128] for t in range(SUB)]
            for c, tile in enumerate(to_classes(tiles)):
                start[q, pl.ds(OWN + 64 * r + place(c), 8, stride=8), :] = tile
        return carry

    lax.fori_loop(0, NQ, classes_of, 0)

    pl.semaphore_wait(barrier, 3 * (NV - 1))

    up = lax.rem(s + NS - 1, NS)
    down = lax.rem(s + 1, NS)
    up2 = lax.rem(s + NS - 2, NS)

    def pot_copies():
        mine = diag_rows.at[pl.ds(OWN, OWN)]
        return (
            remote(mine, diag_rows.at[pl.ds(2 * OWN, OWN)], pot_send.at[0], pot_recv.at[0], strip=up),
            remote(mine, diag_rows.at[pl.ds(0, OWN)], pot_send.at[1], pot_recv.at[1], strip=down),
        )

    def ghost_copies(q):
        mine = start.at[q, pl.ds(OWN, OWN)]
        return (
            remote(mine, start.at[q, pl.ds(2 * OWN, OWN)], ghost_send.at[q, 0], ghost_recv.at[q, 0], strip=up),
            remote(mine, start.at[q, pl.ds(0, OWN)], ghost_send.at[q, 1], ghost_recv.at[q, 1], strip=down),
            remote(
                start.at[q, pl.ds(OWN, SUB)], start.at[q, pl.ds(3 * OWN, SUB)],
                ghost_send.at[q, 2], ghost_recv.at[q, 2], strip=up2,
            ),
        )

    def start_ghosts(q):
        for copy in ghost_copies(q):
            copy.start()

    for copy in pot_copies():
        copy.start()
    start_ghosts(0)

    theta_lo = arccos((edges[2] - center) / spread)
    theta_hi = arccos((edges[3] - center) / spread)
    coef[0:8] = (theta_lo - theta_hi) / math.pi

    def coefficient(k, carry):
        order = jnp.full((8, 128), k, jnp.int32).astype(F32)
        coef[pl.ds(pl.multiple_of(8 * k, 8), 8)] = (
            2.0 * (jnp.sin(order * theta_lo) - jnp.sin(order * theta_hi)) / (order * math.pi)
        )
        return carry

    lax.fori_loop(1, DEGREE + 1, coefficient, 0)

    def pair_place(row):
        return (16 * row, 0) if row <= 48 else (16 * (96 - row), 1)

    for copy in pot_copies():
        copy.wait()
    for row in range(1, 3 * ROWS):
        value = diag_rows[8 * row:8 * row + 8]
        for base, half in {pair_place(row), (16 * (96 - row), 1) if row == 48 else pair_place(row)}:
            diag[pl.ds(base + half, 8, stride=2), :] = value

    sub = lax.broadcasted_iota(jnp.int32, (8, 128), 0)
    lane = lax.broadcasted_iota(jnp.int32, (8, 128), 1)
    index_left = jnp.where(sub >= 6, (lane + 127) % 128, lane)
    index_right = jnp.where(sub < 2, (lane + 1) % 128, lane)
    upper = (sub % 2 == 0)[None, None]

    def update(step, low, high, double, c_now, c_next, accumulate):
        now, then = ((even, odd), (odd, even))[step]
        rows = high - low
        flat = (rows, 8, 128)
        top = min(high + 1, PAIRS)
        ext = now[(low - 1) * 16:top * 16].reshape(top - low + 1, 2, 8, 128)
        above = ext[0:rows]
        mid = ext[1:rows + 1]
        if high == PAIRS:
            crossing = ext[rows - 1:rows]
            crossing = jnp.where(upper, pltpu.roll(crossing, 7, 2), pltpu.roll(crossing, 1, 2))
            below = jnp.concatenate([ext[2:rows + 1], crossing], axis=0)
        else:
            below = ext[2:rows + 2]
        left = pltpu.roll(jnp.take_along_axis(mid[:, 1], jnp.broadcast_to(index_left[None], flat), axis=2), 2, 1)
        right = pltpu.roll(jnp.take_along_axis(mid[:, 0], jnp.broadcast_to(index_right[None], flat), axis=2), 6, 1)
        before = then[low * 16:high * 16].reshape(rows, 2, 8, 128)
        local = diag[low * 16:high * 16].reshape(rows, 2, 8, 128)
        parts = []
        for j, beside in enumerate((left + mid[:, 1], mid[:, 0] + right)):
            old = before[:, j]
            if step == 1:
                old = old * double
            parts.append((local[:, j] * mid[:, j] - old) - scale * ((above[:, j] + below[:, j]) + beside))
        after = jnp.stack(parts, axis=1)
        then[low * 16:high * 16] = after.reshape(rows * 16, 128)
        if accumulate:
            term = (c_now * mid + c_next * after).reshape(rows * 16, 128)
            filt[...] = filt[...] + term

    def vec_copy(q, j):
        peer = lax.rem(v + j, NV)
        return remote(
            filtered.at[q, pl.ds(peer * CHUNKS, HALO)], slab.at[pl.ds((v * NQ + q) * HALO, HALO)],
            vec_send.at[q], vec_recv.at[q], vec=peer,
        )

    def one_vector(q, carry):
        for copy in ghost_copies(q):
            copy.wait()

        @pl.when(q < NQ - 1)
        def _():
            start_ghosts(q + 1)

        for row in range(3 * ROWS + 1):
            value = start[q, 8 * row:8 * row + 8]
            base, half = pair_place(row)
            even[pl.ds(base + half, 8, stride=2), :] = value
            if row == 48:
                even[pl.ds(base + 1, 8, stride=2), :] = value
        odd[...] = jnp.zeros((16 * PAIRS, 128), F32)
        filt[...] = (
            (2.0 * coef[0:8]) * even[16 * ROWS:16 * PAIRS].reshape(2 * (PAIRS - ROWS), 8, 128)
        ).reshape(16 * (PAIRS - ROWS), 128)
        for block in range(4):
            low = 8 * block + 1

            def pair(i, inner, block=block, low=low):
                k = 8 * block + 2 * i + 1
                double = jnp.where(k == 1, 2.0, 1.0).astype(F32)
                c_now = coef[pl.ds(pl.multiple_of(8 * k, 8), 8)]
                c_next = coef[pl.ds(pl.multiple_of(8 * k + 8, 8), 8)]
                for step in range(2):
                    update(step, low, ROWS, double, None, None, False)
                    update(step, ROWS, PAIRS, double, c_now, c_next, step == 1)
                return inner

            lax.fori_loop(0, 4, pair, 0)
        for row in range(ROWS + 1):
            base, half = pair_place(ROWS + row)
            filtered[q, 8 * row:8 * row + 8] = filt[pl.ds(base - 16 * ROWS + half, 8, stride=2), :]
        slab[pl.ds((v * NQ + q) * HALO, HALO)] = filtered[q, pl.ds(v * CHUNKS, HALO)]

        def send(j, inner):
            vec_copy(q, j).start()
            return inner

        lax.fori_loop(1, NV, send, 0)
        return carry

    lax.fori_loop(0, NQ, one_vector, 0)
    for q in range(NQ):
        wait_bytes(slab.at[pl.ds(0, (NV - 1) * HALO)], vec_recv.at[q])

    lane16 = lax.broadcasted_iota(jnp.int32, (16, 128), 1)
    pot_slab = pot_own[pl.ds(v * CHUNKS, CHUNKS)] * 0.5

    def chunk(g, n):
        base = 16 * g * HALO + n
        return jnp.concatenate(
            [slab[pl.ds(base, 8, stride=HALO), :], slab[pl.ds(base + 8 * HALO, 8, stride=HALO), :]], axis=0
        )

    for g in range(NVEC // 16):
        y = [chunk(g, n) for n in range(HALO)]
        for row in range(PIECE):
            for c in range(SUB):
                n = SUB * row + place(c)
                if c < SUB - 1:
                    right = y[SUB * row + place(c + 1)]
                else:
                    right = pltpu.roll(y[SUB * row + place(0)], 127, 1)
                z = pot_slab[n:n + 1] * y[n] - (right + y[n + SUB])
                for part, value in enumerate(split(y[n]) + split(z)):
                    ops[64 * part + 16 * g:64 * part + 16 * g + 16, 128 * n:128 * n + 128] = value
    prod = lax.dot_general(
        ops[...], ops[0:128, :], (((1,), (1,)), ((), ())), preferred_element_type=F32
    )
    rows64 = lax.broadcasted_iota(jnp.int32, (64, 128), 0)
    lanes64 = lax.broadcasted_iota(jnp.int32, (64, 128), 1)
    gram_part = prod[0:64] + prod[64:128]
    cross_part = prod[128:192] + prod[192:256]
    gm[...] = jnp.where(
        lanes64 < 64, gram_part + pltpu.roll(gram_part, 64, 1), cross_part + pltpu.roll(cross_part, 64, 1)
    )

    def to_along(stage, source, target):
        def send(j, carry):
            peer = lax.rem(along + j, NA)
            strip = peer // 2 * 4 + y_lo * 2 + peer % 2
            remote(source(peer), target, small_send.at[stage], small_recv.at[stage], strip=strip).start()
            return carry

        lax.fori_loop(1, NA, send, 0)

    mine_a = pl.ds(along * 8, 8)
    mine_b = pl.ds(across * 8, 8)
    scattered[mine_a] = gm[mine_a]
    to_along(0, lambda peer: gm.at[pl.ds(peer * 8, 8)], scattered.at[mine_a])

    for g in range(NVEC // 16):
        for row in range(PIECE):
            tiles = from_classes([chunk(g, SUB * row + place(c)) for c in range(SUB)])
            for t, tile in enumerate(tiles):
                n = SUB * row + t
                for part, value in enumerate(split(tile)):
                    apply_ops[64 * part + 16 * g:64 * part + 16 * g + 16, 128 * n:128 * n + 128] = value

    wait_bytes(scattered.at[pl.ds(0, 8 * (NA - 1))], small_recv.at[0])
    summed[mine_b] = jnp.sum(scattered[...].reshape(NA, 8, 128), axis=0)

    def send_across(j, carry):
        peer = lax.rem(across + j, NB)
        strip = s + 2 * (peer // NV - y_lo)
        remote(
            summed.at[mine_b], summed.at[mine_b], small_send.at[1], small_recv.at[1], strip=strip, vec=peer % NV
        ).start()
        return carry

    lax.fori_loop(1, NB, send_across, 0)
    wait_bytes(summed.at[pl.ds(0, 8 * (NB - 1))], small_recv.at[1])
    total[mine_a] = jnp.sum(summed[...].reshape(NB, 8, 128), axis=0)
    to_along(2, lambda peer: total.at[mine_a], total.at[mine_a])
    wait_bytes(total.at[pl.ds(0, 8 * (NA - 1))], small_recv.at[2])

    aug = jnp.where(lanes64 < 64, total[...], jnp.where(lanes64 - 64 == rows64, 1.0, 0.0))
    for k in range(NVEC):
        column = aug[:, k:k + 1] / aug[k:k + 1, k:k + 1]
        factor = jnp.where(rows64 > k, jnp.broadcast_to(column, (64, 128)), 0.0)
        aug = aug - factor * aug[k:k + 1, :]
    pivots = jnp.sum(jnp.where(rows64 == lanes64, aug, 0.0), axis=1, keepdims=True)
    inverse = (pltpu.roll(aug, 64, 1) * lax.rsqrt(pivots))[:, 0:64]

    high, low = split(math.sqrt(SITES) * inverse)
    left = jnp.concatenate(
        [jnp.concatenate([high, high], axis=1), jnp.concatenate([low, low], axis=1)], axis=0
    )
    product = jnp.dot(left, apply_ops[...], preferred_element_type=F32)
    for n in range(CHUNKS):
        value = product[0:64, 128 * n:128 * n + 128] + product[64:128, 128 * n:128 * n + 128]
        for g in range(8):
            ortho[pl.ds(n + 8 * g * CHUNKS, 8, stride=CHUNKS), :] = value[8 * g:8 * g + 8]

    def back_copy(j, q):
        peer = lax.rem(v + j, NV)
        return remote(
            ortho.at[pl.ds((peer * NQ + q) * CHUNKS, CHUNKS)], fields.at[q, pl.ds(v * CHUNKS, CHUNKS)],
            back_send.at[0], back_recv.at[0], vec=peer,
        )

    def send_back(j, carry):
        for q in range(NQ):
            back_copy(j, q).start()
        return carry

    lax.fori_loop(1, NV, send_back, 0)
    for q in range(NQ):
        fields[q, pl.ds(v * CHUNKS, CHUNKS)] = ortho[pl.ds((v * NQ + q) * CHUNKS, CHUNKS)]

    cross = pltpu.roll(total[...], 64, 1)[:, 0:64]
    cross = cross + cross.T
    half = jnp.dot(inverse, cross, precision=lax.Precision.HIGHEST, preferred_element_type=F32)
    ritz_ref[...] = float(ROWS) * lax.dot_general(
        inverse, half, (((1,), (1,)), ((), ())), precision=lax.Precision.HIGHEST, preferred_element_type=F32
    )

    wait_bytes(ortho.at[pl.ds(0, (NV - 1) * NQ * CHUNKS)], back_recv.at[0])
    for q in range(NQ):
        for r in range(ROWS // 8):
            for t in range(SUB):
                out_ref[q, 8 * r:8 * r + 8, 128 * t:128 * t + 128] = fields[q, pl.ds(64 * r + t, 8, stride=8), :]

    wait_bytes(ortho.at[pl.ds(0, (NV - 1) * NQ * CHUNKS)], back_send.at[0])
    wait_bytes(scattered.at[pl.ds(0, 8 * (NA - 1))], small_send.at[0])
    wait_bytes(summed.at[pl.ds(0, 8 * (NB - 1))], small_send.at[1])
    wait_bytes(scattered.at[pl.ds(0, 8 * (NA - 1))], small_send.at[2])
    for q in range(NQ):
        wait_bytes(slab.at[pl.ds(0, (NV - 1) * HALO)], vec_send.at[q])


def shards(start_vectors, potential, bounds):
    vmem = pl.BlockSpec(memory_space=pltpu.VMEM)
    hbm = pl.BlockSpec(memory_space=pltpu.HBM)
    dma = pltpu.SemaphoreType.DMA
    return pl.pallas_call(
        kernel,
        out_shape=(
            jax.ShapeDtypeStruct((NQ, ROWS, 1024), F32),
            jax.ShapeDtypeStruct((NVEC, NVEC), F32),
        ),
        in_specs=[pl.BlockSpec(memory_space=pltpu.SMEM), hbm, hbm],
        out_specs=(vmem, vmem),
        scratch_shapes=[
            pltpu.VMEM((NQ, ROWS, 1024), F32),
            pltpu.VMEM((ROWS, 1024), jnp.int32),
            pltpu.VMEM((8 * (DEGREE + 1), 128), F32),
            pltpu.VMEM((NQ, FIELD, 128), F32),
            pltpu.VMEM((16 * PAIRS, 128), F32),
            pltpu.VMEM((16 * PAIRS, 128), F32),
            pltpu.VMEM((16 * (PAIRS - ROWS), 128), F32),
            pltpu.VMEM((NQ, OWN + SUB, 128), F32),
            pltpu.VMEM((FIELD, 128), F32),
            pltpu.VMEM((16 * PAIRS, 128), F32),
            pltpu.VMEM((OWN, 128), F32),
            pltpu.VMEM((NVEC * HALO, 128), F32),
            pltpu.VMEM((256, CHUNKS * 128), BF16),
            pltpu.VMEM((128, CHUNKS * 128), BF16),
            pltpu.VMEM((64, 128), F32),
            pltpu.VMEM((8 * NA, 128), F32),
            pltpu.VMEM((8 * NB, 128), F32),
            pltpu.VMEM((64, 128), F32),
            pltpu.VMEM((NVEC * CHUNKS, 128), F32),
            pltpu.VMEM((NQ, OWN, 128), F32),
            dma((2,)), dma((2,)), dma((2,)), dma((NQ, 3)), dma((NQ, 3)), dma((NQ,)), dma((NQ,)),
            dma((3,)), dma((3,)), dma((1,)), dma((1,)),
        ],
        compiler_params=pltpu.CompilerParams(
            collective_id=0, has_side_effects=True, vmem_limit_bytes=40 << 20
        ),
        name="filter_ritz",
    )(bounds, start_vectors, potential)


def solution(mesh):
    in_specs = (P("vec", "strip", None), P("strip", None), P())
    out_specs = (P("vec", "strip", None), P())
    return jax.shard_map(shards, mesh=mesh, in_specs=in_specs, out_specs=out_specs, check_vma=False)
```

```python
import math

import jax
import jax.numpy as jnp
from jax import lax
from jax.experimental import pallas as pl
from jax.experimental.pallas import tpu as pltpu
from jax.sharding import PartitionSpec as P

DEGREE = 32
POT_LEVELS = 16
NQ = 4
ROWS = 32
NV = 16
NS = 16
NVEC = NQ * NV
PIECE = ROWS // NV
SUB = 8
CHUNKS = PIECE * SUB
HALO = CHUNKS + SUB
FIELD = (3 * ROWS + 1) * SUB
PAIRS = 3 * ROWS // 2 + 1
NA = 8
NB = 32
OWN = ROWS * SUB
HALF_PI = math.pi / 2
SITES = NS * ROWS * 1024

grid_unit = 0.0625
disorder = 2.0
F32 = jnp.float32
BF16 = jnp.bfloat16


def remote(src, dst, send, recv, **where):
    return pltpu.make_async_remote_copy(
        src_ref=src, dst_ref=dst, send_sem=send, recv_sem=recv,
        device_id=where, device_id_type=pl.DeviceIdType.MESH,
    )


def wait_bytes(ref, sem):
    pltpu.make_async_copy(ref, ref, sem).wait()


def split(value):
    high = value.astype(BF16)
    return high, (value - high.astype(F32)).astype(BF16)


def arccos(x):
    size = jnp.abs(x)
    large = size > 0.5
    square = jnp.where(large, 0.5 * (1.0 - size), x * x)
    base = jnp.where(large, jnp.sqrt(square), size)
    poly = 4.2163199048e-2 * square + 2.4181311049e-2
    poly = poly * square + 4.5470025998e-2
    poly = poly * square + 7.4953002686e-2
    poly = poly * square + 1.6666752422e-1
    arcsin = base + base * square * poly
    positive = jnp.where(large, 2.0 * arcsin, HALF_PI - arcsin)
    return jnp.where(x < 0.0, math.pi - positive, positive)


def place(s):
    return 4 * (s % 2) + s // 2


def turn_blocks(tiles):
    tiles = list(tiles)
    block = lax.broadcasted_iota(jnp.int32, tiles[0].shape, 1) // 16
    for bit in (1, 2, 4):
        clear = (block & bit) == 0
        for i in range(8):
            if i & bit == 0:
                one, two = tiles[i], tiles[i + bit]
                tiles[i] = jnp.where(clear, one, pltpu.roll(two, 16 * bit, 1))
                tiles[i + bit] = jnp.where(clear, pltpu.roll(one, 128 - 16 * bit, 1), two)
    return tiles


def to_classes(tiles):
    lane = lax.broadcasted_iota(jnp.int32, tiles[0].shape, 1)
    index = 8 * (lane % 16) + lane // 16
    return turn_blocks([jnp.take_along_axis(tile, index, axis=1) for tile in tiles])


def from_classes(tiles):
    lane = lax.broadcasted_iota(jnp.int32, tiles[0].shape, 1)
    index = 16 * (lane % 8) + lane // 8
    return [jnp.take_along_axis(tile, index, axis=1) for tile in turn_blocks(tiles)]


def inverse_factor(aug):
    rows = [aug[8 * i:8 * i + 8] for i in range(8)]
    sub = lax.broadcasted_iota(jnp.int32, (8, 128), 0)
    done = []

    def spread(value, k):
        return jnp.broadcast_to(value[k:k + 1], (8, 128))

    for p in range(8):
        columns = {
            (j, i): jnp.broadcast_to(rows[i][:, 8 * p + j:8 * p + j + 1], (8, 128))
            for i in range(p, 8) for j in range(8)
        }
        pivots = spread(columns[0, p], 0)
        for k in range(8):
            pivot = spread(columns[k, p], k)
            pivots = jnp.where(sub == k, pivot, pivots)
            inverse = 1.0 / pivot
            row = spread(rows[p], k)
            heads = {j: spread(columns[j, p], k) for j in range(k + 1, 8)}
            for i in range(p, 8):
                factor = columns[k, i] * inverse
                if i == p:
                    factor = jnp.where(sub > k, factor, 0.0)
                rows[i] = rows[i] - factor * row
                for j in range(k + 1, 8):
                    columns[j, i] = columns[j, i] - factor * heads[j]
        done.append(pltpu.roll(rows[p], 64, 1) * lax.rsqrt(pivots))
    return jnp.concatenate(done, axis=0)[:, 0:64]


def kernel(
    bounds_ref, x_hbm, pot_hbm, fields, ritz_ref,
    x_ref, pot_ref, coef, start, even, odd, filt, filtered, diag_rows, diag, pot_own, slab, ops, apply_ops,
    gm, scattered, summed, total, ortho,
    in_sem, pot_send, pot_recv, ghost_send, ghost_recv, vec_send, vec_recv, small_send, small_recv,
    back_send, back_recv,
):
    s = lax.axis_index("strip")
    v = lax.axis_index("vec")
    y_lo = s // 2 % 2
    along = s // 4 * 2 + s % 2
    across = y_lo * NV + v
    flipped = s + 2 - 4 * y_lo

    barrier = pltpu.get_barrier_semaphore()

    def greet(j, carry):
        peer = lax.rem(v + j, NV)
        for where in ({"strip": s, "vec": peer}, {"strip": flipped, "vec": peer}, {"strip": lax.rem(s + j, NS), "vec": v}):
            pl.semaphore_signal(barrier, inc=1, device_id=where, device_id_type=pl.DeviceIdType.MESH)
        return carry

    pot_in = pltpu.make_async_copy(pot_hbm, pot_ref, in_sem.at[0])
    x_in = pltpu.make_async_copy(x_hbm, x_ref, in_sem.at[1])
    pot_in.start()
    x_in.start()
    lax.fori_loop(1, NV, greet, 0)

    def splat(i):
        return jnp.full((8, 128), bounds_ref[i], jnp.int32).astype(F32) * grid_unit

    edges = [splat(i) for i in range(4)]
    center = (edges[0] + edges[1]) * 0.5
    spread = (edges[1] - edges[0]) * 0.5
    scale = 2.0 / spread

    pot_in.wait()
    for r in range(ROWS // 8):
        tiles = []
        for t in range(SUB):
            level = pot_ref[8 * r:8 * r + 8, 128 * t:128 * t + 128].astype(F32)
            tiles.append(disorder * (level / (POT_LEVELS - 1) - 0.5))
        for c, field in enumerate(to_classes(tiles)):
            pot_own[pl.ds(64 * r + place(c), 8, stride=8), :] = field
            diag_rows[pl.ds(OWN + 64 * r + place(c), 8, stride=8), :] = (field - center) * scale

    x_in.wait()

    def classes_of(q, carry):
        for r in range(ROWS // 8):
            tiles = [0.5 * x_ref[q, 8 * r:8 * r + 8, 128 * t:128 * t + 128] for t in range(SUB)]
            for c, tile in enumerate(to_classes(tiles)):
                start[q, pl.ds(OWN + 64 * r + place(c), 8, stride=8), :] = tile
        return carry

    lax.fori_loop(0, NQ, classes_of, 0)

    pl.semaphore_wait(barrier, 3 * (NV - 1))

    up = lax.rem(s + NS - 1, NS)
    down = lax.rem(s + 1, NS)
    up2 = lax.rem(s + NS - 2, NS)

    def pot_copies():
        mine = diag_rows.at[pl.ds(OWN, OWN)]
        return (
            remote(mine, diag_rows.at[pl.ds(2 * OWN, OWN)], pot_send.at[0], pot_recv.at[0], strip=up),
            remote(mine, diag_rows.at[pl.ds(0, OWN)], pot_send.at[1], pot_recv.at[1], strip=down),
        )

    def ghost_copies(q):
        mine = start.at[q, pl.ds(OWN, OWN)]
        return (
            remote(mine, start.at[q, pl.ds(2 * OWN, OWN)], ghost_send.at[q, 0], ghost_recv.at[q, 0], strip=up),
            remote(mine, start.at[q, pl.ds(0, OWN)], ghost_send.at[q, 1], ghost_recv.at[q, 1], strip=down),
            remote(
                start.at[q, pl.ds(OWN, SUB)], start.at[q, pl.ds(3 * OWN, SUB)],
                ghost_send.at[q, 2], ghost_recv.at[q, 2], strip=up2,
            ),
        )

    def start_ghosts(q):
        for copy in ghost_copies(q):
            copy.start()

    for copy in pot_copies():
        copy.start()
    start_ghosts(0)

    theta_lo = arccos((edges[2] - center) / spread)
    theta_hi = arccos((edges[3] - center) / spread)
    coef[0:8] = (theta_lo - theta_hi) / math.pi

    def coefficient(k, carry):
        order = jnp.full((8, 128), k, jnp.int32).astype(F32)
        coef[pl.ds(pl.multiple_of(8 * k, 8), 8)] = (
            2.0 * (jnp.sin(order * theta_lo) - jnp.sin(order * theta_hi)) / (order * math.pi)
        )
        return carry

    lax.fori_loop(1, DEGREE + 1, coefficient, 0)

    def pair_place(row):
        return (16 * row, 0) if row <= 48 else (16 * (96 - row), 1)

    for copy in pot_copies():
        copy.wait()
    for row in range(1, 3 * ROWS):
        value = diag_rows[8 * row:8 * row + 8]
        for base, half in {pair_place(row), (16 * (96 - row), 1) if row == 48 else pair_place(row)}:
            diag[pl.ds(base + half, 8, stride=2), :] = value

    sub = lax.broadcasted_iota(jnp.int32, (8, 128), 0)
    lane = lax.broadcasted_iota(jnp.int32, (8, 128), 1)
    index_left = jnp.where(sub >= 6, (lane + 127) % 128, lane)
    index_right = jnp.where(sub < 2, (lane + 1) % 128, lane)
    upper = (sub % 2 == 0)[None, None]

    def update(step, low, high, double, c_now, c_next, accumulate):
        now, then = ((even, odd), (odd, even))[step]
        rows = high - low
        flat = (rows, 8, 128)
        top = min(high + 1, PAIRS)
        ext = now[(low - 1) * 16:top * 16].reshape(top - low + 1, 2, 8, 128)
        above = ext[0:rows]
        mid = ext[1:rows + 1]
        if high == PAIRS:
            crossing = ext[rows - 1:rows]
            crossing = jnp.where(upper, pltpu.roll(crossing, 7, 2), pltpu.roll(crossing, 1, 2))
            below = jnp.concatenate([ext[2:rows + 1], crossing], axis=0)
        else:
            below = ext[2:rows + 2]
        left = pltpu.roll(jnp.take_along_axis(mid[:, 1], jnp.broadcast_to(index_left[None], flat), axis=2), 2, 1)
        right = pltpu.roll(jnp.take_along_axis(mid[:, 0], jnp.broadcast_to(index_right[None], flat), axis=2), 6, 1)
        before = then[low * 16:high * 16].reshape(rows, 2, 8, 128)
        local = diag[low * 16:high * 16].reshape(rows, 2, 8, 128)
        parts = []
        for j, beside in enumerate((left + mid[:, 1], mid[:, 0] + right)):
            old = before[:, j]
            if step == 1:
                old = old * double
            parts.append((local[:, j] * mid[:, j] - old) - scale * ((above[:, j] + below[:, j]) + beside))
        after = jnp.stack(parts, axis=1)
        then[low * 16:high * 16] = after.reshape(rows * 16, 128)
        if accumulate:
            term = (c_now * mid + c_next * after).reshape(rows * 16, 128)
            filt[...] = filt[...] + term

    def vec_copy(q, j):
        peer = lax.rem(v + j, NV)
        return remote(
            filtered.at[q, pl.ds(peer * CHUNKS, HALO)], slab.at[pl.ds((v * NQ + q) * HALO, HALO)],
            vec_send.at[q], vec_recv.at[q], vec=peer,
        )

    def one_vector(q, carry):
        for copy in ghost_copies(q):
            copy.wait()

        @pl.when(q < NQ - 1)
        def _():
            start_ghosts(q + 1)

        for row in range(3 * ROWS + 1):
            value = start[q, 8 * row:8 * row + 8]
            base, half = pair_place(row)
            even[pl.ds(base + half, 8, stride=2), :] = value
            if row == 48:
                even[pl.ds(base + 1, 8, stride=2), :] = value
        odd[...] = jnp.zeros((16 * PAIRS, 128), F32)
        filt[...] = (
            (2.0 * coef[0:8]) * even[16 * ROWS:16 * PAIRS].reshape(2 * (PAIRS - ROWS), 8, 128)
        ).reshape(16 * (PAIRS - ROWS), 128)
        for block in range(4):
            low = 8 * block + 1

            def pair(i, inner, block=block, low=low):
                k = 8 * block + 2 * i + 1
                double = jnp.where(k == 1, 2.0, 1.0).astype(F32)
                c_now = coef[pl.ds(pl.multiple_of(8 * k, 8), 8)]
                c_next = coef[pl.ds(pl.multiple_of(8 * k + 8, 8), 8)]
                for step in range(2):
                    update(step, low, ROWS, double, None, None, False)
                    update(step, ROWS, PAIRS, double, c_now, c_next, step == 1)
                return inner

            lax.fori_loop(0, 4, pair, 0)
        for row in range(ROWS + 1):
            base, half = pair_place(ROWS + row)
            filtered[q, 8 * row:8 * row + 8] = filt[pl.ds(base - 16 * ROWS + half, 8, stride=2), :]
        slab[pl.ds((v * NQ + q) * HALO, HALO)] = filtered[q, pl.ds(v * CHUNKS, HALO)]

        def send(j, inner):
            vec_copy(q, j).start()
            return inner

        lax.fori_loop(1, NV, send, 0)
        return carry

    lax.fori_loop(0, NQ, one_vector, 0)
    for q in range(NQ):
        wait_bytes(slab.at[pl.ds(0, (NV - 1) * HALO)], vec_recv.at[q])

    lane16 = lax.broadcasted_iota(jnp.int32, (16, 128), 1)
    pot_slab = pot_own[pl.ds(v * CHUNKS, CHUNKS)] * 0.5

    def chunk(g, n):
        base = 16 * g * HALO + n
        return jnp.concatenate(
            [slab[pl.ds(base, 8, stride=HALO), :], slab[pl.ds(base + 8 * HALO, 8, stride=HALO), :]], axis=0
        )

    for g in range(NVEC // 16):
        y = [chunk(g, n) for n in range(HALO)]
        for row in range(PIECE):
            for c in range(SUB):
                n = SUB * row + place(c)
                if c < SUB - 1:
                    right = y[SUB * row + place(c + 1)]
                else:
                    right = pltpu.roll(y[SUB * row + place(0)], 127, 1)
                z = pot_slab[n:n + 1] * y[n] - (right + y[n + SUB])
                for part, value in enumerate(split(y[n]) + split(z)):
                    ops[64 * part + 16 * g:64 * part + 16 * g + 16, 128 * n:128 * n + 128] = value
    prod = lax.dot_general(
        ops[...], ops[0:128, :], (((1,), (1,)), ((), ())), preferred_element_type=F32
    )
    rows64 = lax.broadcasted_iota(jnp.int32, (64, 128), 0)
    lanes64 = lax.broadcasted_iota(jnp.int32, (64, 128), 1)
    gram_part = prod[0:64] + prod[64:128]
    cross_part = prod[128:192] + prod[192:256]
    gm[...] = jnp.where(
        lanes64 < 64, gram_part + pltpu.roll(gram_part, 64, 1), cross_part + pltpu.roll(cross_part, 64, 1)
    )

    def to_along(stage, source, target):
        def send(j, carry):
            peer = lax.rem(along + j, NA)
            strip = peer // 2 * 4 + y_lo * 2 + peer % 2
            remote(source(peer), target, small_send.at[stage], small_recv.at[stage], strip=strip).start()
            return carry

        lax.fori_loop(1, NA, send, 0)

    mine_a = pl.ds(along * 8, 8)
    mine_b = pl.ds(across * 8, 8)
    scattered[mine_a] = gm[mine_a]
    to_along(0, lambda peer: gm.at[pl.ds(peer * 8, 8)], scattered.at[mine_a])

    for g in range(NVEC // 16):
        for row in range(PIECE):
            tiles = from_classes([chunk(g, SUB * row + place(c)) for c in range(SUB)])
            for t, tile in enumerate(tiles):
                n = SUB * row + t
                for part, value in enumerate(split(tile)):
                    apply_ops[64 * part + 16 * g:64 * part + 16 * g + 16, 128 * n:128 * n + 128] = value

    wait_bytes(scattered.at[pl.ds(0, 8 * (NA - 1))], small_recv.at[0])
    summed[mine_b] = jnp.sum(scattered[...].reshape(NA, 8, 128), axis=0)

    def send_across(j, carry):
        peer = lax.rem(across + j, NB)
        strip = s + 2 * (peer // NV - y_lo)
        remote(
            summed.at[mine_b], summed.at[mine_b], small_send.at[1], small_recv.at[1], strip=strip, vec=peer % NV
        ).start()
        return carry

    lax.fori_loop(1, NB, send_across, 0)
    wait_bytes(summed.at[pl.ds(0, 8 * (NB - 1))], small_recv.at[1])
    total[mine_a] = jnp.sum(summed[...].reshape(NB, 8, 128), axis=0)
    to_along(2, lambda peer: total.at[mine_a], total.at[mine_a])
    wait_bytes(total.at[pl.ds(0, 8 * (NA - 1))], small_recv.at[2])

    inverse = inverse_factor(jnp.where(lanes64 < 64, total[...], jnp.where(lanes64 - 64 == rows64, 1.0, 0.0)))

    high, low = split(math.sqrt(SITES) * inverse)
    left = jnp.concatenate(
        [jnp.concatenate([high, high], axis=1), jnp.concatenate([low, low], axis=1)], axis=0
    )
    product = jnp.dot(left, apply_ops[...], preferred_element_type=F32)
    for n in range(CHUNKS):
        value = product[0:64, 128 * n:128 * n + 128] + product[64:128, 128 * n:128 * n + 128]
        for g in range(8):
            ortho[pl.ds(n + 8 * g * CHUNKS, 8, stride=CHUNKS), :] = value[8 * g:8 * g + 8]

    def back_copy(j, q):
        peer = lax.rem(v + j, NV)
        return remote(
            ortho.at[pl.ds((peer * NQ + q) * CHUNKS, CHUNKS)], fields.at[q, pl.ds(v * CHUNKS, CHUNKS)],
            back_send.at[0], back_recv.at[0], vec=peer,
        )

    def send_back(j, carry):
        for q in range(NQ):
            back_copy(j, q).start()
        return carry

    lax.fori_loop(1, NV, send_back, 0)
    for q in range(NQ):
        fields[q, pl.ds(v * CHUNKS, CHUNKS)] = ortho[pl.ds((v * NQ + q) * CHUNKS, CHUNKS)]

    cross = pltpu.roll(total[...], 64, 1)[:, 0:64]
    cross = cross + cross.T
    half = jnp.dot(inverse, cross, precision=lax.Precision.HIGHEST, preferred_element_type=F32)
    ritz_ref[...] = float(ROWS) * lax.dot_general(
        inverse, half, (((1,), (1,)), ((), ())), precision=lax.Precision.HIGHEST, preferred_element_type=F32
    )

    wait_bytes(ortho.at[pl.ds(0, (NV - 1) * NQ * CHUNKS)], back_recv.at[0])
    wait_bytes(ortho.at[pl.ds(0, (NV - 1) * NQ * CHUNKS)], back_send.at[0])
    wait_bytes(scattered.at[pl.ds(0, 8 * (NA - 1))], small_send.at[0])
    wait_bytes(summed.at[pl.ds(0, 8 * (NB - 1))], small_send.at[1])
    wait_bytes(scattered.at[pl.ds(0, 8 * (NA - 1))], small_send.at[2])
    for q in range(NQ):
        wait_bytes(slab.at[pl.ds(0, (NV - 1) * HALO)], vec_send.at[q])


def arrange(fields, ritz, out_ref, ritz_ref):
    for q in range(NQ):
        for r in range(ROWS // 8):
            for t in range(SUB):
                out_ref[q, 8 * r:8 * r + 8, 128 * t:128 * t + 128] = fields[q, pl.ds(64 * r + t, 8, stride=8), :]
    ritz_ref[...] = ritz[...]


def shards(start_vectors, potential, bounds):
    vmem = pl.BlockSpec(memory_space=pltpu.VMEM)
    hbm = pl.BlockSpec(memory_space=pltpu.HBM)
    dma = pltpu.SemaphoreType.DMA
    ritz_shape = jax.ShapeDtypeStruct((NVEC, NVEC), F32)
    fields, ritz = pl.pallas_call(
        kernel,
        out_shape=(jax.ShapeDtypeStruct((NQ, OWN, 128), F32), ritz_shape),
        in_specs=[pl.BlockSpec(memory_space=pltpu.SMEM), hbm, hbm],
        out_specs=(vmem, vmem),
        scratch_shapes=[
            pltpu.VMEM((NQ, ROWS, 1024), F32),
            pltpu.VMEM((ROWS, 1024), jnp.int32),
            pltpu.VMEM((8 * (DEGREE + 1), 128), F32),
            pltpu.VMEM((NQ, FIELD, 128), F32),
            pltpu.VMEM((16 * PAIRS, 128), F32),
            pltpu.VMEM((16 * PAIRS, 128), F32),
            pltpu.VMEM((16 * (PAIRS - ROWS), 128), F32),
            pltpu.VMEM((NQ, OWN + SUB, 128), F32),
            pltpu.VMEM((FIELD, 128), F32),
            pltpu.VMEM((16 * PAIRS, 128), F32),
            pltpu.VMEM((OWN, 128), F32),
            pltpu.VMEM((NVEC * HALO, 128), F32),
            pltpu.VMEM((256, CHUNKS * 128), BF16),
            pltpu.VMEM((128, CHUNKS * 128), BF16),
            pltpu.VMEM((64, 128), F32),
            pltpu.VMEM((8 * NA, 128), F32),
            pltpu.VMEM((8 * NB, 128), F32),
            pltpu.VMEM((64, 128), F32),
            pltpu.VMEM((NVEC * CHUNKS, 128), F32),
            dma((2,)), dma((2,)), dma((2,)), dma((NQ, 3)), dma((NQ, 3)), dma((NQ,)), dma((NQ,)),
            dma((3,)), dma((3,)), dma((1,)), dma((1,)),
        ],
        compiler_params=pltpu.CompilerParams(
            collective_id=0, has_side_effects=True, vmem_limit_bytes=63 << 20
        ),
        name="filter_ritz",
    )(bounds, start_vectors, potential)
    return pl.pallas_call(
        arrange,
        out_shape=(jax.ShapeDtypeStruct((NQ, ROWS, 1024), F32), ritz_shape),
        in_specs=[vmem, vmem],
        out_specs=(vmem, vmem),
        name="arrange",
    )(fields, ritz)


def solution(mesh):
    in_specs = (P("vec", "strip", None), P("strip", None), P())
    out_specs = (P("vec", "strip", None), P())
    return jax.shard_map(shards, mesh=mesh, in_specs=in_specs, out_specs=out_specs, check_vma=False)
```

```python
import math

import jax
import jax.numpy as jnp
from jax import lax
from jax.experimental import pallas as pl
from jax.experimental.pallas import tpu as pltpu
from jax.sharding import PartitionSpec as P

DEGREE = 32
POT_LEVELS = 16
NQ = 4
ROWS = 32
NV = 16
NS = 16
NVEC = NQ * NV
PIECE = ROWS // NV
SUB = 8
CHUNKS = PIECE * SUB
HALO = CHUNKS + SUB
FIELD = (3 * ROWS + 1) * SUB
PAIRS = 3 * ROWS // 2 + 1
NA = 8
NB = 32
OWN = ROWS * SUB
HALF_PI = math.pi / 2
SITES = NS * ROWS * 1024

grid_unit = 0.0625
disorder = 2.0
F32 = jnp.float32
BF16 = jnp.bfloat16


def remote(src, dst, send, recv, **where):
    return pltpu.make_async_remote_copy(
        src_ref=src, dst_ref=dst, send_sem=send, recv_sem=recv,
        device_id=where, device_id_type=pl.DeviceIdType.MESH,
    )


def wait_bytes(ref, sem):
    pltpu.make_async_copy(ref, ref, sem).wait()


def split(value):
    high = value.astype(BF16)
    return high, (value - high.astype(F32)).astype(BF16)


def arccos(x):
    size = jnp.abs(x)
    large = size > 0.5
    square = jnp.where(large, 0.5 * (1.0 - size), x * x)
    base = jnp.where(large, jnp.sqrt(square), size)
    poly = 4.2163199048e-2 * square + 2.4181311049e-2
    poly = poly * square + 4.5470025998e-2
    poly = poly * square + 7.4953002686e-2
    poly = poly * square + 1.6666752422e-1
    arcsin = base + base * square * poly
    positive = jnp.where(large, 2.0 * arcsin, HALF_PI - arcsin)
    return jnp.where(x < 0.0, math.pi - positive, positive)


def place(s):
    return 4 * (s % 2) + s // 2


def turn_blocks(tiles):
    tiles = list(tiles)
    block = lax.broadcasted_iota(jnp.int32, tiles[0].shape, 1) // 16
    for bit in (1, 2, 4):
        clear = (block & bit) == 0
        for i in range(8):
            if i & bit == 0:
                one, two = tiles[i], tiles[i + bit]
                tiles[i] = jnp.where(clear, one, pltpu.roll(two, 16 * bit, 1))
                tiles[i + bit] = jnp.where(clear, pltpu.roll(one, 128 - 16 * bit, 1), two)
    return tiles


def to_classes(tiles):
    lane = lax.broadcasted_iota(jnp.int32, tiles[0].shape, 1)
    index = 8 * (lane % 16) + lane // 16
    return turn_blocks([jnp.take_along_axis(tile, index, axis=1) for tile in tiles])


def from_classes(tiles):
    lane = lax.broadcasted_iota(jnp.int32, tiles[0].shape, 1)
    index = 16 * (lane % 8) + lane // 8
    return [jnp.take_along_axis(tile, index, axis=1) for tile in turn_blocks(tiles)]


def inverse_factor(aug):
    rows = [aug[8 * i:8 * i + 8] for i in range(8)]
    sub = lax.broadcasted_iota(jnp.int32, (8, 128), 0)
    done = []

    def spread(value, k):
        return jnp.broadcast_to(value[k:k + 1], (8, 128))

    for p in range(8):
        columns = {
            (j, i): jnp.broadcast_to(rows[i][:, 8 * p + j:8 * p + j + 1], (8, 128))
            for i in range(p, 8) for j in range(8)
        }
        pivots = spread(columns[0, p], 0)
        for k in range(8):
            pivot = spread(columns[k, p], k)
            pivots = jnp.where(sub == k, pivot, pivots)
            inverse = 1.0 / pivot
            row = spread(rows[p], k)
            heads = {j: spread(columns[j, p], k) for j in range(k + 1, 8)}
            for i in range(p, 8):
                factor = columns[k, i] * inverse
                if i == p:
                    factor = jnp.where(sub > k, factor, 0.0)
                rows[i] = rows[i] - factor * row
                for j in range(k + 1, 8):
                    columns[j, i] = columns[j, i] - factor * heads[j]
        done.append(pltpu.roll(rows[p], 64, 1) * lax.rsqrt(pivots))
    return jnp.concatenate(done, axis=0)[:, 0:64]


def kernel(
    bounds_ref, x_hbm, pot_hbm, fields, ritz_ref,
    x_ref, pot_ref, coef, start, even, odd, filt, filtered, diag_rows, diag, pot_own, slab, ops, apply_ops,
    gm, scattered, summed, total, ortho,
    in_sem, pot_send, pot_recv, ghost_send, ghost_recv, vec_send, vec_recv, small_send, small_recv,
    back_send, back_recv,
):
    s = lax.axis_index("strip")
    v = lax.axis_index("vec")
    y_lo = s // 2 % 2
    along = s // 4 * 2 + s % 2
    across = y_lo * NV + v
    flipped = s + 2 - 4 * y_lo

    barrier = pltpu.get_barrier_semaphore()

    def greet(j, carry):
        peer = lax.rem(v + j, NV)
        for where in ({"strip": s, "vec": peer}, {"strip": flipped, "vec": peer}, {"strip": lax.rem(s + j, NS), "vec": v}):
            pl.semaphore_signal(barrier, inc=1, device_id=where, device_id_type=pl.DeviceIdType.MESH)
        return carry

    pot_in = pltpu.make_async_copy(pot_hbm, pot_ref, in_sem.at[0])
    x_in = pltpu.make_async_copy(x_hbm, x_ref, in_sem.at[1])
    pot_in.start()
    x_in.start()
    lax.fori_loop(1, NV, greet, 0)

    def splat(i):
        return jnp.full((8, 128), bounds_ref[i], jnp.int32).astype(F32) * grid_unit

    edges = [splat(i) for i in range(4)]
    center = (edges[0] + edges[1]) * 0.5
    spread = (edges[1] - edges[0]) * 0.5
    scale = 2.0 / spread

    pot_in.wait()
    for r in range(ROWS // 8):
        tiles = []
        for t in range(SUB):
            level = pot_ref[8 * r:8 * r + 8, 128 * t:128 * t + 128].astype(F32)
            tiles.append(disorder * (level / (POT_LEVELS - 1) - 0.5))
        for c, field in enumerate(to_classes(tiles)):
            pot_own[pl.ds(64 * r + place(c), 8, stride=8), :] = field
            diag_rows[pl.ds(OWN + 64 * r + place(c), 8, stride=8), :] = (field - center) * scale

    x_in.wait()

    def classes_of(q, carry):
        for r in range(ROWS // 8):
            tiles = [0.5 * x_ref[q, 8 * r:8 * r + 8, 128 * t:128 * t + 128] for t in range(SUB)]
            for c, tile in enumerate(to_classes(tiles)):
                start[q, pl.ds(OWN + 64 * r + place(c), 8, stride=8), :] = tile
        return carry

    classes_of(0, 0)

    pl.semaphore_wait(barrier, 3 * (NV - 1))

    up = lax.rem(s + NS - 1, NS)
    down = lax.rem(s + 1, NS)
    up2 = lax.rem(s + NS - 2, NS)

    def pot_copies():
        mine = diag_rows.at[pl.ds(OWN, OWN)]
        return (
            remote(mine, diag_rows.at[pl.ds(2 * OWN, OWN)], pot_send.at[0], pot_recv.at[0], strip=up),
            remote(mine, diag_rows.at[pl.ds(0, OWN)], pot_send.at[1], pot_recv.at[1], strip=down),
        )

    def ghost_copies(q):
        mine = start.at[q, pl.ds(OWN, OWN)]
        return (
            remote(mine, start.at[q, pl.ds(2 * OWN, OWN)], ghost_send.at[q, 0], ghost_recv.at[q, 0], strip=up),
            remote(mine, start.at[q, pl.ds(0, OWN)], ghost_send.at[q, 1], ghost_recv.at[q, 1], strip=down),
            remote(
                start.at[q, pl.ds(OWN, SUB)], start.at[q, pl.ds(3 * OWN, SUB)],
                ghost_send.at[q, 2], ghost_recv.at[q, 2], strip=up2,
            ),
        )

    def start_ghosts(q):
        for copy in ghost_copies(q):
            copy.start()

    for copy in pot_copies():
        copy.start()
    start_ghosts(0)
    lax.fori_loop(1, NQ, classes_of, 0)

    theta_lo = arccos((edges[2] - center) / spread)
    theta_hi = arccos((edges[3] - center) / spread)
    coef[0:8] = (theta_lo - theta_hi) / math.pi

    def coefficient(k, carry):
        order = jnp.full((8, 128), k, jnp.int32).astype(F32)
        coef[pl.ds(pl.multiple_of(8 * k, 8), 8)] = (
            2.0 * (jnp.sin(order * theta_lo) - jnp.sin(order * theta_hi)) / (order * math.pi)
        )
        return carry

    lax.fori_loop(1, DEGREE + 1, coefficient, 0)

    def pair_place(row):
        return (16 * row, 0) if row <= 48 else (16 * (96 - row), 1)

    for copy in pot_copies():
        copy.wait()
    for row in range(1, 3 * ROWS):
        value = diag_rows[8 * row:8 * row + 8]
        for base, half in {pair_place(row), (16 * (96 - row), 1) if row == 48 else pair_place(row)}:
            diag[pl.ds(base + half, 8, stride=2), :] = value

    sub = lax.broadcasted_iota(jnp.int32, (8, 128), 0)
    lane = lax.broadcasted_iota(jnp.int32, (8, 128), 1)
    index_left = jnp.where(sub >= 6, (lane + 127) % 128, lane)
    index_right = jnp.where(sub < 2, (lane + 1) % 128, lane)
    upper = (sub % 2 == 0)[None, None]

    def shift(value, index, by):
        index = jnp.broadcast_to(index[None], value.shape)
        return pltpu.roll(jnp.take_along_axis(value, index, axis=2), by, 1)

    def update(k, low, high):
        now, then = (even, odd) if k % 2 else (odd, even)
        rows = high - low
        top = min(high + 1, PAIRS)
        ext = now[(low - 1) * 16:top * 16].reshape(top - low + 1, 2, 8, 128)
        above = ext[0:rows]
        mid = ext[1:rows + 1]
        if high == PAIRS:
            crossing = ext[rows - 1:rows]
            crossing = jnp.where(upper, pltpu.roll(crossing, 7, 2), pltpu.roll(crossing, 1, 2))
            below = jnp.concatenate([ext[2:rows + 1], crossing], axis=0)
        else:
            below = ext[2:rows + 2]
        left = shift(mid[:, 1], index_left, 2)
        right = shift(mid[:, 0], index_right, 6)
        before = then[low * 16:high * 16].reshape(rows, 2, 8, 128)
        local = diag[low * 16:high * 16].reshape(rows, 2, 8, 128)
        parts = []
        for j, beside in enumerate((left + mid[:, 1], mid[:, 0] + right)):
            old = before[:, j]
            if k == 2:
                old = old + old
            parts.append((local[:, j] * mid[:, j] - old) - scale * ((above[:, j] + below[:, j]) + beside))
        after = jnp.stack(parts, axis=1)
        then[low * 16:high * 16] = after.reshape(rows * 16, 128)
        if k % 2 == 0 and high == PAIRS:
            first = max(ROWS, low)
            c_now = coef[8 * k - 8:8 * k]
            c_next = coef[8 * k:8 * k + 8]
            term = c_now * mid[first - low:] + c_next * after[first - low:]
            place_in = slice((first - ROWS) * 16, (PAIRS - ROWS) * 16)
            filt[place_in] = filt[place_in] + term.reshape((PAIRS - first) * 16, 128)

    def vec_copy(q, j):
        peer = lax.rem(v + j, NV)
        return remote(
            filtered.at[q, pl.ds(peer * CHUNKS, HALO)], slab.at[pl.ds((v * NQ + q) * HALO, HALO)],
            vec_send.at[q], vec_recv.at[q], vec=peer,
        )

    def one_vector(q, carry):
        for copy in ghost_copies(q):
            copy.wait()

        @pl.when(q < NQ - 1)
        def _():
            start_ghosts(q + 1)

        for row in range(3 * ROWS + 1):
            value = start[q, 8 * row:8 * row + 8]
            base, half = pair_place(row)
            even[pl.ds(base + half, 8, stride=2), :] = value
            if row == 48:
                even[pl.ds(base + 1, 8, stride=2), :] = value
        odd[...] = jnp.zeros((16 * PAIRS, 128), F32)
        filt[...] = (
            (2.0 * coef[0:8]) * even[16 * ROWS:16 * PAIRS].reshape(2 * (PAIRS - ROWS), 8, 128)
        ).reshape(16 * (PAIRS - ROWS), 128)
        for k in range(1, DEGREE + 1):
            if k < ROWS - 1:
                update(k, k, ROWS)
                update(k, ROWS, PAIRS)
            else:
                update(k, k, PAIRS)
        for row in range(ROWS + 1):
            base, half = pair_place(ROWS + row)
            filtered[q, 8 * row:8 * row + 8] = filt[pl.ds(base - 16 * ROWS + half, 8, stride=2), :]
        slab[pl.ds((v * NQ + q) * HALO, HALO)] = filtered[q, pl.ds(v * CHUNKS, HALO)]

        def send(j, inner):
            vec_copy(q, j).start()
            return inner

        lax.fori_loop(1, NV, send, 0)
        return carry

    lax.fori_loop(0, NQ, one_vector, 0)
    for q in range(NQ):
        wait_bytes(slab.at[pl.ds(0, (NV - 1) * HALO)], vec_recv.at[q])

    lane16 = lax.broadcasted_iota(jnp.int32, (16, 128), 1)
    pot_slab = pot_own[pl.ds(v * CHUNKS, CHUNKS)] * 0.5

    def chunk(g, n):
        base = 16 * g * HALO + n
        return jnp.concatenate(
            [slab[pl.ds(base, 8, stride=HALO), :], slab[pl.ds(base + 8 * HALO, 8, stride=HALO), :]], axis=0
        )

    for g in range(NVEC // 16):
        y = [chunk(g, n) for n in range(HALO)]
        for row in range(PIECE):
            for c in range(SUB):
                n = SUB * row + place(c)
                if c < SUB - 1:
                    right = y[SUB * row + place(c + 1)]
                else:
                    right = pltpu.roll(y[SUB * row + place(0)], 127, 1)
                z = pot_slab[n:n + 1] * y[n] - (right + y[n + SUB])
                for part, value in enumerate(split(y[n]) + split(z)):
                    ops[64 * part + 16 * g:64 * part + 16 * g + 16, 128 * n:128 * n + 128] = value
    prod = lax.dot_general(
        ops[...], ops[0:128, :], (((1,), (1,)), ((), ())), preferred_element_type=F32
    )
    rows64 = lax.broadcasted_iota(jnp.int32, (64, 128), 0)
    lanes64 = lax.broadcasted_iota(jnp.int32, (64, 128), 1)
    gram_part = prod[0:64] + prod[64:128]
    cross_part = prod[128:192] + prod[192:256]
    gm[...] = jnp.where(
        lanes64 < 64, gram_part + pltpu.roll(gram_part, 64, 1), cross_part + pltpu.roll(cross_part, 64, 1)
    )

    def to_along(stage, source, target):
        def send(j, carry):
            peer = lax.rem(along + j, NA)
            strip = peer // 2 * 4 + y_lo * 2 + peer % 2
            remote(source(peer), target, small_send.at[stage], small_recv.at[stage], strip=strip).start()
            return carry

        lax.fori_loop(1, NA, send, 0)

    mine_a = pl.ds(along * 8, 8)
    mine_b = pl.ds(across * 8, 8)
    scattered[mine_a] = gm[mine_a]
    to_along(0, lambda peer: gm.at[pl.ds(peer * 8, 8)], scattered.at[mine_a])

    for g in range(NVEC // 16):
        for row in range(PIECE):
            tiles = from_classes([chunk(g, SUB * row + place(c)) for c in range(SUB)])
            for t, tile in enumerate(tiles):
                n = SUB * row + t
                for part, value in enumerate(split(tile)):
                    apply_ops[64 * part + 16 * g:64 * part + 16 * g + 16, 128 * n:128 * n + 128] = value

    wait_bytes(scattered.at[pl.ds(0, 8 * (NA - 1))], small_recv.at[0])
    summed[mine_b] = jnp.sum(scattered[...].reshape(NA, 8, 128), axis=0)

    def send_across(j, carry):
        peer = lax.rem(across + j, NB)
        strip = s + 2 * (peer // NV - y_lo)
        remote(
            summed.at[mine_b], summed.at[mine_b], small_send.at[1], small_recv.at[1], strip=strip, vec=peer % NV
        ).start()
        return carry

    lax.fori_loop(1, NB, send_across, 0)
    wait_bytes(summed.at[pl.ds(0, 8 * (NB - 1))], small_recv.at[1])
    total[mine_a] = jnp.sum(summed[...].reshape(NB, 8, 128), axis=0)
    to_along(2, lambda peer: total.at[mine_a], total.at[mine_a])
    wait_bytes(total.at[pl.ds(0, 8 * (NA - 1))], small_recv.at[2])

    inverse = inverse_factor(jnp.where(lanes64 < 64, total[...], jnp.where(lanes64 - 64 == rows64, 1.0, 0.0)))

    high, low = split(math.sqrt(SITES) * inverse)
    left = jnp.concatenate(
        [jnp.concatenate([high, high], axis=1), jnp.concatenate([low, low], axis=1)], axis=0
    )
    product = jnp.dot(left, apply_ops[...], preferred_element_type=F32)
    for n in range(CHUNKS):
        value = product[0:64, 128 * n:128 * n + 128] + product[64:128, 128 * n:128 * n + 128]
        for g in range(8):
            ortho[pl.ds(n + 8 * g * CHUNKS, 8, stride=CHUNKS), :] = value[8 * g:8 * g + 8]

    def back_copy(j, q):
        peer = lax.rem(v + j, NV)
        return remote(
            ortho.at[pl.ds((peer * NQ + q) * CHUNKS, CHUNKS)], fields.at[q, pl.ds(v * CHUNKS, CHUNKS)],
            back_send.at[0], back_recv.at[0], vec=peer,
        )

    def send_back(j, carry):
        for q in range(NQ):
            back_copy(j, q).start()
        return carry

    lax.fori_loop(1, NV, send_back, 0)
    for q in range(NQ):
        fields[q, pl.ds(v * CHUNKS, CHUNKS)] = ortho[pl.ds((v * NQ + q) * CHUNKS, CHUNKS)]

    cross = pltpu.roll(total[...], 64, 1)[:, 0:64]
    cross = cross + cross.T
    half = jnp.dot(inverse, cross, precision=lax.Precision.HIGHEST, preferred_element_type=F32)
    ritz_ref[...] = float(ROWS) * lax.dot_general(
        inverse, half, (((1,), (1,)), ((), ())), precision=lax.Precision.HIGHEST, preferred_element_type=F32
    )

    wait_bytes(ortho.at[pl.ds(0, (NV - 1) * NQ * CHUNKS)], back_recv.at[0])
    wait_bytes(ortho.at[pl.ds(0, (NV - 1) * NQ * CHUNKS)], back_send.at[0])
    wait_bytes(scattered.at[pl.ds(0, 8 * (NA - 1))], small_send.at[0])
    wait_bytes(summed.at[pl.ds(0, 8 * (NB - 1))], small_send.at[1])
    wait_bytes(scattered.at[pl.ds(0, 8 * (NA - 1))], small_send.at[2])
    for q in range(NQ):
        wait_bytes(slab.at[pl.ds(0, (NV - 1) * HALO)], vec_send.at[q])


def arrange(fields, ritz, out_ref, ritz_ref):
    for q in range(NQ):
        for r in range(ROWS // 8):
            for t in range(SUB):
                out_ref[q, 8 * r:8 * r + 8, 128 * t:128 * t + 128] = fields[q, pl.ds(64 * r + t, 8, stride=8), :]
    ritz_ref[...] = ritz[...]


def shards(start_vectors, potential, bounds):
    vmem = pl.BlockSpec(memory_space=pltpu.VMEM)
    hbm = pl.BlockSpec(memory_space=pltpu.HBM)
    dma = pltpu.SemaphoreType.DMA
    ritz_shape = jax.ShapeDtypeStruct((NVEC, NVEC), F32)
    fields, ritz = pl.pallas_call(
        kernel,
        out_shape=(pltpu.VMEM((NQ, OWN, 128), F32), pltpu.VMEM((NVEC, NVEC), F32)),
        in_specs=[pl.BlockSpec(memory_space=pltpu.SMEM), hbm, hbm],
        out_specs=(vmem, vmem),
        scratch_shapes=[
            pltpu.VMEM((NQ, ROWS, 1024), F32),
            pltpu.VMEM((ROWS, 1024), jnp.int32),
            pltpu.VMEM((8 * (DEGREE + 1), 128), F32),
            pltpu.VMEM((NQ, FIELD, 128), F32),
            pltpu.VMEM((16 * PAIRS, 128), F32),
            pltpu.VMEM((16 * PAIRS, 128), F32),
            pltpu.VMEM((16 * (PAIRS - ROWS), 128), F32),
            pltpu.VMEM((NQ, OWN + SUB, 128), F32),
            pltpu.VMEM((FIELD, 128), F32),
            pltpu.VMEM((16 * PAIRS, 128), F32),
            pltpu.VMEM((OWN, 128), F32),
            pltpu.VMEM((NVEC * HALO, 128), F32),
            pltpu.VMEM((256, CHUNKS * 128), BF16),
            pltpu.VMEM((128, CHUNKS * 128), BF16),
            pltpu.VMEM((64, 128), F32),
            pltpu.VMEM((8 * NA, 128), F32),
            pltpu.VMEM((8 * NB, 128), F32),
            pltpu.VMEM((64, 128), F32),
            pltpu.VMEM((NVEC * CHUNKS, 128), F32),
            dma((2,)), dma((2,)), dma((2,)), dma((NQ, 3)), dma((NQ, 3)), dma((NQ,)), dma((NQ,)),
            dma((3,)), dma((3,)), dma((1,)), dma((1,)),
        ],
        compiler_params=pltpu.CompilerParams(
            collective_id=0, has_side_effects=True, vmem_limit_bytes=60 << 20
        ),
        name="filter_ritz",
    )(bounds, start_vectors, potential)
    return pl.pallas_call(
        arrange,
        out_shape=(jax.ShapeDtypeStruct((NQ, ROWS, 1024), F32), ritz_shape),
        in_specs=[vmem, vmem],
        out_specs=(vmem, vmem),
        name="arrange",
    )(pltpu.with_memory_space_constraint(fields, pltpu.VMEM), pltpu.with_memory_space_constraint(ritz, pltpu.VMEM))


def solution(mesh):
    in_specs = (P("vec", "strip", None), P("strip", None), P())
    out_specs = (P("vec", "strip", None), P())
    return jax.shard_map(shards, mesh=mesh, in_specs=in_specs, out_specs=out_specs, check_vma=False)
```

```python
import math

import jax
import jax.numpy as jnp
from jax import lax
from jax.experimental import pallas as pl
from jax.experimental.pallas import tpu as pltpu
from jax.sharding import PartitionSpec as P

DEGREE = 32
POT_LEVELS = 16
NQ = 4
ROWS = 32
NV = 16
NS = 16
NVEC = NQ * NV
PIECE = ROWS // NV
SUB = 8
CHUNKS = PIECE * SUB
FIELD = (3 * ROWS + 1) * SUB
PAIRS = 3 * ROWS // 2 + 1
STRIP_STEPS = sorted(
    ((a, b, c) for a in range(4) for b in range(2) for c in range(2) if a or b or c),
    key=lambda step: -(2 * min(step[0], 4 - step[0]) + 2 * step[1] + step[2]),
)
VEC_STEPS = sorted(
    ((a, b) for a in range(2) for b in range(8) if a or b), key=lambda step: -(2 * step[0] + min(step[1], 8 - step[1]))
)
PART = NVEC // NS
OWN = ROWS * SUB
HALF_PI = math.pi / 2
SITES = NS * ROWS * 1024

grid_unit = 0.0625
disorder = 2.0
F32 = jnp.float32
BF16 = jnp.bfloat16


def remote(src, dst, send, recv, **where):
    return pltpu.make_async_remote_copy(
        src_ref=src, dst_ref=dst, send_sem=send, recv_sem=recv,
        device_id=where, device_id_type=pl.DeviceIdType.MESH,
    )


def wait_bytes(ref, sem):
    pltpu.make_async_copy(ref, ref, sem).wait()


def split(value):
    high = value.astype(BF16)
    return high, (value - high.astype(F32)).astype(BF16)


def arccos(x):
    size = jnp.abs(x)
    large = size > 0.5
    square = jnp.where(large, 0.5 * (1.0 - size), x * x)
    base = jnp.where(large, jnp.sqrt(square), size)
    poly = 4.2163199048e-2 * square + 2.4181311049e-2
    poly = poly * square + 4.5470025998e-2
    poly = poly * square + 7.4953002686e-2
    poly = poly * square + 1.6666752422e-1
    arcsin = base + base * square * poly
    positive = jnp.where(large, 2.0 * arcsin, HALF_PI - arcsin)
    return jnp.where(x < 0.0, math.pi - positive, positive)


def place(s):
    return 4 * (s % 2) + s // 2


def turn_blocks(tiles):
    tiles = list(tiles)
    block = lax.broadcasted_iota(jnp.int32, tiles[0].shape, 1) // 16
    for bit in (1, 2, 4):
        clear = (block & bit) == 0
        for i in range(8):
            if i & bit == 0:
                one, two = tiles[i], tiles[i + bit]
                tiles[i] = jnp.where(clear, one, pltpu.roll(two, 16 * bit, 1))
                tiles[i + bit] = jnp.where(clear, pltpu.roll(one, 128 - 16 * bit, 1), two)
    return tiles


def to_classes(tiles):
    lane = lax.broadcasted_iota(jnp.int32, tiles[0].shape, 1)
    index = 8 * (lane % 16) + lane // 16
    return turn_blocks([jnp.take_along_axis(tile, index, axis=1) for tile in tiles])


def from_classes(tiles):
    lane = lax.broadcasted_iota(jnp.int32, tiles[0].shape, 1)
    index = 16 * (lane % 8) + lane // 8
    return [jnp.take_along_axis(tile, index, axis=1) for tile in turn_blocks(tiles)]


def inverse_factor(aug):
    rows = [aug[8 * i:8 * i + 8] for i in range(8)]
    sub = lax.broadcasted_iota(jnp.int32, (8, 128), 0)
    done = []

    def spread(value, k):
        return jnp.broadcast_to(value[k:k + 1], (8, 128))

    for p in range(8):
        columns = {
            (j, i): jnp.broadcast_to(rows[i][:, 8 * p + j:8 * p + j + 1], (8, 128))
            for i in range(p, 8) for j in range(8)
        }
        pivots = spread(columns[0, p], 0)
        for k in range(8):
            pivot = spread(columns[k, p], k)
            pivots = jnp.where(sub == k, pivot, pivots)
            inverse = 1.0 / pivot
            row = spread(rows[p], k)
            heads = {j: spread(columns[j, p], k) for j in range(k + 1, 8)}
            for i in range(p, 8):
                factor = columns[k, i] * inverse
                if i == p:
                    factor = jnp.where(sub > k, factor, 0.0)
                rows[i] = rows[i] - factor * row
                for j in range(k + 1, 8):
                    columns[j, i] = columns[j, i] - factor * heads[j]
        done.append(pltpu.roll(rows[p], 64, 1) * lax.rsqrt(pivots))
    return jnp.concatenate(done, axis=0)[:, 0:64]


def kernel(
    bounds_ref, x_hbm, pot_hbm, fields, ritz_ref,
    x_ref, pot_ref, coef, start, even, odd, filt, filtered, diag_rows, diag, pot_own, slab, halos, ops_y, ops_z, apply_ops,
    parts, scattered, summed, total, ortho,
    in_sem, pot_send, pot_recv, ghost_send, ghost_recv, vec_send, vec_recv, halo_send, halo_recv, small_send, small_recv,
    back_send, back_recv,
):
    s = lax.axis_index("strip")
    v = lax.axis_index("vec")
    y_lo = s // 2 % 2

    barrier = pltpu.get_barrier_semaphore()

    def greet(j, carry):
        for where in ({"vec": lax.rem(v + j, NV)}, {"strip": lax.rem(s + j, NS)}):
            pl.semaphore_signal(barrier, inc=1, device_id=where, device_id_type=pl.DeviceIdType.MESH)
        return carry

    pot_in = pltpu.make_async_copy(pot_hbm, pot_ref, in_sem.at[0])
    x_in = pltpu.make_async_copy(x_hbm, x_ref, in_sem.at[1])
    pot_in.start()
    x_in.start()
    lax.fori_loop(1, NV, greet, 0)

    def splat(i):
        return jnp.full((8, 128), bounds_ref[i], jnp.int32).astype(F32) * grid_unit

    edges = [splat(i) for i in range(4)]
    center = (edges[0] + edges[1]) * 0.5
    spread = (edges[1] - edges[0]) * 0.5
    scale = 2.0 / spread

    pot_in.wait()
    for r in range(ROWS // 8):
        tiles = []
        for t in range(SUB):
            level = pot_ref[8 * r:8 * r + 8, 128 * t:128 * t + 128].astype(F32)
            tiles.append(disorder * (level / (POT_LEVELS - 1) - 0.5))
        for c, field in enumerate(to_classes(tiles)):
            pot_own[pl.ds(64 * r + place(c), 8, stride=8), :] = field
            diag_rows[pl.ds(OWN + 64 * r + place(c), 8, stride=8), :] = (field - center) * scale

    x_in.wait()

    def classes_of(q, carry):
        for r in range(ROWS // 8):
            tiles = [0.5 * x_ref[q, 8 * r:8 * r + 8, 128 * t:128 * t + 128] for t in range(SUB)]
            for c, tile in enumerate(to_classes(tiles)):
                start[q, pl.ds(OWN + 64 * r + place(c), 8, stride=8), :] = tile
        return carry

    classes_of(0, 0)

    pl.semaphore_wait(barrier, NV + NS - 2)

    up = lax.rem(s + NS - 1, NS)
    down = lax.rem(s + 1, NS)
    up2 = lax.rem(s + NS - 2, NS)

    def pot_copies():
        mine = diag_rows.at[pl.ds(OWN, OWN)]
        return (
            remote(mine, diag_rows.at[pl.ds(2 * OWN, OWN)], pot_send.at[0], pot_recv.at[0], strip=up),
            remote(mine, diag_rows.at[pl.ds(0, OWN)], pot_send.at[1], pot_recv.at[1], strip=down),
        )

    def ghost_copies(q):
        mine = start.at[q, pl.ds(OWN, OWN)]
        return (
            remote(mine, start.at[q, pl.ds(2 * OWN, OWN)], ghost_send.at[q, 0], ghost_recv.at[q, 0], strip=up),
            remote(mine, start.at[q, pl.ds(0, OWN)], ghost_send.at[q, 1], ghost_recv.at[q, 1], strip=down),
            remote(
                start.at[q, pl.ds(OWN, SUB)], start.at[q, pl.ds(3 * OWN, SUB)],
                ghost_send.at[q, 2], ghost_recv.at[q, 2], strip=up2,
            ),
        )

    def start_ghosts(q):
        for copy in ghost_copies(q):
            copy.start()

    for copy in pot_copies():
        copy.start()
    start_ghosts(0)
    lax.fori_loop(1, NQ, classes_of, 0)

    theta_lo = arccos((edges[2] - center) / spread)
    theta_hi = arccos((edges[3] - center) / spread)
    coef[0:8] = (theta_lo - theta_hi) / math.pi

    def coefficient(k, carry):
        order = jnp.full((8, 128), k, jnp.int32).astype(F32)
        coef[pl.ds(pl.multiple_of(8 * k, 8), 8)] = (
            2.0 * (jnp.sin(order * theta_lo) - jnp.sin(order * theta_hi)) / (order * math.pi)
        )
        return carry

    lax.fori_loop(1, DEGREE + 1, coefficient, 0)

    def pair_place(row):
        return (16 * row, 0) if row <= 48 else (16 * (96 - row), 1)

    for copy in pot_copies() + ghost_copies(0):
        copy.wait_send()
    start_ghosts(1)

    for copy in pot_copies():
        copy.wait_recv()
    for row in range(1, 3 * ROWS):
        value = diag_rows[8 * row:8 * row + 8]
        for base, half in {pair_place(row), (16 * (96 - row), 1) if row == 48 else pair_place(row)}:
            diag[pl.ds(base + half, 8, stride=2), :] = value

    sub = lax.broadcasted_iota(jnp.int32, (8, 128), 0)
    lane = lax.broadcasted_iota(jnp.int32, (8, 128), 1)
    index_left = jnp.where(sub >= 6, (lane + 127) % 128, lane)
    index_right = jnp.where(sub < 2, (lane + 1) % 128, lane)
    upper = (sub % 2 == 0)[None, None]

    def shift(value, index, by):
        index = jnp.broadcast_to(index[None], value.shape)
        return pltpu.roll(jnp.take_along_axis(value, index, axis=2), by, 1)

    def update(k, low, high):
        now, then = (even, odd) if k % 2 else (odd, even)
        rows = high - low
        top = min(high + 1, PAIRS)
        ext = now[(low - 1) * 16:top * 16].reshape(top - low + 1, 2, 8, 128)
        above = ext[0:rows]
        mid = ext[1:rows + 1]
        if high == PAIRS:
            crossing = ext[rows - 1:rows]
            crossing = jnp.where(upper, pltpu.roll(crossing, 7, 2), pltpu.roll(crossing, 1, 2))
            below = jnp.concatenate([ext[2:rows + 1], crossing], axis=0)
        else:
            below = ext[2:rows + 2]
        left = shift(mid[:, 1], index_left, 2)
        right = shift(mid[:, 0], index_right, 6)
        before = then[low * 16:high * 16].reshape(rows, 2, 8, 128) if k > 1 else None
        local = diag[low * 16:high * 16].reshape(rows, 2, 8, 128)
        halves = []
        for j, beside in enumerate((left + mid[:, 1], mid[:, 0] + right)):
            inside = local[:, j] * mid[:, j]
            if k == 2:
                inside = inside - (before[:, j] + before[:, j])
            elif k > 2:
                inside = inside - before[:, j]
            halves.append(inside - scale * ((above[:, j] + below[:, j]) + beside))
        after = jnp.stack(halves, axis=1)
        then[low * 16:high * 16] = after.reshape(rows * 16, 128)
        if k % 2 == 0 and high == PAIRS:
            first = max(ROWS, low)
            c_now = coef[8 * k - 8:8 * k]
            c_next = coef[8 * k:8 * k + 8]
            term = c_now * mid[first - low:] + c_next * after[first - low:]
            place_in = slice((first - ROWS) * 16, (PAIRS - ROWS) * 16)
            filt[place_in] = filt[place_in] + term.reshape((PAIRS - first) * 16, 128)

    def vec_copy(q, j):
        peer = lax.rem(v + j, NV)
        return remote(
            filtered.at[q, pl.ds(peer * CHUNKS, CHUNKS)], slab.at[pl.ds((v * NQ + q) * CHUNKS, CHUNKS)],
            vec_send.at[q], vec_recv.at[q], vec=peer,
        )

    def one_vector(q, carry):
        for copy in ghost_copies(q):
            copy.wait_recv()
        for row in range(3 * ROWS + 1):
            value = start[q, 8 * row:8 * row + 8]
            base, half = pair_place(row)
            even[pl.ds(base + half, 8, stride=2), :] = value
            if row == 48:
                even[pl.ds(base + 1, 8, stride=2), :] = value
        filt[...] = (
            (2.0 * coef[0:8]) * even[16 * ROWS:16 * PAIRS].reshape(2 * (PAIRS - ROWS), 8, 128)
        ).reshape(16 * (PAIRS - ROWS), 128)
        for k in range(1, DEGREE + 1):
            if k < ROWS - 1:
                update(k, k, ROWS)
                update(k, ROWS, PAIRS)
            else:
                update(k, k, PAIRS)
            if k == DEGREE // 2:
                @pl.when(q < NQ - 2)
                def _():
                    for copy in ghost_copies(q + 1):
                        copy.wait_send()
                    start_ghosts(q + 2)

        for row in range(ROWS + 1):
            base, half = pair_place(ROWS + row)
            filtered[q, 8 * row:8 * row + 8] = filt[pl.ds(base - 16 * ROWS + half, 8, stride=2), :]
        slab[pl.ds((v * NQ + q) * CHUNKS, CHUNKS)] = filtered[q, pl.ds(v * CHUNKS, CHUNKS)]

        def send(j, inner):
            vec_copy(q, j).start()
            return inner

        lax.fori_loop(1, NV, send, 0)
        return carry

    lax.fori_loop(0, NQ, one_vector, 0)

    def send_halos(j, carry):
        peer = lax.rem(v + j, NV)
        for q in range(NQ):
            remote(
                filtered.at[q, pl.ds(peer * CHUNKS + CHUNKS, SUB)], halos.at[pl.ds((v * NQ + q) * SUB, SUB)],
                halo_send.at[0], halo_recv.at[0], vec=peer,
            ).start()
        return carry

    lax.fori_loop(1, NV, send_halos, 0)
    for q in range(NQ):
        halos[pl.ds((v * NQ + q) * SUB, SUB)] = filtered[q, pl.ds(v * CHUNKS + CHUNKS, SUB)]
    for q in range(NQ):
        wait_bytes(slab.at[pl.ds(0, (NV - 1) * CHUNKS)], vec_recv.at[q])

    def take(source, stride, g, n):
        base = 16 * g * stride + n
        return jnp.concatenate(
            [source[pl.ds(base, 8, stride=stride), :], source[pl.ds(base + 8 * stride, 8, stride=stride), :]], axis=0
        )

    def keep(target, g, n, value):
        for part, half in enumerate(split(value)):
            target[64 * part + 16 * g:64 * part + 16 * g + 16, 128 * n:128 * n + 128] = half

    def matrix_part(left):
        prod = lax.dot_general(left[...], ops_y[...], (((1,), (1,)), ((), ())), preferred_element_type=F32)
        return prod[0:64] + prod[64:128]

    def along_strip(stage, i, source, target):
        for a, b, c in STRIP_STEPS:
            peer = lax.rem(s // 4 + a, 4) * 4 + lax.rem(y_lo + b, 2) * 2 + lax.rem(s % 2 + c, 2)
            remote(source(peer), target, small_send.at[i, stage], small_recv.at[i, stage], strip=peer).start()

    def scatter(i, value):
        for c in range(NS):
            parts[i, c] = value[PART * c:PART * c + PART]
        scattered[i, s] = parts[i, s]
        along_strip(0, i, lambda peer: parts.at[i, peer], scattered.at[i, s])

    def exchange(i):
        wait_bytes(scattered.at[i, pl.ds(0, NS - 1)], small_recv.at[i, 0])
        summed[i, v] = jnp.sum(scattered[i], axis=0)
        for a, b in VEC_STEPS:
            peer = lax.rem(v // 8 + a, 2) * 8 + lax.rem(v % 8 + b, 8)
            remote(
                summed.at[i, v], summed.at[i, v], small_send.at[i, 1], small_recv.at[i, 1], vec=peer
            ).start()

    def gather(i):
        wait_bytes(summed.at[i, pl.ds(0, NV - 1)], small_recv.at[i, 1])
        total[i, s] = jnp.sum(summed[i], axis=0)
        along_strip(2, i, lambda peer: total.at[i, s], total.at[i, s])

    def finish(i):
        wait_bytes(total.at[i, pl.ds(0, NS - 1)], small_recv.at[i, 2])
        value = jnp.concatenate([total[i, c] for c in range(NS)], axis=0)
        return value + pltpu.roll(value, 64, 1)

    for g in range(NVEC // 16):
        for n in range(CHUNKS):
            keep(ops_y, g, n, take(slab, CHUNKS, g, n))
    scatter(0, matrix_part(ops_y))

    for g in range(NVEC // 16):
        for row in range(PIECE):
            tiles = from_classes([take(slab, CHUNKS, g, SUB * row + place(c)) for c in range(SUB)])
            for t, tile in enumerate(tiles):
                keep(apply_ops, g, SUB * row + t, tile)
    exchange(0)

    wait_bytes(halos.at[pl.ds(0, (NV - 1) * NQ * SUB)], halo_recv.at[0])
    pot_slab = pot_own[pl.ds(v * CHUNKS, CHUNKS)] * 0.5
    for g in range(NVEC // 16):
        y = [take(slab, CHUNKS, g, n) for n in range(CHUNKS)]
        y += [take(halos, SUB, g, n) for n in range(SUB)]
        for row in range(PIECE):
            for c in range(SUB):
                n = SUB * row + place(c)
                if c < SUB - 1:
                    right = y[SUB * row + place(c + 1)]
                else:
                    right = pltpu.roll(y[SUB * row + place(0)], 127, 1)
                keep(ops_z, g, n, pot_slab[n:n + 1] * y[n] - (right + y[n + SUB]))
    scatter(1, matrix_part(ops_z))
    gather(0)
    exchange(1)

    rows64 = lax.broadcasted_iota(jnp.int32, (64, 128), 0)
    lanes64 = lax.broadcasted_iota(jnp.int32, (64, 128), 1)
    gram = finish(0)
    inverse = inverse_factor(jnp.where(lanes64 < 64, gram, jnp.where(lanes64 - 64 == rows64, 1.0, 0.0)))

    high, low = split(math.sqrt(SITES) * inverse)
    left = jnp.concatenate(
        [jnp.concatenate([high, high], axis=1), jnp.concatenate([low, low], axis=1)], axis=0
    )
    product = jnp.dot(left, apply_ops[...], preferred_element_type=F32)
    for n in range(CHUNKS):
        value = product[0:64, 128 * n:128 * n + 128] + product[64:128, 128 * n:128 * n + 128]
        for g in range(8):
            ortho[pl.ds(n + 8 * g * CHUNKS, 8, stride=CHUNKS), :] = value[8 * g:8 * g + 8]

    def back_copy(j, q):
        peer = lax.rem(v + j, NV)
        return remote(
            ortho.at[pl.ds((peer * NQ + q) * CHUNKS, CHUNKS)], fields.at[q, pl.ds(v * CHUNKS, CHUNKS)],
            back_send.at[0], back_recv.at[0], vec=peer,
        )

    def send_back(j, carry):
        for q in range(NQ):
            back_copy(j, q).start()
        return carry

    lax.fori_loop(1, NV, send_back, 0)
    for q in range(NQ):
        fields[q, pl.ds(v * CHUNKS, CHUNKS)] = ortho[pl.ds((v * NQ + q) * CHUNKS, CHUNKS)]

    gather(1)
    cross = finish(1)[:, 0:64]
    cross = cross + cross.T
    half = jnp.dot(inverse, cross, precision=lax.Precision.HIGHEST, preferred_element_type=F32)
    ritz_ref[...] = float(ROWS) * lax.dot_general(
        inverse, half, (((1,), (1,)), ((), ())), precision=lax.Precision.HIGHEST, preferred_element_type=F32
    )

    wait_bytes(ortho.at[pl.ds(0, (NV - 1) * NQ * CHUNKS)], back_recv.at[0])
    wait_bytes(ortho.at[pl.ds(0, (NV - 1) * NQ * CHUNKS)], back_send.at[0])
    for i in range(2):
        for stage in range(3):
            wait_bytes(total.at[i, pl.ds(0, NS - 1)], small_send.at[i, stage])
    wait_bytes(halos.at[pl.ds(0, (NV - 1) * NQ * SUB)], halo_send.at[0])
    for q in range(NQ):
        wait_bytes(slab.at[pl.ds(0, (NV - 1) * CHUNKS)], vec_send.at[q])
    for copy in ghost_copies(NQ - 1):
        copy.wait_send()


def arrange(fields, ritz, out_ref, ritz_ref):
    for q in range(NQ):
        for r in range(ROWS // 8):
            for t in range(SUB):
                out_ref[q, 8 * r:8 * r + 8, 128 * t:128 * t + 128] = fields[q, pl.ds(64 * r + t, 8, stride=8), :]
    ritz_ref[...] = ritz[...]


def shards(start_vectors, potential, bounds):
    vmem = pl.BlockSpec(memory_space=pltpu.VMEM)
    hbm = pl.BlockSpec(memory_space=pltpu.HBM)
    dma = pltpu.SemaphoreType.DMA
    ritz_shape = jax.ShapeDtypeStruct((NVEC, NVEC), F32)
    fields, ritz = pl.pallas_call(
        kernel,
        out_shape=(pltpu.VMEM((NQ, OWN, 128), F32), pltpu.VMEM((NVEC, NVEC), F32)),
        in_specs=[pl.BlockSpec(memory_space=pltpu.SMEM), hbm, hbm],
        out_specs=(vmem, vmem),
        scratch_shapes=[
            pltpu.VMEM((NQ, ROWS, 1024), F32),
            pltpu.VMEM((ROWS, 1024), jnp.int32),
            pltpu.VMEM((8 * (DEGREE + 1), 128), F32),
            pltpu.VMEM((NQ, FIELD, 128), F32),
            pltpu.VMEM((16 * PAIRS, 128), F32),
            pltpu.VMEM((16 * PAIRS, 128), F32),
            pltpu.VMEM((16 * (PAIRS - ROWS), 128), F32),
            pltpu.VMEM((NQ, OWN + SUB, 128), F32),
            pltpu.VMEM((FIELD, 128), F32),
            pltpu.VMEM((16 * PAIRS, 128), F32),
            pltpu.VMEM((OWN, 128), F32),
            pltpu.VMEM((NVEC * CHUNKS, 128), F32),
            pltpu.VMEM((NVEC * SUB, 128), F32),
            pltpu.VMEM((128, CHUNKS * 128), BF16),
            pltpu.VMEM((128, CHUNKS * 128), BF16),
            pltpu.VMEM((128, CHUNKS * 128), BF16),
            pltpu.VMEM((2, NS, PART, 128), F32),
            pltpu.VMEM((2, NS, PART, 128), F32),
            pltpu.VMEM((2, NV, PART, 128), F32),
            pltpu.VMEM((2, NS, PART, 128), F32),
            pltpu.VMEM((NVEC * CHUNKS, 128), F32),
            dma((2,)), dma((2,)), dma((2,)), dma((NQ, 3)), dma((NQ, 3)), dma((NQ,)), dma((NQ,)), dma((1,)), dma((1,)),
            dma((2, 3)), dma((2, 3)), dma((1,)), dma((1,)),
        ],
        compiler_params=pltpu.CompilerParams(
            collective_id=0, has_side_effects=True, vmem_limit_bytes=60 << 20
        ),
        name="filter_ritz",
    )(bounds, start_vectors, potential)
    return pl.pallas_call(
        arrange,
        out_shape=(jax.ShapeDtypeStruct((NQ, ROWS, 1024), F32), ritz_shape),
        in_specs=[vmem, vmem],
        out_specs=(vmem, vmem),
        name="arrange",
    )(pltpu.with_memory_space_constraint(fields, pltpu.VMEM), pltpu.with_memory_space_constraint(ritz, pltpu.VMEM))


def solution(mesh):
    in_specs = (P("vec", "strip", None), P("strip", None), P())
    out_specs = (P("vec", "strip", None), P())
    return jax.shard_map(shards, mesh=mesh, in_specs=in_specs, out_specs=out_specs, check_vma=False)
```

```python
import math

import jax
import jax.numpy as jnp
from jax import lax
from jax.experimental import pallas as pl
from jax.experimental.pallas import tpu as pltpu
from jax.sharding import PartitionSpec as P

DEGREE = 32
POT_LEVELS = 16
NQ = 4
ROWS = 32
NV = 16
NS = 16
NVEC = NQ * NV
PIECE = ROWS // NV
SUB = 8
CHUNKS = PIECE * SUB
FIELD = (3 * ROWS + 1) * SUB
PAIRS = 3 * ROWS // 2 + 1
STRIP_STEPS = sorted(
    ((a, b, c) for a in range(4) for b in range(2) for c in range(2) if a or b or c),
    key=lambda step: -(2 * min(step[0], 4 - step[0]) + 2 * step[1] + step[2]),
)
VEC_STEPS = sorted(
    ((a, b) for a in range(2) for b in range(8) if a or b), key=lambda step: -(2 * step[0] + min(step[1], 8 - step[1]))
)
PART = NVEC // NS
OWN = ROWS * SUB
HALF_PI = math.pi / 2
SITES = NS * ROWS * 1024

grid_unit = 0.0625
disorder = 2.0
F32 = jnp.float32
BF16 = jnp.bfloat16


def remote(src, dst, send, recv, **where):
    return pltpu.make_async_remote_copy(
        src_ref=src, dst_ref=dst, send_sem=send, recv_sem=recv,
        device_id=where, device_id_type=pl.DeviceIdType.MESH,
    )


def wait_bytes(ref, sem):
    pltpu.make_async_copy(ref, ref, sem).wait()


def split(value):
    high = value.astype(BF16)
    return high, (value - high.astype(F32)).astype(BF16)


def arccos(x):
    size = jnp.abs(x)
    large = size > 0.5
    square = jnp.where(large, 0.5 * (1.0 - size), x * x)
    base = jnp.where(large, jnp.sqrt(square), size)
    poly = 4.2163199048e-2 * square + 2.4181311049e-2
    poly = poly * square + 4.5470025998e-2
    poly = poly * square + 7.4953002686e-2
    poly = poly * square + 1.6666752422e-1
    arcsin = base + base * square * poly
    positive = jnp.where(large, 2.0 * arcsin, HALF_PI - arcsin)
    return jnp.where(x < 0.0, math.pi - positive, positive)


def place(s):
    return 4 * (s % 2) + s // 2


def turn_blocks(tiles):
    tiles = list(tiles)
    block = lax.broadcasted_iota(jnp.int32, tiles[0].shape, 1) // 16
    for bit in (1, 2, 4):
        clear = (block & bit) == 0
        for i in range(8):
            if i & bit == 0:
                one, two = tiles[i], tiles[i + bit]
                tiles[i] = jnp.where(clear, one, pltpu.roll(two, 16 * bit, 1))
                tiles[i + bit] = jnp.where(clear, pltpu.roll(one, 128 - 16 * bit, 1), two)
    return tiles


def to_classes(tiles):
    lane = lax.broadcasted_iota(jnp.int32, tiles[0].shape, 1)
    index = 8 * (lane % 16) + lane // 16
    return turn_blocks([jnp.take_along_axis(tile, index, axis=1) for tile in tiles])


def from_classes(tiles):
    lane = lax.broadcasted_iota(jnp.int32, tiles[0].shape, 1)
    index = 16 * (lane % 8) + lane // 8
    return [jnp.take_along_axis(tile, index, axis=1) for tile in turn_blocks(tiles)]


def inverse_factor(aug):
    rows = [aug[8 * i:8 * i + 8] for i in range(8)]
    sub = lax.broadcasted_iota(jnp.int32, (8, 128), 0)
    done = []

    def spread(value, k):
        return jnp.broadcast_to(value[k:k + 1], (8, 128))

    for p in range(8):
        columns = {
            (j, i): jnp.broadcast_to(rows[i][:, 8 * p + j:8 * p + j + 1], (8, 128))
            for i in range(p, 8) for j in range(8)
        }
        pivots = spread(columns[0, p], 0)
        for k in range(8):
            pivot = spread(columns[k, p], k)
            pivots = jnp.where(sub == k, pivot, pivots)
            inverse = 1.0 / pivot
            row = spread(rows[p], k)
            heads = {j: spread(columns[j, p], k) for j in range(k + 1, 8)}
            for i in range(p, 8):
                factor = columns[k, i] * inverse
                if i == p:
                    factor = jnp.where(sub > k, factor, 0.0)
                rows[i] = rows[i] - factor * row
                for j in range(k + 1, 8):
                    columns[j, i] = columns[j, i] - factor * heads[j]
        done.append(pltpu.roll(rows[p], 64, 1) * lax.rsqrt(pivots))
    return jnp.concatenate(done, axis=0)[:, 0:64]


def kernel(
    bounds_ref, x_hbm, pot_hbm, fields, ritz_ref,
    x_ref, pot_ref, coef, start, even, odd, filt, filtered, diag_rows, diag, pot_own, slab, halos, ops_y, ops_z, apply_ops,
    parts, scattered, summed, total, ortho,
    in_sem, pot_send, pot_recv, ghost_send, ghost_recv, vec_send, vec_recv, halo_send, halo_recv, small_send, small_recv,
    back_send, back_recv,
):
    s = lax.axis_index("strip")
    v = lax.axis_index("vec")
    y_lo = s // 2 % 2

    barrier = pltpu.get_barrier_semaphore()

    def greet(j, carry):
        for where in ({"vec": lax.rem(v + j, NV)}, {"strip": lax.rem(s + j, NS)}):
            pl.semaphore_signal(barrier, inc=1, device_id=where, device_id_type=pl.DeviceIdType.MESH)
        return carry

    pot_in = pltpu.make_async_copy(pot_hbm, pot_ref, in_sem.at[0])
    x_in = pltpu.make_async_copy(x_hbm, x_ref, in_sem.at[1])
    pot_in.start()
    x_in.start()
    lax.fori_loop(1, NV, greet, 0)

    def splat(i):
        return jnp.full((8, 128), bounds_ref[i], jnp.int32).astype(F32) * grid_unit

    edges = [splat(i) for i in range(4)]
    center = (edges[0] + edges[1]) * 0.5
    spread = (edges[1] - edges[0]) * 0.5
    scale = 2.0 / spread

    pot_in.wait()
    for r in range(ROWS // 8):
        tiles = []
        for t in range(SUB):
            level = pot_ref[8 * r:8 * r + 8, 128 * t:128 * t + 128].astype(F32)
            tiles.append(disorder * (level / (POT_LEVELS - 1) - 0.5))
        for c, field in enumerate(to_classes(tiles)):
            pot_own[pl.ds(64 * r + place(c), 8, stride=8), :] = field
            diag_rows[pl.ds(OWN + 64 * r + place(c), 8, stride=8), :] = (field - center) * scale

    x_in.wait()

    def classes_of(q, carry):
        for r in range(ROWS // 8):
            tiles = [0.5 * x_ref[q, 8 * r:8 * r + 8, 128 * t:128 * t + 128] for t in range(SUB)]
            for c, tile in enumerate(to_classes(tiles)):
                start[q, pl.ds(OWN + 64 * r + place(c), 8, stride=8), :] = tile
        return carry

    classes_of(0, 0)

    pl.semaphore_wait(barrier, NV + NS - 2)

    up = lax.rem(s + NS - 1, NS)
    down = lax.rem(s + 1, NS)
    up2 = lax.rem(s + NS - 2, NS)

    def pot_copies():
        mine = diag_rows.at[pl.ds(OWN, OWN)]
        return (
            remote(mine, diag_rows.at[pl.ds(2 * OWN, OWN)], pot_send.at[0], pot_recv.at[0], strip=up),
            remote(mine, diag_rows.at[pl.ds(0, OWN)], pot_send.at[1], pot_recv.at[1], strip=down),
        )

    def ghost_copies(q):
        mine = start.at[q, pl.ds(OWN, OWN)]
        return (
            remote(mine, start.at[q, pl.ds(2 * OWN, OWN)], ghost_send.at[q, 0], ghost_recv.at[q, 0], strip=up),
            remote(mine, start.at[q, pl.ds(0, OWN)], ghost_send.at[q, 1], ghost_recv.at[q, 1], strip=down),
            remote(
                start.at[q, pl.ds(OWN, SUB)], start.at[q, pl.ds(3 * OWN, SUB)],
                ghost_send.at[q, 2], ghost_recv.at[q, 2], strip=up2,
            ),
        )

    def start_ghosts(q):
        for copy in ghost_copies(q):
            copy.start()

    for copy in pot_copies():
        copy.start()
    start_ghosts(0)
    lax.fori_loop(1, NQ, classes_of, 0)

    theta_lo = arccos((edges[2] - center) / spread)
    theta_hi = arccos((edges[3] - center) / spread)
    coef[0:8] = (theta_lo - theta_hi) / math.pi

    def coefficient(k, carry):
        order = jnp.full((8, 128), k, jnp.int32).astype(F32)
        coef[pl.ds(pl.multiple_of(8 * k, 8), 8)] = (
            2.0 * (jnp.sin(order * theta_lo) - jnp.sin(order * theta_hi)) / (order * math.pi)
        )
        return carry

    lax.fori_loop(1, DEGREE + 1, coefficient, 0)

    def pair_place(row):
        return (16 * row, 0) if row <= 48 else (16 * (96 - row), 1)

    for copy in pot_copies() + ghost_copies(0):
        copy.wait_send()
    start_ghosts(1)

    for copy in pot_copies():
        copy.wait_recv()
    for row in range(1, 3 * ROWS):
        value = diag_rows[8 * row:8 * row + 8]
        for base, half in {pair_place(row), (16 * (96 - row), 1) if row == 48 else pair_place(row)}:
            diag[pl.ds(base + half, 8, stride=2), :] = value

    sub = lax.broadcasted_iota(jnp.int32, (8, 128), 0)
    lane = lax.broadcasted_iota(jnp.int32, (8, 128), 1)
    index_left = jnp.where(sub >= 6, (lane + 127) % 128, lane)
    index_right = jnp.where(sub < 2, (lane + 1) % 128, lane)
    upper = (sub % 2 == 0)[None, None]

    def shift(value, index, by):
        index = jnp.broadcast_to(index[None], value.shape)
        return pltpu.roll(jnp.take_along_axis(value, index, axis=2), by, 1)

    def update(k, low, high):
        now, then = (even, odd) if k % 2 else (odd, even)
        rows = high - low
        top = min(high + 1, PAIRS)
        ext = now[(low - 1) * 16:top * 16].reshape(top - low + 1, 2, 8, 128)
        above = ext[0:rows]
        mid = ext[1:rows + 1]
        if high == PAIRS:
            crossing = ext[rows - 1:rows]
            crossing = jnp.where(upper, pltpu.roll(crossing, 7, 2), pltpu.roll(crossing, 1, 2))
            below = jnp.concatenate([ext[2:rows + 1], crossing], axis=0)
        else:
            below = ext[2:rows + 2]
        left = shift(mid[:, 1], index_left, 2)
        right = shift(mid[:, 0], index_right, 6)
        before = then[low * 16:high * 16].reshape(rows, 2, 8, 128) if k > 1 else None
        local = diag[low * 16:high * 16].reshape(rows, 2, 8, 128)
        halves = []
        for j, beside in enumerate((left + mid[:, 1], mid[:, 0] + right)):
            inside = local[:, j] * mid[:, j]
            if k == 2:
                inside = inside - (before[:, j] + before[:, j])
            elif k > 2:
                inside = inside - before[:, j]
            halves.append(inside - scale * ((above[:, j] + below[:, j]) + beside))
        after = jnp.stack(halves, axis=1)
        then[low * 16:high * 16] = after.reshape(rows * 16, 128)
        if k % 2 == 0 and high == PAIRS:
            first = max(ROWS, low)
            c_now = coef[8 * k - 8:8 * k]
            c_next = coef[8 * k:8 * k + 8]
            term = c_now * mid[first - low:] + c_next * after[first - low:]
            place_in = slice((first - ROWS) * 16, (PAIRS - ROWS) * 16)
            filt[place_in] = filt[place_in] + term.reshape((PAIRS - first) * 16, 128)

    def vec_copy(q, j):
        peer = lax.rem(v + j, NV)
        return remote(
            filtered.at[q, pl.ds(peer * CHUNKS, CHUNKS)], slab.at[pl.ds((v * NQ + q) * CHUNKS, CHUNKS)],
            vec_send.at[q], vec_recv.at[q], vec=peer,
        )

    def one_vector(q, carry):
        for copy in ghost_copies(q):
            copy.wait_recv()
        for row in range(3 * ROWS + 1):
            value = start[q, 8 * row:8 * row + 8]
            base, half = pair_place(row)
            even[pl.ds(base + half, 8, stride=2), :] = value
            if row == 48:
                even[pl.ds(base + 1, 8, stride=2), :] = value
        filt[...] = (
            (2.0 * coef[0:8]) * even[16 * ROWS:16 * PAIRS].reshape(2 * (PAIRS - ROWS), 8, 128)
        ).reshape(16 * (PAIRS - ROWS), 128)
        for k in range(1, DEGREE + 1):
            if k < ROWS - 1:
                update(k, k, ROWS)
                update(k, ROWS, PAIRS)
            else:
                update(k, k, PAIRS)
            if k == DEGREE // 2:
                @pl.when(q < NQ - 2)
                def _():
                    for copy in ghost_copies(q + 1):
                        copy.wait_send()
                    start_ghosts(q + 2)

        for row in range(ROWS + 1):
            base, half = pair_place(ROWS + row)
            filtered[q, 8 * row:8 * row + 8] = filt[pl.ds(base - 16 * ROWS + half, 8, stride=2), :]
        slab[pl.ds((v * NQ + q) * CHUNKS, CHUNKS)] = filtered[q, pl.ds(v * CHUNKS, CHUNKS)]

        def send(j, inner):
            vec_copy(q, j).start()
            return inner

        lax.fori_loop(1, NV, send, 0)
        return carry

    lax.fori_loop(0, NQ, one_vector, 0)

    wait_bytes(slab.at[pl.ds(0, (NV - 1) * CHUNKS)], vec_send.at[NQ - 1])

    def send_halos(j, carry):
        peer = lax.rem(v + j, NV)
        remote(
            filtered.at[:, pl.ds(peer * CHUNKS + CHUNKS, SUB)], halos.at[pl.ds(v * NQ, NQ)],
            halo_send.at[0], halo_recv.at[0], vec=peer,
        ).start()
        return carry

    lax.fori_loop(1, NV, send_halos, 0)
    halos[pl.ds(v * NQ, NQ)] = filtered[:, pl.ds(v * CHUNKS + CHUNKS, SUB)]
    for q in range(NQ):
        wait_bytes(slab.at[pl.ds(0, (NV - 1) * CHUNKS)], vec_recv.at[q])

    def take(source, stride, g, n):
        base = 16 * g * stride + n
        return jnp.concatenate(
            [source[pl.ds(base, 8, stride=stride), :], source[pl.ds(base + 8 * stride, 8, stride=stride), :]], axis=0
        )

    def keep(target, g, n, value):
        for part, half in enumerate(split(value)):
            target[64 * part + 16 * g:64 * part + 16 * g + 16, 128 * n:128 * n + 128] = half

    def matrix_part(left):
        prod = lax.dot_general(left[...], ops_y[...], (((1,), (1,)), ((), ())), preferred_element_type=F32)
        return prod[0:64] + prod[64:128]

    def along_strip(stage, i, source, target):
        for a, b, c in STRIP_STEPS:
            peer = lax.rem(s // 4 + a, 4) * 4 + lax.rem(y_lo + b, 2) * 2 + lax.rem(s % 2 + c, 2)
            remote(source(peer), target, small_send.at[i, stage], small_recv.at[i, stage], strip=peer).start()

    def scatter(i, value):
        for c in range(NS):
            parts[i, c] = value[PART * c:PART * c + PART]
        scattered[i, s] = parts[i, s]
        along_strip(0, i, lambda peer: parts.at[i, peer], scattered.at[i, s])

    def exchange(i):
        wait_bytes(scattered.at[i, pl.ds(0, NS - 1)], small_recv.at[i, 0])
        summed[i, v] = jnp.sum(scattered[i], axis=0)
        for a, b in VEC_STEPS:
            peer = lax.rem(v // 8 + a, 2) * 8 + lax.rem(v % 8 + b, 8)
            remote(
                summed.at[i, v], summed.at[i, v], small_send.at[i, 1], small_recv.at[i, 1], vec=peer
            ).start()

    def gather(i):
        wait_bytes(summed.at[i, pl.ds(0, NV - 1)], small_recv.at[i, 1])
        total[i, s] = jnp.sum(summed[i], axis=0)
        along_strip(2, i, lambda peer: total.at[i, s], total.at[i, s])

    def finish(i):
        wait_bytes(total.at[i, pl.ds(0, NS - 1)], small_recv.at[i, 2])
        value = jnp.concatenate([total[i, c] for c in range(NS)], axis=0)
        return value + pltpu.roll(value, 64, 1)

    for g in range(NVEC // 16):
        for n in range(CHUNKS):
            keep(ops_y, g, n, take(slab, CHUNKS, g, n))
    scatter(0, matrix_part(ops_y))

    for g in range(NVEC // 16):
        for row in range(PIECE):
            tiles = from_classes([take(slab, CHUNKS, g, SUB * row + place(c)) for c in range(SUB)])
            for t, tile in enumerate(tiles):
                keep(apply_ops, g, SUB * row + t, tile)
    exchange(0)

    wait_bytes(halos.at[pl.ds(0, (NV - 1) * NQ)], halo_recv.at[0])
    pot_slab = pot_own[pl.ds(v * CHUNKS, CHUNKS)] * 0.5
    for g in range(NVEC // 16):
        y = [take(slab, CHUNKS, g, n) for n in range(CHUNKS)]
        y += [take(halos.reshape(NVEC * SUB, 128), SUB, g, n) for n in range(SUB)]
        for row in range(PIECE):
            for c in range(SUB):
                n = SUB * row + place(c)
                if c < SUB - 1:
                    right = y[SUB * row + place(c + 1)]
                else:
                    right = pltpu.roll(y[SUB * row + place(0)], 127, 1)
                keep(ops_z, g, n, pot_slab[n:n + 1] * y[n] - (right + y[n + SUB]))
    scatter(1, matrix_part(ops_z))
    gather(0)
    exchange(1)

    rows64 = lax.broadcasted_iota(jnp.int32, (64, 128), 0)
    lanes64 = lax.broadcasted_iota(jnp.int32, (64, 128), 1)
    gram = finish(0)
    inverse = inverse_factor(jnp.where(lanes64 < 64, gram, jnp.where(lanes64 - 64 == rows64, 1.0, 0.0)))

    high, low = split(math.sqrt(SITES) * inverse)
    left = jnp.concatenate(
        [jnp.concatenate([high, high], axis=1), jnp.concatenate([low, low], axis=1)], axis=0
    )
    product = jnp.dot(left, apply_ops[...], preferred_element_type=F32)
    flat = ortho.reshape(NVEC * CHUNKS, 128)
    for n in range(CHUNKS):
        value = product[0:64, 128 * n:128 * n + 128] + product[64:128, 128 * n:128 * n + 128]
        for g in range(8):
            flat[pl.ds(n + 8 * g * CHUNKS, 8, stride=CHUNKS), :] = value[8 * g:8 * g + 8]

    def send_back(j, carry):
        peer = lax.rem(v + j, NV)
        remote(
            ortho.at[pl.ds(peer * NQ, NQ)], fields.at[:, pl.ds(v * CHUNKS, CHUNKS)],
            back_send.at[0], back_recv.at[0], vec=peer,
        ).start()
        return carry

    lax.fori_loop(1, NV, send_back, 0)
    fields[:, pl.ds(v * CHUNKS, CHUNKS)] = ortho[pl.ds(v * NQ, NQ)]

    gather(1)
    cross = finish(1)[:, 0:64]
    cross = cross + cross.T
    half = jnp.dot(inverse, cross, precision=lax.Precision.HIGHEST, preferred_element_type=F32)
    ritz_ref[...] = float(ROWS) * lax.dot_general(
        inverse, half, (((1,), (1,)), ((), ())), precision=lax.Precision.HIGHEST, preferred_element_type=F32
    )

    wait_bytes(ortho.at[pl.ds(0, (NV - 1) * NQ)], back_recv.at[0])
    wait_bytes(ortho.at[pl.ds(0, (NV - 1) * NQ)], back_send.at[0])
    for i in range(2):
        for stage in range(3):
            wait_bytes(total.at[i, pl.ds(0, NS - 1)], small_send.at[i, stage])
    wait_bytes(halos.at[pl.ds(0, (NV - 1) * NQ)], halo_send.at[0])
    for q in range(NQ - 1):
        wait_bytes(slab.at[pl.ds(0, (NV - 1) * CHUNKS)], vec_send.at[q])
    for copy in ghost_copies(NQ - 1):
        copy.wait_send()


def arrange(fields, ritz, out_ref, ritz_ref):
    for q in range(NQ):
        for r in range(ROWS // 8):
            for t in range(SUB):
                out_ref[q, 8 * r:8 * r + 8, 128 * t:128 * t + 128] = fields[q, pl.ds(64 * r + t, 8, stride=8), :]
    ritz_ref[...] = ritz[...]


def shards(start_vectors, potential, bounds):
    vmem = pl.BlockSpec(memory_space=pltpu.VMEM)
    hbm = pl.BlockSpec(memory_space=pltpu.HBM)
    dma = pltpu.SemaphoreType.DMA
    ritz_shape = jax.ShapeDtypeStruct((NVEC, NVEC), F32)
    fields, ritz = pl.pallas_call(
        kernel,
        out_shape=(pltpu.VMEM((NQ, OWN, 128), F32), pltpu.VMEM((NVEC, NVEC), F32)),
        in_specs=[pl.BlockSpec(memory_space=pltpu.SMEM), hbm, hbm],
        out_specs=(vmem, vmem),
        scratch_shapes=[
            pltpu.VMEM((NQ, ROWS, 1024), F32),
            pltpu.VMEM((ROWS, 1024), jnp.int32),
            pltpu.VMEM((8 * (DEGREE + 1), 128), F32),
            pltpu.VMEM((NQ, FIELD, 128), F32),
            pltpu.VMEM((16 * PAIRS, 128), F32),
            pltpu.VMEM((16 * PAIRS, 128), F32),
            pltpu.VMEM((16 * (PAIRS - ROWS), 128), F32),
            pltpu.VMEM((NQ, OWN + SUB, 128), F32),
            pltpu.VMEM((FIELD, 128), F32),
            pltpu.VMEM((16 * PAIRS, 128), F32),
            pltpu.VMEM((OWN, 128), F32),
            pltpu.VMEM((NVEC * CHUNKS, 128), F32),
            pltpu.VMEM((NVEC, SUB, 128), F32),
            pltpu.VMEM((128, CHUNKS * 128), BF16),
            pltpu.VMEM((128, CHUNKS * 128), BF16),
            pltpu.VMEM((128, CHUNKS * 128), BF16),
            pltpu.VMEM((2, NS, PART, 128), F32),
            pltpu.VMEM((2, NS, PART, 128), F32),
            pltpu.VMEM((2, NV, PART, 128), F32),
            pltpu.VMEM((2, NS, PART, 128), F32),
            pltpu.VMEM((NVEC, CHUNKS, 128), F32),
            dma((2,)), dma((2,)), dma((2,)), dma((NQ, 3)), dma((NQ, 3)), dma((NQ,)), dma((NQ,)), dma((1,)), dma((1,)),
            dma((2, 3)), dma((2, 3)), dma((1,)), dma((1,)),
        ],
        compiler_params=pltpu.CompilerParams(
            collective_id=0, has_side_effects=True, vmem_limit_bytes=60 << 20
        ),
        name="filter_ritz",
    )(bounds, start_vectors, potential)
    return pl.pallas_call(
        arrange,
        out_shape=(jax.ShapeDtypeStruct((NQ, ROWS, 1024), F32), ritz_shape),
        in_specs=[vmem, vmem],
        out_specs=(vmem, vmem),
        name="arrange",
    )(pltpu.with_memory_space_constraint(fields, pltpu.VMEM), pltpu.with_memory_space_constraint(ritz, pltpu.VMEM))


def solution(mesh):
    in_specs = (P("vec", "strip", None), P("strip", None), P())
    out_specs = (P("vec", "strip", None), P())
    return jax.shard_map(shards, mesh=mesh, in_specs=in_specs, out_specs=out_specs, check_vma=False)
```

```python
import math

import jax
import jax.numpy as jnp
from jax import lax
from jax.experimental import pallas as pl
from jax.experimental.pallas import tpu as pltpu
from jax.sharding import PartitionSpec as P

DEGREE = 32
POT_LEVELS = 16
NQ = 4
ROWS = 32
NV = 16
NS = 16
NVEC = NQ * NV
PIECE = ROWS // NV
SUB = 8
CHUNKS = PIECE * SUB
HALO = CHUNKS + SUB
LAST = NQ - 1
FIELD = (3 * ROWS + 1) * SUB
PAIRS = 3 * ROWS // 2 + 1
STRIP_STEPS = sorted(
    ((a, b, c) for a in range(4) for b in range(2) for c in range(2) if a or b or c),
    key=lambda step: -(2 * min(step[0], 4 - step[0]) + 2 * step[1] + step[2]),
)
VEC_STEPS = sorted(
    ((a, b) for a in range(2) for b in range(8) if a or b), key=lambda step: -(2 * step[0] + min(step[1], 8 - step[1]))
)
PART = NVEC // NS
OWN = ROWS * SUB
HALF_PI = math.pi / 2
SITES = NS * ROWS * 1024

grid_unit = 0.0625
disorder = 2.0
F32 = jnp.float32
BF16 = jnp.bfloat16


def remote(src, dst, send, recv, **where):
    return pltpu.make_async_remote_copy(
        src_ref=src, dst_ref=dst, send_sem=send, recv_sem=recv,
        device_id=where, device_id_type=pl.DeviceIdType.MESH,
    )


def wait_bytes(ref, sem):
    pltpu.make_async_copy(ref, ref, sem).wait()


def split(value):
    high = value.astype(BF16)
    return high, (value - high.astype(F32)).astype(BF16)


def arccos(x):
    size = jnp.abs(x)
    large = size > 0.5
    square = jnp.where(large, 0.5 * (1.0 - size), x * x)
    base = jnp.where(large, jnp.sqrt(square), size)
    poly = 4.2163199048e-2 * square + 2.4181311049e-2
    poly = poly * square + 4.5470025998e-2
    poly = poly * square + 7.4953002686e-2
    poly = poly * square + 1.6666752422e-1
    arcsin = base + base * square * poly
    positive = jnp.where(large, 2.0 * arcsin, HALF_PI - arcsin)
    return jnp.where(x < 0.0, math.pi - positive, positive)


def place(s):
    return 4 * (s % 2) + s // 2


def turn_blocks(tiles):
    tiles = list(tiles)
    block = lax.broadcasted_iota(jnp.int32, tiles[0].shape, 1) // 16
    for bit in (1, 2, 4):
        clear = (block & bit) == 0
        for i in range(8):
            if i & bit == 0:
                one, two = tiles[i], tiles[i + bit]
                tiles[i] = jnp.where(clear, one, pltpu.roll(two, 16 * bit, 1))
                tiles[i + bit] = jnp.where(clear, pltpu.roll(one, 128 - 16 * bit, 1), two)
    return tiles


def to_classes(tiles):
    lane = lax.broadcasted_iota(jnp.int32, tiles[0].shape, 1)
    index = 8 * (lane % 16) + lane // 16
    return turn_blocks([jnp.take_along_axis(tile, index, axis=1) for tile in tiles])


def from_classes(tiles):
    lane = lax.broadcasted_iota(jnp.int32, tiles[0].shape, 1)
    index = 16 * (lane % 8) + lane // 8
    return [jnp.take_along_axis(tile, index, axis=1) for tile in turn_blocks(tiles)]


def inverse_factor(aug):
    rows = [aug[8 * i:8 * i + 8] for i in range(8)]
    sub = lax.broadcasted_iota(jnp.int32, (8, 128), 0)
    done = []

    def spread(value, k):
        return jnp.broadcast_to(value[k:k + 1], (8, 128))

    for p in range(8):
        columns = {
            (j, i): jnp.broadcast_to(rows[i][:, 8 * p + j:8 * p + j + 1], (8, 128))
            for i in range(p, 8) for j in range(8)
        }
        pivots = spread(columns[0, p], 0)
        for k in range(8):
            pivot = spread(columns[k, p], k)
            pivots = jnp.where(sub == k, pivot, pivots)
            inverse = 1.0 / pivot
            row = spread(rows[p], k)
            heads = {j: spread(columns[j, p], k) for j in range(k + 1, 8)}
            for i in range(p, 8):
                factor = columns[k, i] * inverse
                if i == p:
                    factor = jnp.where(sub > k, factor, 0.0)
                rows[i] = rows[i] - factor * row
                for j in range(k + 1, 8):
                    columns[j, i] = columns[j, i] - factor * heads[j]
        done.append(pltpu.roll(rows[p], 64, 1) * lax.rsqrt(pivots))
    return jnp.concatenate(done, axis=0)[:, 0:64]


def kernel(
    bounds_ref, x_hbm, pot_hbm, fields, ritz_ref,
    x_ref, pot_ref, coef, start, even, odd, filt, filtered, diag_rows, diag, pot_own, slab, halos, ops_y, ops_z, apply_ops,
    parts, scattered, summed, total, ortho,
    in_sem, pot_send, pot_recv, ghost_send, ghost_recv, vec_send, vec_recv, halo_send, halo_recv, small_send, small_recv,
    back_send, back_recv,
):
    s = lax.axis_index("strip")
    v = lax.axis_index("vec")
    y_lo = s // 2 % 2

    barrier = pltpu.get_barrier_semaphore()

    def greet(j, carry):
        for where in ({"vec": lax.rem(v + j, NV)}, {"strip": lax.rem(s + j, NS)}):
            pl.semaphore_signal(barrier, inc=1, device_id=where, device_id_type=pl.DeviceIdType.MESH)
        return carry

    pot_in = pltpu.make_async_copy(pot_hbm, pot_ref, in_sem.at[0])
    x_in = pltpu.make_async_copy(x_hbm, x_ref, in_sem.at[1])
    pot_in.start()
    x_in.start()
    lax.fori_loop(1, NV, greet, 0)

    def splat(i):
        return jnp.full((8, 128), bounds_ref[i], jnp.int32).astype(F32) * grid_unit

    edges = [splat(i) for i in range(4)]
    center = (edges[0] + edges[1]) * 0.5
    spread = (edges[1] - edges[0]) * 0.5
    scale = 2.0 / spread

    pot_in.wait()
    for r in range(ROWS // 8):
        tiles = []
        for t in range(SUB):
            level = pot_ref[8 * r:8 * r + 8, 128 * t:128 * t + 128].astype(F32)
            tiles.append(disorder * (level / (POT_LEVELS - 1) - 0.5))
        for c, field in enumerate(to_classes(tiles)):
            pot_own[pl.ds(64 * r + place(c), 8, stride=8), :] = field
            diag_rows[pl.ds(OWN + 64 * r + place(c), 8, stride=8), :] = (field - center) * scale

    x_in.wait()

    def classes_of(q, carry):
        for r in range(ROWS // 8):
            tiles = [0.5 * x_ref[q, 8 * r:8 * r + 8, 128 * t:128 * t + 128] for t in range(SUB)]
            for c, tile in enumerate(to_classes(tiles)):
                start[q, pl.ds(OWN + 64 * r + place(c), 8, stride=8), :] = tile
        return carry

    classes_of(0, 0)

    pl.semaphore_wait(barrier, NV + NS - 2)

    up = lax.rem(s + NS - 1, NS)
    down = lax.rem(s + 1, NS)
    up2 = lax.rem(s + NS - 2, NS)

    def pot_copies():
        mine = diag_rows.at[pl.ds(OWN, OWN)]
        return (
            remote(mine, diag_rows.at[pl.ds(2 * OWN, OWN)], pot_send.at[0], pot_recv.at[0], strip=up),
            remote(mine, diag_rows.at[pl.ds(0, OWN)], pot_send.at[1], pot_recv.at[1], strip=down),
        )

    def ghost_copies(q):
        mine = start.at[q, pl.ds(OWN, OWN)]
        return (
            remote(mine, start.at[q, pl.ds(2 * OWN, OWN)], ghost_send.at[q, 0], ghost_recv.at[q, 0], strip=up),
            remote(mine, start.at[q, pl.ds(0, OWN)], ghost_send.at[q, 1], ghost_recv.at[q, 1], strip=down),
            remote(
                start.at[q, pl.ds(OWN, SUB)], start.at[q, pl.ds(3 * OWN, SUB)],
                ghost_send.at[q, 2], ghost_recv.at[q, 2], strip=up2,
            ),
        )

    def start_ghosts(q):
        for copy in ghost_copies(q):
            copy.start()

    for copy in pot_copies():
        copy.start()
    start_ghosts(0)
    lax.fori_loop(1, NQ, classes_of, 0)

    theta_lo = arccos((edges[2] - center) / spread)
    theta_hi = arccos((edges[3] - center) / spread)
    coef[0:8] = (theta_lo - theta_hi) / math.pi

    def coefficient(k, carry):
        order = jnp.full((8, 128), k, jnp.int32).astype(F32)
        coef[pl.ds(pl.multiple_of(8 * k, 8), 8)] = (
            2.0 * (jnp.sin(order * theta_lo) - jnp.sin(order * theta_hi)) / (order * math.pi)
        )
        return carry

    lax.fori_loop(1, DEGREE + 1, coefficient, 0)

    def pair_place(row):
        return (16 * row, 0) if row <= 48 else (16 * (96 - row), 1)

    for copy in pot_copies() + ghost_copies(0):
        copy.wait_send()
    start_ghosts(1)

    for copy in pot_copies():
        copy.wait_recv()
    for row in range(1, 3 * ROWS):
        value = diag_rows[8 * row:8 * row + 8]
        for base, half in {pair_place(row), (16 * (96 - row), 1) if row == 48 else pair_place(row)}:
            diag[pl.ds(base + half, 8, stride=2), :] = value

    sub = lax.broadcasted_iota(jnp.int32, (8, 128), 0)
    lane = lax.broadcasted_iota(jnp.int32, (8, 128), 1)
    index_left = jnp.where(sub >= 6, (lane + 127) % 128, lane)
    index_right = jnp.where(sub < 2, (lane + 1) % 128, lane)
    upper = (sub % 2 == 0)[None, None]

    def shift(value, index, by):
        index = jnp.broadcast_to(index[None], value.shape)
        return pltpu.roll(jnp.take_along_axis(value, index, axis=2), by, 1)

    def update(k, low, high):
        now, then = (even, odd) if k % 2 else (odd, even)
        rows = high - low
        top = min(high + 1, PAIRS)
        ext = now[(low - 1) * 16:top * 16].reshape(top - low + 1, 2, 8, 128)
        above = ext[0:rows]
        mid = ext[1:rows + 1]
        if high == PAIRS:
            crossing = ext[rows - 1:rows]
            crossing = jnp.where(upper, pltpu.roll(crossing, 7, 2), pltpu.roll(crossing, 1, 2))
            below = jnp.concatenate([ext[2:rows + 1], crossing], axis=0)
        else:
            below = ext[2:rows + 2]
        left = shift(mid[:, 1], index_left, 2)
        right = shift(mid[:, 0], index_right, 6)
        before = then[low * 16:high * 16].reshape(rows, 2, 8, 128) if k > 1 else None
        local = diag[low * 16:high * 16].reshape(rows, 2, 8, 128)
        halves = []
        for j, beside in enumerate((left + mid[:, 1], mid[:, 0] + right)):
            inside = local[:, j] * mid[:, j]
            if k == 2:
                inside = inside - (before[:, j] + before[:, j])
            elif k > 2:
                inside = inside - before[:, j]
            halves.append(inside - scale * ((above[:, j] + below[:, j]) + beside))
        after = jnp.stack(halves, axis=1)
        then[low * 16:high * 16] = after.reshape(rows * 16, 128)
        if k % 2 == 0 and high == PAIRS:
            first = max(ROWS, low)
            c_now = coef[8 * k - 8:8 * k]
            c_next = coef[8 * k:8 * k + 8]
            term = c_now * mid[first - low:] + c_next * after[first - low:]
            place_in = slice((first - ROWS) * 16, (PAIRS - ROWS) * 16)
            filt[place_in] = filt[place_in] + term.reshape((PAIRS - first) * 16, 128)

    def send_vector(q, count):
        def send(j, carry):
            peer = lax.rem(v + j, NV)
            remote(
                filtered.at[q, pl.ds(peer * CHUNKS, count)], slab.at[pl.ds((v * NQ + q) * HALO, count)],
                vec_send.at[q], vec_recv.at[q], vec=peer,
            ).start()
            return carry

        lax.fori_loop(1, NV, send, 0)

    def one_vector(q, carry):
        for copy in ghost_copies(q):
            copy.wait_recv()
        for row in range(3 * ROWS + 1):
            value = start[q, 8 * row:8 * row + 8]
            base, half = pair_place(row)
            even[pl.ds(base + half, 8, stride=2), :] = value
            if row == 48:
                even[pl.ds(base + 1, 8, stride=2), :] = value
        filt[...] = (
            (2.0 * coef[0:8]) * even[16 * ROWS:16 * PAIRS].reshape(2 * (PAIRS - ROWS), 8, 128)
        ).reshape(16 * (PAIRS - ROWS), 128)
        for k in range(1, DEGREE + 1):
            if k < ROWS - 1:
                update(k, k, ROWS)
                update(k, ROWS, PAIRS)
            else:
                update(k, k, PAIRS)
            if k == DEGREE // 2:
                @pl.when(q < NQ - 2)
                def _():
                    for copy in ghost_copies(q + 1):
                        copy.wait_send()
                    start_ghosts(q + 2)

        for row in range(ROWS + 1):
            base, half = pair_place(ROWS + row)
            filtered[q, 8 * row:8 * row + 8] = filt[pl.ds(base - 16 * ROWS + half, 8, stride=2), :]
        slab[pl.ds((v * NQ + q) * HALO, HALO)] = filtered[q, pl.ds(v * CHUNKS, HALO)]

        @pl.when(q < LAST)
        def _():
            send_vector(q, HALO)

        @pl.when(q == LAST)
        def _():
            send_vector(q, CHUNKS)

        return carry

    lax.fori_loop(0, NQ, one_vector, 0)
    for q in range(NQ):
        wait_bytes(slab.at[pl.ds(0, (NV - 1) * (CHUNKS if q == LAST else HALO))], vec_recv.at[q])

    def take(source, stride, g, n):
        base = 16 * g * stride + n
        return jnp.concatenate(
            [source[pl.ds(base, 8, stride=stride), :], source[pl.ds(base + 8 * stride, 8, stride=stride), :]], axis=0
        )

    def keep(target, g, n, value):
        for part, half in enumerate(split(value)):
            target[64 * part + 16 * g:64 * part + 16 * g + 16, 128 * n:128 * n + 128] = half

    def matrix_part(left):
        prod = lax.dot_general(left[...], ops_y[...], (((1,), (1,)), ((), ())), preferred_element_type=F32)
        return prod[0:64] + prod[64:128]

    def along_strip(stage, i, source, target):
        for a, b, c in STRIP_STEPS:
            peer = lax.rem(s // 4 + a, 4) * 4 + lax.rem(y_lo + b, 2) * 2 + lax.rem(s % 2 + c, 2)
            remote(source(peer), target, small_send.at[i, stage], small_recv.at[i, stage], strip=peer).start()

    def scatter(i, value):
        for c in range(NS):
            parts[i, c] = value[PART * c:PART * c + PART]
        scattered[i, s] = parts[i, s]
        along_strip(0, i, lambda peer: parts.at[i, peer], scattered.at[i, s])

    def exchange(i):
        wait_bytes(scattered.at[i, pl.ds(0, NS - 1)], small_recv.at[i, 0])
        summed[i, v] = jnp.sum(scattered[i], axis=0)
        for a, b in VEC_STEPS:
            peer = lax.rem(v // 8 + a, 2) * 8 + lax.rem(v % 8 + b, 8)
            remote(
                summed.at[i, v], summed.at[i, v], small_send.at[i, 1], small_recv.at[i, 1], vec=peer
            ).start()

    def gather(i):
        wait_bytes(summed.at[i, pl.ds(0, NV - 1)], small_recv.at[i, 1])
        total[i, s] = jnp.sum(summed[i], axis=0)
        along_strip(2, i, lambda peer: total.at[i, s], total.at[i, s])

    def finish(i):
        wait_bytes(total.at[i, pl.ds(0, NS - 1)], small_recv.at[i, 2])
        value = jnp.concatenate([total[i, c] for c in range(NS)], axis=0)
        return value + pltpu.roll(value, 64, 1)

    for g in range(NVEC // 16):
        for n in range(CHUNKS):
            keep(ops_y, g, n, take(slab, HALO, g, n))
    scatter(0, matrix_part(ops_y))

    def send_halos(j, carry):
        peer = lax.rem(v + j, NV)
        remote(
            filtered.at[LAST, pl.ds(peer * CHUNKS + CHUNKS, SUB)], halos.at[v], halo_send.at[0], halo_recv.at[0], vec=peer
        ).start()
        return carry

    lax.fori_loop(1, NV, send_halos, 0)
    halos[v] = filtered[LAST, pl.ds(v * CHUNKS + CHUNKS, SUB)]

    for g in range(NVEC // 16):
        for row in range(PIECE):
            tiles = from_classes([take(slab, HALO, g, SUB * row + place(c)) for c in range(SUB)])
            for t, tile in enumerate(tiles):
                keep(apply_ops, g, SUB * row + t, tile)
    exchange(0)

    wait_bytes(halos.at[pl.ds(0, NV - 1)], halo_recv.at[0])
    for peer in range(NV):
        base = (peer * NQ + LAST) * HALO + CHUNKS
        slab[base:base + SUB] = halos[peer]
    pot_slab = pot_own[pl.ds(v * CHUNKS, CHUNKS)] * 0.5
    for g in range(NVEC // 16):
        y = [take(slab, HALO, g, n) for n in range(HALO)]
        for row in range(PIECE):
            for c in range(SUB):
                n = SUB * row + place(c)
                if c < SUB - 1:
                    right = y[SUB * row + place(c + 1)]
                else:
                    right = pltpu.roll(y[SUB * row + place(0)], 127, 1)
                keep(ops_z, g, n, pot_slab[n:n + 1] * y[n] - (right + y[n + SUB]))
    scatter(1, matrix_part(ops_z))
    gather(0)
    exchange(1)

    rows64 = lax.broadcasted_iota(jnp.int32, (64, 128), 0)
    lanes64 = lax.broadcasted_iota(jnp.int32, (64, 128), 1)
    gram = finish(0)
    inverse = inverse_factor(jnp.where(lanes64 < 64, gram, jnp.where(lanes64 - 64 == rows64, 1.0, 0.0)))

    high, low = split(math.sqrt(SITES) * inverse)
    left = jnp.concatenate(
        [jnp.concatenate([high, high], axis=1), jnp.concatenate([low, low], axis=1)], axis=0
    )
    product = jnp.dot(left, apply_ops[...], preferred_element_type=F32)
    flat = ortho.reshape(NVEC * CHUNKS, 128)
    for n in range(CHUNKS):
        value = product[0:64, 128 * n:128 * n + 128] + product[64:128, 128 * n:128 * n + 128]
        for g in range(8):
            flat[pl.ds(n + 8 * g * CHUNKS, 8, stride=CHUNKS), :] = value[8 * g:8 * g + 8]

    def send_back(j, carry):
        peer = lax.rem(v + j, NV)
        remote(
            ortho.at[pl.ds(peer * NQ, NQ)], fields.at[:, pl.ds(v * CHUNKS, CHUNKS)],
            back_send.at[0], back_recv.at[0], vec=peer,
        ).start()
        return carry

    lax.fori_loop(1, NV, send_back, 0)
    fields[:, pl.ds(v * CHUNKS, CHUNKS)] = ortho[pl.ds(v * NQ, NQ)]

    gather(1)
    cross = finish(1)[:, 0:64]
    cross = cross + cross.T
    half = jnp.dot(inverse, cross, precision=lax.Precision.HIGHEST, preferred_element_type=F32)
    ritz_ref[...] = float(ROWS) * lax.dot_general(
        inverse, half, (((1,), (1,)), ((), ())), precision=lax.Precision.HIGHEST, preferred_element_type=F32
    )

    wait_bytes(ortho.at[pl.ds(0, (NV - 1) * NQ)], back_recv.at[0])
    wait_bytes(ortho.at[pl.ds(0, (NV - 1) * NQ)], back_send.at[0])
    for i in range(2):
        for stage in range(3):
            wait_bytes(total.at[i, pl.ds(0, NS - 1)], small_send.at[i, stage])
    wait_bytes(halos.at[pl.ds(0, NV - 1)], halo_send.at[0])
    for q in range(NQ):
        wait_bytes(slab.at[pl.ds(0, (NV - 1) * (CHUNKS if q == LAST else HALO))], vec_send.at[q])
    for copy in ghost_copies(NQ - 1):
        copy.wait_send()


def arrange(fields, ritz, out_ref, ritz_ref):
    for q in range(NQ):
        for r in range(ROWS // 8):
            for t in range(SUB):
                out_ref[q, 8 * r:8 * r + 8, 128 * t:128 * t + 128] = fields[q, pl.ds(64 * r + t, 8, stride=8), :]
    ritz_ref[...] = ritz[...]


def shards(start_vectors, potential, bounds):
    vmem = pl.BlockSpec(memory_space=pltpu.VMEM)
    hbm = pl.BlockSpec(memory_space=pltpu.HBM)
    dma = pltpu.SemaphoreType.DMA
    ritz_shape = jax.ShapeDtypeStruct((NVEC, NVEC), F32)
    fields, ritz = pl.pallas_call(
        kernel,
        out_shape=(pltpu.VMEM((NQ, OWN, 128), F32), pltpu.VMEM((NVEC, NVEC), F32)),
        in_specs=[pl.BlockSpec(memory_space=pltpu.SMEM), hbm, hbm],
        out_specs=(vmem, vmem),
        scratch_shapes=[
            pltpu.VMEM((NQ, ROWS, 1024), F32),
            pltpu.VMEM((ROWS, 1024), jnp.int32),
            pltpu.VMEM((8 * (DEGREE + 1), 128), F32),
            pltpu.VMEM((NQ, FIELD, 128), F32),
            pltpu.VMEM((16 * PAIRS, 128), F32),
            pltpu.VMEM((16 * PAIRS, 128), F32),
            pltpu.VMEM((16 * (PAIRS - ROWS), 128), F32),
            pltpu.VMEM((NQ, OWN + SUB, 128), F32),
            pltpu.VMEM((FIELD, 128), F32),
            pltpu.VMEM((16 * PAIRS, 128), F32),
            pltpu.VMEM((OWN, 128), F32),
            pltpu.VMEM((NVEC * HALO, 128), F32),
            pltpu.VMEM((NV, SUB, 128), F32),
            pltpu.VMEM((128, CHUNKS * 128), BF16),
            pltpu.VMEM((128, CHUNKS * 128), BF16),
            pltpu.VMEM((128, CHUNKS * 128), BF16),
            pltpu.VMEM((2, NS, PART, 128), F32),
            pltpu.VMEM((2, NS, PART, 128), F32),
            pltpu.VMEM((2, NV, PART, 128), F32),
            pltpu.VMEM((2, NS, PART, 128), F32),
            pltpu.VMEM((NVEC, CHUNKS, 128), F32),
            dma((2,)), dma((2,)), dma((2,)), dma((NQ, 3)), dma((NQ, 3)), dma((NQ,)), dma((NQ,)), dma((1,)), dma((1,)),
            dma((2, 3)), dma((2, 3)), dma((1,)), dma((1,)),
        ],
        compiler_params=pltpu.CompilerParams(
            collective_id=0, has_side_effects=True, vmem_limit_bytes=60 << 20
        ),
        name="filter_ritz",
    )(bounds, start_vectors, potential)
    return pl.pallas_call(
        arrange,
        out_shape=(jax.ShapeDtypeStruct((NQ, ROWS, 1024), F32), ritz_shape),
        in_specs=[vmem, vmem],
        out_specs=(vmem, vmem),
        name="arrange",
    )(pltpu.with_memory_space_constraint(fields, pltpu.VMEM), pltpu.with_memory_space_constraint(ritz, pltpu.VMEM))


def solution(mesh):
    in_specs = (P("vec", "strip", None), P("strip", None), P())
    out_specs = (P("vec", "strip", None), P())
    return jax.shard_map(shards, mesh=mesh, in_specs=in_specs, out_specs=out_specs, check_vma=False)
```

```python
import math

import jax
import jax.numpy as jnp
from jax import lax
from jax.experimental import pallas as pl
from jax.experimental.pallas import tpu as pltpu
from jax.sharding import PartitionSpec as P

DEGREE = 32
POT_LEVELS = 16
NQ = 4
ROWS = 32
NV = 16
NS = 16
NVEC = NQ * NV
PIECE = ROWS // NV
SUB = 8
CHUNKS = PIECE * SUB
HALO = CHUNKS + SUB
LAST = NQ - 1
FIELD = (3 * ROWS + 1) * SUB
PAIRS = 3 * ROWS // 2 + 1
STRIP_STEPS = sorted(
    ((a, b, c) for a in range(4) for b in range(2) for c in range(2) if a or b or c),
    key=lambda step: -(2 * min(step[0], 4 - step[0]) + 2 * step[1] + step[2]),
)
VEC_STEPS = sorted(
    ((a, b) for a in range(2) for b in range(8) if a or b), key=lambda step: -(2 * step[0] + min(step[1], 8 - step[1]))
)
PART = NVEC // NS
OWN = ROWS * SUB
HALF_PI = math.pi / 2
SITES = NS * ROWS * 1024

grid_unit = 0.0625
disorder = 2.0
F32 = jnp.float32
BF16 = jnp.bfloat16


def remote(src, dst, send, recv, **where):
    return pltpu.make_async_remote_copy(
        src_ref=src, dst_ref=dst, send_sem=send, recv_sem=recv,
        device_id=where, device_id_type=pl.DeviceIdType.MESH,
    )


def wait_bytes(ref, sem):
    pltpu.make_async_copy(ref, ref, sem).wait()


def split(value):
    high = value.astype(BF16)
    return high, (value - high.astype(F32)).astype(BF16)


def arccos(x):
    size = jnp.abs(x)
    large = size > 0.5
    square = jnp.where(large, 0.5 * (1.0 - size), x * x)
    base = jnp.where(large, jnp.sqrt(square), size)
    poly = 4.2163199048e-2 * square + 2.4181311049e-2
    poly = poly * square + 4.5470025998e-2
    poly = poly * square + 7.4953002686e-2
    poly = poly * square + 1.6666752422e-1
    arcsin = base + base * square * poly
    positive = jnp.where(large, 2.0 * arcsin, HALF_PI - arcsin)
    return jnp.where(x < 0.0, math.pi - positive, positive)


def place(s):
    return 4 * (s % 2) + s // 2


def turn_blocks(tiles):
    tiles = list(tiles)
    block = lax.broadcasted_iota(jnp.int32, tiles[0].shape, 1) // 16
    for bit in (1, 2, 4):
        clear = (block & bit) == 0
        for i in range(8):
            if i & bit == 0:
                one, two = tiles[i], tiles[i + bit]
                tiles[i] = jnp.where(clear, one, pltpu.roll(two, 16 * bit, 1))
                tiles[i + bit] = jnp.where(clear, pltpu.roll(one, 128 - 16 * bit, 1), two)
    return tiles


def to_classes(tiles):
    lane = lax.broadcasted_iota(jnp.int32, tiles[0].shape, 1)
    index = 8 * (lane % 16) + lane // 16
    return turn_blocks([jnp.take_along_axis(tile, index, axis=1) for tile in tiles])


def from_classes(tiles):
    lane = lax.broadcasted_iota(jnp.int32, tiles[0].shape, 1)
    index = 16 * (lane % 8) + lane // 8
    return [jnp.take_along_axis(tile, index, axis=1) for tile in turn_blocks(tiles)]


def eliminate(rows, panels):
    sub = lax.broadcasted_iota(jnp.int32, (8, 128), 0)
    done = []

    def spread(value, k):
        return jnp.broadcast_to(value[k:k + 1], (8, 128))

    for p in panels:
        columns = {
            (j, i): jnp.broadcast_to(rows[i][:, 8 * p + j:8 * p + j + 1], (8, 128))
            for i in range(p, 8) for j in range(8)
        }
        pivots = spread(columns[0, p], 0)
        for k in range(8):
            pivot = spread(columns[k, p], k)
            pivots = jnp.where(sub == k, pivot, pivots)
            inverse = 1.0 / pivot
            row = spread(rows[p], k)
            heads = {j: spread(columns[j, p], k) for j in range(k + 1, 8)}
            for i in range(p, 8):
                factor = columns[k, i] * inverse
                if i == p:
                    factor = jnp.where(sub > k, factor, 0.0)
                rows[i] = rows[i] - factor * row
                for j in range(k + 1, 8):
                    columns[j, i] = columns[j, i] - factor * heads[j]
        done.append(pltpu.roll(rows[p], 64, 1) * lax.rsqrt(pivots))
    return jnp.concatenate(done, axis=0)[:, 0:64]


def kernel(
    bounds_ref, x_hbm, pot_hbm, fields, ritz_ref,
    x_ref, pot_ref, coef, start, even, odd, filt, filtered, diag_rows, diag, pot_own, slab, halos, ops_y, ops_z, apply_ops,
    parts, scattered, summed, total, ortho_first, ortho_second,
    in_sem, pot_send, pot_recv, ghost_send, ghost_recv, vec_send, vec_recv, halo_send, halo_recv, small_send, small_recv,
    back_send, back_recv,
):
    s = lax.axis_index("strip")
    v = lax.axis_index("vec")
    y_lo = s // 2 % 2

    barrier = pltpu.get_barrier_semaphore()

    def greet(j, carry):
        for where in ({"vec": lax.rem(v + j, NV)}, {"strip": lax.rem(s + j, NS)}):
            pl.semaphore_signal(barrier, inc=1, device_id=where, device_id_type=pl.DeviceIdType.MESH)
        return carry

    pot_in = pltpu.make_async_copy(pot_hbm, pot_ref, in_sem.at[0])
    x_in = pltpu.make_async_copy(x_hbm, x_ref, in_sem.at[1])
    pot_in.start()
    x_in.start()
    lax.fori_loop(1, NV, greet, 0)

    def splat(i):
        return jnp.full((8, 128), bounds_ref[i], jnp.int32).astype(F32) * grid_unit

    edges = [splat(i) for i in range(4)]
    center = (edges[0] + edges[1]) * 0.5
    spread = (edges[1] - edges[0]) * 0.5
    scale = 2.0 / spread

    pot_in.wait()
    for r in range(ROWS // 8):
        tiles = []
        for t in range(SUB):
            level = pot_ref[8 * r:8 * r + 8, 128 * t:128 * t + 128].astype(F32)
            tiles.append(disorder * (level / (POT_LEVELS - 1) - 0.5))
        for c, field in enumerate(to_classes(tiles)):
            pot_own[pl.ds(64 * r + place(c), 8, stride=8), :] = field
            diag_rows[pl.ds(OWN + 64 * r + place(c), 8, stride=8), :] = (field - center) * scale

    x_in.wait()

    def classes_of(q, carry):
        for r in range(ROWS // 8):
            tiles = [0.5 * x_ref[q, 8 * r:8 * r + 8, 128 * t:128 * t + 128] for t in range(SUB)]
            for c, tile in enumerate(to_classes(tiles)):
                start[q, pl.ds(OWN + 64 * r + place(c), 8, stride=8), :] = tile
        return carry

    classes_of(0, 0)

    pl.semaphore_wait(barrier, NV + NS - 2)

    up = lax.rem(s + NS - 1, NS)
    down = lax.rem(s + 1, NS)
    up2 = lax.rem(s + NS - 2, NS)

    def pot_copies():
        mine = diag_rows.at[pl.ds(OWN, OWN)]
        return (
            remote(mine, diag_rows.at[pl.ds(2 * OWN, OWN)], pot_send.at[0], pot_recv.at[0], strip=up),
            remote(mine, diag_rows.at[pl.ds(0, OWN)], pot_send.at[1], pot_recv.at[1], strip=down),
        )

    def ghost_copies(q):
        mine = start.at[q, pl.ds(OWN, OWN)]
        return (
            remote(mine, start.at[q, pl.ds(2 * OWN, OWN)], ghost_send.at[q, 0], ghost_recv.at[q, 0], strip=up),
            remote(mine, start.at[q, pl.ds(0, OWN)], ghost_send.at[q, 1], ghost_recv.at[q, 1], strip=down),
            remote(
                start.at[q, pl.ds(OWN, SUB)], start.at[q, pl.ds(3 * OWN, SUB)],
                ghost_send.at[q, 2], ghost_recv.at[q, 2], strip=up2,
            ),
        )

    def start_ghosts(q):
        for copy in ghost_copies(q):
            copy.start()

    for copy in pot_copies():
        copy.start()
    start_ghosts(0)
    lax.fori_loop(1, NQ, classes_of, 0)

    theta_lo = arccos((edges[2] - center) / spread)
    theta_hi = arccos((edges[3] - center) / spread)
    coef[0:8] = (theta_lo - theta_hi) / math.pi

    def coefficient(k, carry):
        order = jnp.full((8, 128), k, jnp.int32).astype(F32)
        coef[pl.ds(pl.multiple_of(8 * k, 8), 8)] = (
            2.0 * (jnp.sin(order * theta_lo) - jnp.sin(order * theta_hi)) / (order * math.pi)
        )
        return carry

    lax.fori_loop(1, DEGREE + 1, coefficient, 0)

    def pair_place(row):
        return (16 * row, 0) if row <= 48 else (16 * (96 - row), 1)

    for copy in pot_copies() + ghost_copies(0):
        copy.wait_send()
    start_ghosts(1)

    for copy in pot_copies():
        copy.wait_recv()
    for row in range(1, 3 * ROWS):
        value = diag_rows[8 * row:8 * row + 8]
        for base, half in {pair_place(row), (16 * (96 - row), 1) if row == 48 else pair_place(row)}:
            diag[pl.ds(base + half, 8, stride=2), :] = value

    sub = lax.broadcasted_iota(jnp.int32, (8, 128), 0)
    lane = lax.broadcasted_iota(jnp.int32, (8, 128), 1)
    index_left = jnp.where(sub >= 6, (lane + 127) % 128, lane)
    index_right = jnp.where(sub < 2, (lane + 1) % 128, lane)
    upper = (sub % 2 == 0)[None, None]

    def shift(value, index, by):
        index = jnp.broadcast_to(index[None], value.shape)
        return pltpu.roll(jnp.take_along_axis(value, index, axis=2), by, 1)

    def update(k, low, high):
        now, then = (even, odd) if k % 2 else (odd, even)
        rows = high - low
        top = min(high + 1, PAIRS)
        ext = now[(low - 1) * 16:top * 16].reshape(top - low + 1, 2, 8, 128)
        above = ext[0:rows]
        mid = ext[1:rows + 1]
        if high == PAIRS:
            crossing = ext[rows - 1:rows]
            crossing = jnp.where(upper, pltpu.roll(crossing, 7, 2), pltpu.roll(crossing, 1, 2))
            below = jnp.concatenate([ext[2:rows + 1], crossing], axis=0)
        else:
            below = ext[2:rows + 2]
        left = shift(mid[:, 1], index_left, 2)
        right = shift(mid[:, 0], index_right, 6)
        before = then[low * 16:high * 16].reshape(rows, 2, 8, 128) if k > 1 else None
        local = diag[low * 16:high * 16].reshape(rows, 2, 8, 128)
        halves = []
        for j, beside in enumerate((left + mid[:, 1], mid[:, 0] + right)):
            inside = local[:, j] * mid[:, j]
            if k == 2:
                inside = inside - (before[:, j] + before[:, j])
            elif k > 2:
                inside = inside - before[:, j]
            halves.append(inside - scale * ((above[:, j] + below[:, j]) + beside))
        after = jnp.stack(halves, axis=1)
        then[low * 16:high * 16] = after.reshape(rows * 16, 128)
        if k % 2 == 0 and high == PAIRS:
            first = max(ROWS, low)
            c_now = coef[8 * k - 8:8 * k]
            c_next = coef[8 * k:8 * k + 8]
            term = c_now * mid[first - low:] + c_next * after[first - low:]
            place_in = slice((first - ROWS) * 16, (PAIRS - ROWS) * 16)
            filt[place_in] = filt[place_in] + term.reshape((PAIRS - first) * 16, 128)

    def send_vector(q, count):
        def send(j, carry):
            peer = lax.rem(v + j, NV)
            remote(
                filtered.at[q, pl.ds(peer * CHUNKS, count)], slab.at[pl.ds((v * NQ + q) * HALO, count)],
                vec_send.at[q], vec_recv.at[q], vec=peer,
            ).start()
            return carry

        lax.fori_loop(1, NV, send, 0)

    def one_vector(q, carry):
        for copy in ghost_copies(q):
            copy.wait_recv()
        for row in range(3 * ROWS + 1):
            value = start[q, 8 * row:8 * row + 8]
            base, half = pair_place(row)
            even[pl.ds(base + half, 8, stride=2), :] = value
            if row == 48:
                even[pl.ds(base + 1, 8, stride=2), :] = value
        filt[...] = (
            (2.0 * coef[0:8]) * even[16 * ROWS:16 * PAIRS].reshape(2 * (PAIRS - ROWS), 8, 128)
        ).reshape(16 * (PAIRS - ROWS), 128)
        for k in range(1, DEGREE + 1):
            if k < ROWS - 1:
                update(k, k, ROWS)
                update(k, ROWS, PAIRS)
            else:
                update(k, k, PAIRS)
            if k == DEGREE // 2:
                @pl.when(q < NQ - 2)
                def _():
                    for copy in ghost_copies(q + 1):
                        copy.wait_send()
                    start_ghosts(q + 2)

        for row in range(ROWS + 1):
            base, half = pair_place(ROWS + row)
            filtered[q, 8 * row:8 * row + 8] = filt[pl.ds(base - 16 * ROWS + half, 8, stride=2), :]
        slab[pl.ds((v * NQ + q) * HALO, HALO)] = filtered[q, pl.ds(v * CHUNKS, HALO)]

        @pl.when(q < LAST)
        def _():
            send_vector(q, HALO)

        @pl.when(q == LAST)
        def _():
            send_vector(q, CHUNKS)

        return carry

    lax.fori_loop(0, NQ, one_vector, 0)
    for q in range(NQ):
        wait_bytes(slab.at[pl.ds(0, (NV - 1) * (CHUNKS if q == LAST else HALO))], vec_recv.at[q])

    def take(source, stride, g, n):
        base = 16 * g * stride + n
        return jnp.concatenate(
            [source[pl.ds(base, 8, stride=stride), :], source[pl.ds(base + 8 * stride, 8, stride=stride), :]], axis=0
        )

    def keep(target, g, n, value):
        for part, half in enumerate(split(value)):
            target[64 * part + 16 * g:64 * part + 16 * g + 16, 128 * n:128 * n + 128] = half

    def matrix_part(left):
        prod = lax.dot_general(left[...], ops_y[...], (((1,), (1,)), ((), ())), preferred_element_type=F32)
        return prod[0:64] + prod[64:128]

    def along_strip(stage, i, source, target):
        for a, b, c in STRIP_STEPS:
            peer = lax.rem(s // 4 + a, 4) * 4 + lax.rem(y_lo + b, 2) * 2 + lax.rem(s % 2 + c, 2)
            remote(source(peer), target, small_send.at[i, stage], small_recv.at[i, stage], strip=peer).start()

    def scatter(i, value):
        for c in range(NS):
            parts[i, c] = value[PART * c:PART * c + PART]
        scattered[i, s] = parts[i, s]
        along_strip(0, i, lambda peer: parts.at[i, peer], scattered.at[i, s])

    def exchange(i):
        wait_bytes(scattered.at[i, pl.ds(0, NS - 1)], small_recv.at[i, 0])
        summed[i, v] = jnp.sum(scattered[i], axis=0)
        for a, b in VEC_STEPS:
            peer = lax.rem(v // 8 + a, 2) * 8 + lax.rem(v % 8 + b, 8)
            remote(
                summed.at[i, v], summed.at[i, v], small_send.at[i, 1], small_recv.at[i, 1], vec=peer
            ).start()

    def gather(i):
        wait_bytes(summed.at[i, pl.ds(0, NV - 1)], small_recv.at[i, 1])
        total[i, s] = jnp.sum(summed[i], axis=0)
        along_strip(2, i, lambda peer: total.at[i, s], total.at[i, s])

    def finish(i):
        wait_bytes(total.at[i, pl.ds(0, NS - 1)], small_recv.at[i, 2])
        value = jnp.concatenate([total[i, c] for c in range(NS)], axis=0)
        return value + pltpu.roll(value, 64, 1)

    for g in range(NVEC // 16):
        for n in range(CHUNKS):
            keep(ops_y, g, n, take(slab, HALO, g, n))
    scatter(0, matrix_part(ops_y))

    def send_halos(j, carry):
        peer = lax.rem(v + j, NV)
        remote(
            filtered.at[LAST, pl.ds(peer * CHUNKS + CHUNKS, SUB)], halos.at[v], halo_send.at[0], halo_recv.at[0], vec=peer
        ).start()
        return carry

    lax.fori_loop(1, NV, send_halos, 0)
    halos[v] = filtered[LAST, pl.ds(v * CHUNKS + CHUNKS, SUB)]

    for g in range(NVEC // 16):
        for row in range(PIECE):
            tiles = from_classes([take(slab, HALO, g, SUB * row + place(c)) for c in range(SUB)])
            for t, tile in enumerate(tiles):
                keep(apply_ops, g, SUB * row + t, tile)
    exchange(0)

    wait_bytes(halos.at[pl.ds(0, NV - 1)], halo_recv.at[0])
    for peer in range(NV):
        base = (peer * NQ + LAST) * HALO + CHUNKS
        slab[base:base + SUB] = halos[peer]
    pot_slab = pot_own[pl.ds(v * CHUNKS, CHUNKS)] * 0.5
    for g in range(NVEC // 16):
        y = [take(slab, HALO, g, n) for n in range(HALO)]
        for row in range(PIECE):
            for c in range(SUB):
                n = SUB * row + place(c)
                if c < SUB - 1:
                    right = y[SUB * row + place(c + 1)]
                else:
                    right = pltpu.roll(y[SUB * row + place(0)], 127, 1)
                keep(ops_z, g, n, pot_slab[n:n + 1] * y[n] - (right + y[n + SUB]))
    scatter(1, matrix_part(ops_z))
    gather(0)
    exchange(1)

    rows64 = lax.broadcasted_iota(jnp.int32, (64, 128), 0)
    lanes64 = lax.broadcasted_iota(jnp.int32, (64, 128), 1)
    gram = finish(0)
    aug = jnp.where(lanes64 < 64, gram, jnp.where(lanes64 - 64 == rows64, 1.0, 0.0))
    aug_rows = [aug[8 * i:8 * i + 8] for i in range(8)]

    blocks = []
    for half, ortho in enumerate((ortho_first, ortho_second)):
        block = eliminate(aug_rows, range(4 * half, 4 * half + 4))
        blocks.append(block)
        high, low = split(math.sqrt(SITES) * block)
        left = jnp.concatenate(
            [jnp.concatenate([high, high], axis=1), jnp.concatenate([low, low], axis=1)], axis=0
        )
        product = jnp.dot(left, apply_ops[...], preferred_element_type=F32)
        flat = ortho.reshape(NVEC // 2 * CHUNKS, 128)
        for n in range(CHUNKS):
            value = product[0:32, 128 * n:128 * n + 128] + product[32:64, 128 * n:128 * n + 128]
            for g in range(4):
                flat[pl.ds(n + 8 * g * CHUNKS, 8, stride=CHUNKS), :] = value[8 * g:8 * g + 8]

        def send_back(j, carry, half=half, ortho=ortho):
            local = lax.rem(v + j, NV // 2)
            peer = local + half * (NV // 2)

            @pl.when(peer != v)
            def _():
                remote(
                    ortho.at[pl.ds(local * NQ, NQ)], fields.at[:, pl.ds(v * CHUNKS, CHUNKS)],
                    back_send.at[0], back_recv.at[0], vec=peer,
                ).start()

            @pl.when(peer == v)
            def _():
                fields[:, pl.ds(v * CHUNKS, CHUNKS)] = ortho[pl.ds(local * NQ, NQ)]

            return carry

        lax.fori_loop(0, NV // 2, send_back, 0)
    inverse = jnp.concatenate(blocks, axis=0)

    gather(1)
    cross = finish(1)[:, 0:64]
    cross = cross + cross.T
    half = jnp.dot(inverse, cross, precision=lax.Precision.HIGHEST, preferred_element_type=F32)
    ritz_ref[...] = float(ROWS) * lax.dot_general(
        inverse, half, (((1,), (1,)), ((), ())), precision=lax.Precision.HIGHEST, preferred_element_type=F32
    )

    wait_bytes(slab.at[pl.ds(0, (NV - 1) * NQ * CHUNKS)], back_recv.at[0])
    wait_bytes(slab.at[pl.ds(0, (NV - 1) * NQ * CHUNKS)], back_send.at[0])
    for i in range(2):
        for stage in range(3):
            wait_bytes(total.at[i, pl.ds(0, NS - 1)], small_send.at[i, stage])
    wait_bytes(halos.at[pl.ds(0, NV - 1)], halo_send.at[0])
    for q in range(NQ):
        wait_bytes(slab.at[pl.ds(0, (NV - 1) * (CHUNKS if q == LAST else HALO))], vec_send.at[q])
    for copy in ghost_copies(NQ - 1):
        copy.wait_send()


def arrange(fields, ritz, out_ref, ritz_ref):
    for q in range(NQ):
        for r in range(ROWS // 8):
            for t in range(SUB):
                out_ref[q, 8 * r:8 * r + 8, 128 * t:128 * t + 128] = fields[q, pl.ds(64 * r + t, 8, stride=8), :]
    ritz_ref[...] = ritz[...]


def shards(start_vectors, potential, bounds):
    vmem = pl.BlockSpec(memory_space=pltpu.VMEM)
    hbm = pl.BlockSpec(memory_space=pltpu.HBM)
    dma = pltpu.SemaphoreType.DMA
    ritz_shape = jax.ShapeDtypeStruct((NVEC, NVEC), F32)
    fields, ritz = pl.pallas_call(
        kernel,
        out_shape=(pltpu.VMEM((NQ, OWN, 128), F32), pltpu.VMEM((NVEC, NVEC), F32)),
        in_specs=[pl.BlockSpec(memory_space=pltpu.SMEM), hbm, hbm],
        out_specs=(vmem, vmem),
        scratch_shapes=[
            pltpu.VMEM((NQ, ROWS, 1024), F32),
            pltpu.VMEM((ROWS, 1024), jnp.int32),
            pltpu.VMEM((8 * (DEGREE + 1), 128), F32),
            pltpu.VMEM((NQ, FIELD, 128), F32),
            pltpu.VMEM((16 * PAIRS, 128), F32),
            pltpu.VMEM((16 * PAIRS, 128), F32),
            pltpu.VMEM((16 * (PAIRS - ROWS), 128), F32),
            pltpu.VMEM((NQ, OWN + SUB, 128), F32),
            pltpu.VMEM((FIELD, 128), F32),
            pltpu.VMEM((16 * PAIRS, 128), F32),
            pltpu.VMEM((OWN, 128), F32),
            pltpu.VMEM((NVEC * HALO, 128), F32),
            pltpu.VMEM((NV, SUB, 128), F32),
            pltpu.VMEM((128, CHUNKS * 128), BF16),
            pltpu.VMEM((128, CHUNKS * 128), BF16),
            pltpu.VMEM((128, CHUNKS * 128), BF16),
            pltpu.VMEM((2, NS, PART, 128), F32),
            pltpu.VMEM((2, NS, PART, 128), F32),
            pltpu.VMEM((2, NV, PART, 128), F32),
            pltpu.VMEM((2, NS, PART, 128), F32),
            pltpu.VMEM((NVEC // 2, CHUNKS, 128), F32),
            pltpu.VMEM((NVEC // 2, CHUNKS, 128), F32),
            dma((2,)), dma((2,)), dma((2,)), dma((NQ, 3)), dma((NQ, 3)), dma((NQ,)), dma((NQ,)), dma((1,)), dma((1,)),
            dma((2, 3)), dma((2, 3)), dma((1,)), dma((1,)),
        ],
        compiler_params=pltpu.CompilerParams(
            collective_id=0, has_side_effects=True, vmem_limit_bytes=60 << 20
        ),
        name="filter_ritz",
    )(bounds, start_vectors, potential)
    return pl.pallas_call(
        arrange,
        out_shape=(jax.ShapeDtypeStruct((NQ, ROWS, 1024), F32), ritz_shape),
        in_specs=[vmem, vmem],
        out_specs=(vmem, vmem),
        name="arrange",
    )(pltpu.with_memory_space_constraint(fields, pltpu.VMEM), pltpu.with_memory_space_constraint(ritz, pltpu.VMEM))


def solution(mesh):
    in_specs = (P("vec", "strip", None), P("strip", None), P())
    out_specs = (P("vec", "strip", None), P())
    return jax.shard_map(shards, mesh=mesh, in_specs=in_specs, out_specs=out_specs, check_vma=False)
```

```python
import math

import jax
import jax.numpy as jnp
from jax import lax
from jax.experimental import pallas as pl
from jax.experimental.pallas import tpu as pltpu
from jax.sharding import PartitionSpec as P

DEGREE = 32
POT_LEVELS = 16
NQ = 4
ROWS = 32
NV = 16
NS = 16
NVEC = NQ * NV
PIECE = ROWS // NV
SUB = 8
CHUNKS = PIECE * SUB
HALO = CHUNKS + SUB
LAST = NQ - 1
FIELD = (3 * ROWS + 1) * SUB
PAIRS = 3 * ROWS // 2 + 1
STRIP_STEPS = sorted(
    ((a, b, c) for a in range(4) for b in range(2) for c in range(2) if a or b or c),
    key=lambda step: -(2 * min(step[0], 4 - step[0]) + 2 * step[1] + step[2]),
)
VEC_STEPS = sorted(
    ((a, b) for a in range(2) for b in range(8) if a or b), key=lambda step: -(2 * step[0] + min(step[1], 8 - step[1]))
)
PART = NVEC // NS
OWN = ROWS * SUB
HALF_PI = math.pi / 2
SITES = NS * ROWS * 1024

grid_unit = 0.0625
disorder = 2.0
F32 = jnp.float32
BF16 = jnp.bfloat16


def remote(src, dst, send, recv, **where):
    return pltpu.make_async_remote_copy(
        src_ref=src, dst_ref=dst, send_sem=send, recv_sem=recv,
        device_id=where, device_id_type=pl.DeviceIdType.MESH,
    )


def wait_bytes(ref, sem):
    pltpu.make_async_copy(ref, ref, sem).wait()


def split(value):
    high = value.astype(BF16)
    return high, (value - high.astype(F32)).astype(BF16)


def arccos(x):
    size = jnp.abs(x)
    large = size > 0.5
    square = jnp.where(large, 0.5 * (1.0 - size), x * x)
    base = jnp.where(large, jnp.sqrt(square), size)
    poly = 4.2163199048e-2 * square + 2.4181311049e-2
    poly = poly * square + 4.5470025998e-2
    poly = poly * square + 7.4953002686e-2
    poly = poly * square + 1.6666752422e-1
    arcsin = base + base * square * poly
    positive = jnp.where(large, 2.0 * arcsin, HALF_PI - arcsin)
    return jnp.where(x < 0.0, math.pi - positive, positive)


def place(s):
    return 4 * (s % 2) + s // 2


def turn_blocks(tiles):
    tiles = list(tiles)
    block = lax.broadcasted_iota(jnp.int32, tiles[0].shape, 1) // 16
    for bit in (1, 2, 4):
        clear = (block & bit) == 0
        for i in range(8):
            if i & bit == 0:
                one, two = tiles[i], tiles[i + bit]
                tiles[i] = jnp.where(clear, one, pltpu.roll(two, 16 * bit, 1))
                tiles[i + bit] = jnp.where(clear, pltpu.roll(one, 128 - 16 * bit, 1), two)
    return tiles


def to_classes(tiles):
    lane = lax.broadcasted_iota(jnp.int32, tiles[0].shape, 1)
    index = 8 * (lane % 16) + lane // 16
    return turn_blocks([jnp.take_along_axis(tile, index, axis=1) for tile in tiles])


def from_classes(tiles):
    lane = lax.broadcasted_iota(jnp.int32, tiles[0].shape, 1)
    index = 16 * (lane % 8) + lane // 8
    return [jnp.take_along_axis(tile, index, axis=1) for tile in turn_blocks(tiles)]


def eliminate(rows, panels):
    sub = lax.broadcasted_iota(jnp.int32, (8, 128), 0)
    done = []

    def spread(value, k):
        return jnp.broadcast_to(value[k:k + 1], (8, 128))

    for p in panels:
        columns = {
            (j, i): jnp.broadcast_to(rows[i][:, 8 * p + j:8 * p + j + 1], (8, 128))
            for i in range(p, 8) for j in range(8)
        }
        pivots = spread(columns[0, p], 0)
        for k in range(8):
            pivot = spread(columns[k, p], k)
            pivots = jnp.where(sub == k, pivot, pivots)
            inverse = 1.0 / pivot
            row = spread(rows[p], k)
            heads = {j: spread(columns[j, p], k) for j in range(k + 1, 8)}
            for i in range(p, 8):
                factor = columns[k, i] * inverse
                if i == p:
                    factor = jnp.where(sub > k, factor, 0.0)
                rows[i] = rows[i] - factor * row
                for j in range(k + 1, 8):
                    columns[j, i] = columns[j, i] - factor * heads[j]
        done.append(pltpu.roll(rows[p], 64, 1) * lax.rsqrt(pivots))
    return jnp.concatenate(done, axis=0)[:, 0:64]


def kernel(
    bounds_ref, x_hbm, pot_hbm, fields, ritz_ref,
    x_ref, pot_ref, coef, start, even, odd, filt, filtered, diag_rows, diag, pot_own, slab, halos, ops_y, ops_z, apply_ops,
    parts, scattered, summed, total, ortho_first, ortho_second,
    in_sem, pot_send, pot_recv, ghost_send, ghost_recv, vec_send, vec_recv, halo_send, halo_recv, small_send, small_recv,
    back_send, back_recv,
):
    s = lax.axis_index("strip")
    v = lax.axis_index("vec")
    y_lo = s // 2 % 2

    barrier = pltpu.get_barrier_semaphore()

    def greet(j, carry):
        for where in ({"vec": lax.rem(v + j, NV)}, {"strip": lax.rem(s + j, NS)}):
            pl.semaphore_signal(barrier, inc=1, device_id=where, device_id_type=pl.DeviceIdType.MESH)
        return carry

    pot_in = pltpu.make_async_copy(pot_hbm, pot_ref, in_sem.at[0])
    x_in = pltpu.make_async_copy(x_hbm, x_ref, in_sem.at[1])
    pot_in.start()
    x_in.start()
    lax.fori_loop(1, NV, greet, 0)

    def splat(i):
        return jnp.full((8, 128), bounds_ref[i], jnp.int32).astype(F32) * grid_unit

    edges = [splat(i) for i in range(4)]
    center = (edges[0] + edges[1]) * 0.5
    spread = (edges[1] - edges[0]) * 0.5
    scale = 2.0 / spread

    pot_in.wait()
    for r in range(ROWS // 8):
        tiles = []
        for t in range(SUB):
            level = pot_ref[8 * r:8 * r + 8, 128 * t:128 * t + 128].astype(F32)
            tiles.append(disorder * (level / (POT_LEVELS - 1) - 0.5))
        for c, field in enumerate(to_classes(tiles)):
            pot_own[pl.ds(64 * r + place(c), 8, stride=8), :] = field
            diag_rows[pl.ds(OWN + 64 * r + place(c), 8, stride=8), :] = (field - center) * scale

    x_in.wait()

    def classes_of(q, carry):
        for r in range(ROWS // 8):
            tiles = [0.5 * x_ref[q, 8 * r:8 * r + 8, 128 * t:128 * t + 128] for t in range(SUB)]
            for c, tile in enumerate(to_classes(tiles)):
                start[q, pl.ds(OWN + 64 * r + place(c), 8, stride=8), :] = tile
        return carry

    classes_of(0, 0)

    pl.semaphore_wait(barrier, NV + NS - 2)

    up = lax.rem(s + NS - 1, NS)
    down = lax.rem(s + 1, NS)
    up2 = lax.rem(s + NS - 2, NS)

    def pot_copies():
        mine = diag_rows.at[pl.ds(OWN, OWN)]
        return (
            remote(mine, diag_rows.at[pl.ds(2 * OWN, OWN)], pot_send.at[0], pot_recv.at[0], strip=up),
            remote(mine, diag_rows.at[pl.ds(0, OWN)], pot_send.at[1], pot_recv.at[1], strip=down),
        )

    def ghost_copies(q):
        mine = start.at[q, pl.ds(OWN, OWN)]
        return (
            remote(mine, start.at[q, pl.ds(2 * OWN, OWN)], ghost_send.at[q, 0], ghost_recv.at[q, 0], strip=up),
            remote(mine, start.at[q, pl.ds(0, OWN)], ghost_send.at[q, 1], ghost_recv.at[q, 1], strip=down),
            remote(
                start.at[q, pl.ds(OWN, SUB)], start.at[q, pl.ds(3 * OWN, SUB)],
                ghost_send.at[q, 2], ghost_recv.at[q, 2], strip=up2,
            ),
        )

    def start_ghosts(q):
        for copy in ghost_copies(q):
            copy.start()

    for copy in pot_copies():
        copy.start()
    start_ghosts(0)
    lax.fori_loop(1, NQ, classes_of, 0)

    theta_lo = arccos((edges[2] - center) / spread)
    theta_hi = arccos((edges[3] - center) / spread)
    coef[0:8] = (theta_lo - theta_hi) / math.pi

    def coefficient(k, carry):
        order = jnp.full((8, 128), k, jnp.int32).astype(F32)
        coef[pl.ds(pl.multiple_of(8 * k, 8), 8)] = (
            2.0 * (jnp.sin(order * theta_lo) - jnp.sin(order * theta_hi)) / (order * math.pi)
        )
        return carry

    lax.fori_loop(1, DEGREE + 1, coefficient, 0)

    def pair_place(row):
        return (16 * row, 0) if row <= 48 else (16 * (96 - row), 1)

    for copy in pot_copies() + ghost_copies(0):
        copy.wait_send()
    start_ghosts(1)

    for copy in pot_copies():
        copy.wait_recv()
    for row in range(1, 3 * ROWS):
        value = diag_rows[8 * row:8 * row + 8]
        for base, half in {pair_place(row), (16 * (96 - row), 1) if row == 48 else pair_place(row)}:
            diag[pl.ds(base + half, 8, stride=2), :] = value

    sub = lax.broadcasted_iota(jnp.int32, (8, 128), 0)
    lane = lax.broadcasted_iota(jnp.int32, (8, 128), 1)
    index_left = jnp.where(sub >= 6, (lane + 127) % 128, lane)
    index_right = jnp.where(sub < 2, (lane + 1) % 128, lane)
    upper = (sub % 2 == 0)[None, None]

    def shift(value, index, by):
        index = jnp.broadcast_to(index[None], value.shape)
        return pltpu.roll(jnp.take_along_axis(value, index, axis=2), by, 1)

    def update(k, low, high):
        now, then = (even, odd) if k % 2 else (odd, even)
        rows = high - low
        top = min(high + 1, PAIRS)
        ext = now[(low - 1) * 16:top * 16].reshape(top - low + 1, 2, 8, 128)
        above = ext[0:rows]
        mid = ext[1:rows + 1]
        if high == PAIRS:
            crossing = ext[rows - 1:rows]
            crossing = jnp.where(upper, pltpu.roll(crossing, 7, 2), pltpu.roll(crossing, 1, 2))
            below = jnp.concatenate([ext[2:rows + 1], crossing], axis=0)
        else:
            below = ext[2:rows + 2]
        left = shift(mid[:, 1], index_left, 2)
        right = shift(mid[:, 0], index_right, 6)
        before = then[low * 16:high * 16].reshape(rows, 2, 8, 128) if k > 1 else None
        local = diag[low * 16:high * 16].reshape(rows, 2, 8, 128)
        halves = []
        for j, beside in enumerate((left + mid[:, 1], mid[:, 0] + right)):
            inside = local[:, j] * mid[:, j]
            if k == 2:
                inside = inside - (before[:, j] + before[:, j])
            elif k > 2:
                inside = inside - before[:, j]
            halves.append(inside - scale * ((above[:, j] + below[:, j]) + beside))
        after = jnp.stack(halves, axis=1)
        then[low * 16:high * 16] = after.reshape(rows * 16, 128)
        if k % 2 == 0 and high == PAIRS:
            first = max(ROWS, low)
            c_now = coef[8 * k - 8:8 * k]
            c_next = coef[8 * k:8 * k + 8]
            term = c_now * mid[first - low:] + c_next * after[first - low:]
            place_in = slice((first - ROWS) * 16, (PAIRS - ROWS) * 16)
            filt[place_in] = filt[place_in] + term.reshape((PAIRS - first) * 16, 128)

    def vec_peer(step):
        return lax.rem(v // 8 + step[0], 2) * 8 + lax.rem(v % 8 + step[1], 8)

    def send_vector(q, count):
        for step in VEC_STEPS:
            peer = vec_peer(step)
            remote(
                filtered.at[q, pl.ds(peer * CHUNKS, count)], slab.at[pl.ds((v * NQ + q) * HALO, count)],
                vec_send.at[q], vec_recv.at[q], vec=peer,
            ).start()

    def one_vector(q, carry):
        for copy in ghost_copies(q):
            copy.wait_recv()
        for row in range(3 * ROWS + 1):
            value = start[q, 8 * row:8 * row + 8]
            base, half = pair_place(row)
            even[pl.ds(base + half, 8, stride=2), :] = value
            if row == 48:
                even[pl.ds(base + 1, 8, stride=2), :] = value
        filt[...] = (
            (2.0 * coef[0:8]) * even[16 * ROWS:16 * PAIRS].reshape(2 * (PAIRS - ROWS), 8, 128)
        ).reshape(16 * (PAIRS - ROWS), 128)
        for k in range(1, DEGREE + 1):
            if k < ROWS - 1:
                update(k, k, ROWS)
                update(k, ROWS, PAIRS)
            else:
                update(k, k, PAIRS)
            if k == DEGREE // 2:
                @pl.when(q < NQ - 2)
                def _():
                    for copy in ghost_copies(q + 1):
                        copy.wait_send()
                    start_ghosts(q + 2)

        for row in range(ROWS + 1):
            base, half = pair_place(ROWS + row)
            filtered[q, 8 * row:8 * row + 8] = filt[pl.ds(base - 16 * ROWS + half, 8, stride=2), :]
        slab[pl.ds((v * NQ + q) * HALO, HALO)] = filtered[q, pl.ds(v * CHUNKS, HALO)]

        @pl.when(q < LAST)
        def _():
            send_vector(q, HALO)

        @pl.when(q == LAST)
        def _():
            send_vector(q, CHUNKS)

        return carry

    lax.fori_loop(0, NQ, one_vector, 0)
    for q in range(NQ):
        wait_bytes(slab.at[pl.ds(0, (NV - 1) * (CHUNKS if q == LAST else HALO))], vec_recv.at[q])

    def take(source, stride, g, n):
        base = 16 * g * stride + n
        return jnp.concatenate(
            [source[pl.ds(base, 8, stride=stride), :], source[pl.ds(base + 8 * stride, 8, stride=stride), :]], axis=0
        )

    def keep(target, g, n, value):
        for part, half in enumerate(split(value)):
            target[64 * part + 16 * g:64 * part + 16 * g + 16, 128 * n:128 * n + 128] = half

    def matrix_part(left):
        prod = lax.dot_general(left[...], ops_y[...], (((1,), (1,)), ((), ())), preferred_element_type=F32)
        return prod[0:64] + prod[64:128]

    def along_strip(stage, i, source, target):
        for a, b, c in STRIP_STEPS:
            peer = lax.rem(s // 4 + a, 4) * 4 + lax.rem(y_lo + b, 2) * 2 + lax.rem(s % 2 + c, 2)
            remote(source(peer), target, small_send.at[i, stage], small_recv.at[i, stage], strip=peer).start()

    def scatter(i, value):
        for c in range(NS):
            parts[i, c] = value[PART * c:PART * c + PART]
        scattered[i, s] = parts[i, s]
        along_strip(0, i, lambda peer: parts.at[i, peer], scattered.at[i, s])

    def exchange(i):
        wait_bytes(scattered.at[i, pl.ds(0, NS - 1)], small_recv.at[i, 0])
        summed[i, v] = jnp.sum(scattered[i], axis=0)
        for step in VEC_STEPS:
            remote(
                summed.at[i, v], summed.at[i, v], small_send.at[i, 1], small_recv.at[i, 1], vec=vec_peer(step)
            ).start()

    def gather(i):
        wait_bytes(summed.at[i, pl.ds(0, NV - 1)], small_recv.at[i, 1])
        total[i, s] = jnp.sum(summed[i], axis=0)
        along_strip(2, i, lambda peer: total.at[i, s], total.at[i, s])

    def finish(i):
        wait_bytes(total.at[i, pl.ds(0, NS - 1)], small_recv.at[i, 2])
        value = jnp.concatenate([total[i, c] for c in range(NS)], axis=0)
        return value + pltpu.roll(value, 64, 1)

    for g in range(NVEC // 16):
        for n in range(CHUNKS):
            keep(ops_y, g, n, take(slab, HALO, g, n))
    scatter(0, matrix_part(ops_y))

    def send_halos(j, carry):
        peer = lax.rem(v + j, NV)
        remote(
            filtered.at[LAST, pl.ds(peer * CHUNKS + CHUNKS, SUB)], halos.at[v], halo_send.at[0], halo_recv.at[0], vec=peer
        ).start()
        return carry

    lax.fori_loop(1, NV, send_halos, 0)
    halos[v] = filtered[LAST, pl.ds(v * CHUNKS + CHUNKS, SUB)]

    for g in range(NVEC // 16):
        for row in range(PIECE):
            tiles = from_classes([take(slab, HALO, g, SUB * row + place(c)) for c in range(SUB)])
            for t, tile in enumerate(tiles):
                keep(apply_ops, g, SUB * row + t, tile)
    exchange(0)

    wait_bytes(halos.at[pl.ds(0, NV - 1)], halo_recv.at[0])
    for peer in range(NV):
        base = (peer * NQ + LAST) * HALO + CHUNKS
        slab[base:base + SUB] = halos[peer]
    pot_slab = pot_own[pl.ds(v * CHUNKS, CHUNKS)] * 0.5
    for g in range(NVEC // 16):
        y = [take(slab, HALO, g, n) for n in range(HALO)]
        for row in range(PIECE):
            for c in range(SUB):
                n = SUB * row + place(c)
                if c < SUB - 1:
                    right = y[SUB * row + place(c + 1)]
                else:
                    right = pltpu.roll(y[SUB * row + place(0)], 127, 1)
                keep(ops_z, g, n, pot_slab[n:n + 1] * y[n] - (right + y[n + SUB]))
    scatter(1, matrix_part(ops_z))
    gather(0)
    exchange(1)

    rows64 = lax.broadcasted_iota(jnp.int32, (64, 128), 0)
    lanes64 = lax.broadcasted_iota(jnp.int32, (64, 128), 1)
    gram = finish(0)
    aug = jnp.where(lanes64 < 64, gram, jnp.where(lanes64 - 64 == rows64, 1.0, 0.0))
    aug_rows = [aug[8 * i:8 * i + 8] for i in range(8)]

    blocks = []
    for half, ortho in enumerate((ortho_first, ortho_second)):
        block = eliminate(aug_rows, range(4 * half, 4 * half + 4))
        blocks.append(block)
        high, low = split(math.sqrt(SITES) * block)
        left = jnp.concatenate(
            [jnp.concatenate([high, high], axis=1), jnp.concatenate([low, low], axis=1)], axis=0
        )
        product = jnp.dot(left, apply_ops[...], preferred_element_type=F32)
        flat = ortho.reshape(NVEC // 2 * CHUNKS, 128)
        for n in range(CHUNKS):
            value = product[0:32, 128 * n:128 * n + 128] + product[32:64, 128 * n:128 * n + 128]
            for g in range(4):
                flat[pl.ds(n + 8 * g * CHUNKS, 8, stride=CHUNKS), :] = value[8 * g:8 * g + 8]

        def send_back(j, carry, half=half, ortho=ortho):
            local = lax.rem(v + j, NV // 2)
            peer = local + half * (NV // 2)

            @pl.when(peer != v)
            def _():
                remote(
                    ortho.at[pl.ds(local * NQ, NQ)], fields.at[:, pl.ds(v * CHUNKS, CHUNKS)],
                    back_send.at[0], back_recv.at[0], vec=peer,
                ).start()

            @pl.when(peer == v)
            def _():
                fields[:, pl.ds(v * CHUNKS, CHUNKS)] = ortho[pl.ds(local * NQ, NQ)]

            return carry

        lax.fori_loop(0, NV // 2, send_back, 0)
    inverse = jnp.concatenate(blocks, axis=0)

    gather(1)
    cross = finish(1)[:, 0:64]
    cross = cross + cross.T
    half = jnp.dot(inverse, cross, precision=lax.Precision.HIGHEST, preferred_element_type=F32)
    ritz_ref[...] = float(ROWS) * lax.dot_general(
        inverse, half, (((1,), (1,)), ((), ())), precision=lax.Precision.HIGHEST, preferred_element_type=F32
    )

    wait_bytes(slab.at[pl.ds(0, (NV - 1) * NQ * CHUNKS)], back_recv.at[0])
    wait_bytes(slab.at[pl.ds(0, (NV - 1) * NQ * CHUNKS)], back_send.at[0])
    for i in range(2):
        for stage in range(3):
            wait_bytes(total.at[i, pl.ds(0, NS - 1)], small_send.at[i, stage])
    wait_bytes(halos.at[pl.ds(0, NV - 1)], halo_send.at[0])
    for q in range(NQ):
        wait_bytes(slab.at[pl.ds(0, (NV - 1) * (CHUNKS if q == LAST else HALO))], vec_send.at[q])
    for copy in ghost_copies(NQ - 1):
        copy.wait_send()


def arrange(fields, ritz, out_ref, ritz_ref):
    q = pl.program_id(0)
    for r in range(ROWS // 8):
        for t in range(SUB):
            out_ref[0, 8 * r:8 * r + 8, 128 * t:128 * t + 128] = fields[q, pl.ds(64 * r + t, 8, stride=8), :]
    ritz_ref[...] = ritz[...]


def shards(start_vectors, potential, bounds):
    vmem = pl.BlockSpec(memory_space=pltpu.VMEM)
    hbm = pl.BlockSpec(memory_space=pltpu.HBM)
    dma = pltpu.SemaphoreType.DMA
    ritz_shape = jax.ShapeDtypeStruct((NVEC, NVEC), F32)
    fields, ritz = pl.pallas_call(
        kernel,
        out_shape=(pltpu.VMEM((NQ, OWN, 128), F32), pltpu.VMEM((NVEC, NVEC), F32)),
        in_specs=[pl.BlockSpec(memory_space=pltpu.SMEM), hbm, hbm],
        out_specs=(vmem, vmem),
        scratch_shapes=[
            pltpu.VMEM((NQ, ROWS, 1024), F32),
            pltpu.VMEM((ROWS, 1024), jnp.int32),
            pltpu.VMEM((8 * (DEGREE + 1), 128), F32),
            pltpu.VMEM((NQ, FIELD, 128), F32),
            pltpu.VMEM((16 * PAIRS, 128), F32),
            pltpu.VMEM((16 * PAIRS, 128), F32),
            pltpu.VMEM((16 * (PAIRS - ROWS), 128), F32),
            pltpu.VMEM((NQ, OWN + SUB, 128), F32),
            pltpu.VMEM((FIELD, 128), F32),
            pltpu.VMEM((16 * PAIRS, 128), F32),
            pltpu.VMEM((OWN, 128), F32),
            pltpu.VMEM((NVEC * HALO, 128), F32),
            pltpu.VMEM((NV, SUB, 128), F32),
            pltpu.VMEM((128, CHUNKS * 128), BF16),
            pltpu.VMEM((128, CHUNKS * 128), BF16),
            pltpu.VMEM((128, CHUNKS * 128), BF16),
            pltpu.VMEM((2, NS, PART, 128), F32),
            pltpu.VMEM((2, NS, PART, 128), F32),
            pltpu.VMEM((2, NV, PART, 128), F32),
            pltpu.VMEM((2, NS, PART, 128), F32),
            pltpu.VMEM((NVEC // 2, CHUNKS, 128), F32),
            pltpu.VMEM((NVEC // 2, CHUNKS, 128), F32),
            dma((2,)), dma((2,)), dma((2,)), dma((NQ, 3)), dma((NQ, 3)), dma((NQ,)), dma((NQ,)), dma((1,)), dma((1,)),
            dma((2, 3)), dma((2, 3)), dma((1,)), dma((1,)),
        ],
        compiler_params=pltpu.CompilerParams(
            collective_id=0, has_side_effects=True, vmem_limit_bytes=60 << 20
        ),
        name="filter_ritz",
    )(bounds, start_vectors, potential)
    return pl.pallas_call(
        arrange,
        out_shape=(jax.ShapeDtypeStruct((NQ, ROWS, 1024), F32), ritz_shape),
        grid=(NQ,),
        in_specs=[vmem, vmem],
        out_specs=(pl.BlockSpec((1, ROWS, 1024), lambda q: (q, 0, 0)), pl.BlockSpec((NVEC, NVEC), lambda q: (0, 0))),
        name="arrange",
    )(pltpu.with_memory_space_constraint(fields, pltpu.VMEM), pltpu.with_memory_space_constraint(ritz, pltpu.VMEM))


def solution(mesh):
    in_specs = (P("vec", "strip", None), P("strip", None), P())
    out_specs = (P("vec", "strip", None), P())
    return jax.shard_map(shards, mesh=mesh, in_specs=in_specs, out_specs=out_specs, check_vma=False)
```

```python
import math

import jax
import jax.numpy as jnp
from jax import lax
from jax.experimental import pallas as pl
from jax.experimental.pallas import tpu as pltpu
from jax.sharding import PartitionSpec as P

DEGREE = 32
POT_LEVELS = 16
NQ = 4
ROWS = 32
NV = 16
NS = 16
NVEC = NQ * NV
PIECE = ROWS // NV
SUB = 8
CHUNKS = PIECE * SUB
HALO = CHUNKS + SUB
LAST = NQ - 1
FIELD = (3 * ROWS + 1) * SUB
PAIRS = 3 * ROWS // 2 + 1
STRIP_STEPS = sorted(
    ((a, b, c) for a in range(4) for b in range(2) for c in range(2) if a or b or c),
    key=lambda step: -(2 * min(step[0], 4 - step[0]) + 2 * step[1] + step[2]),
)
VEC_STEPS = sorted(
    ((a, b) for a in range(2) for b in range(8) if a or b), key=lambda step: -(2 * step[0] + min(step[1], 8 - step[1]))
)
PART = NVEC // NS
OWN = ROWS * SUB
HALF_PI = math.pi / 2
SITES = NS * ROWS * 1024

grid_unit = 0.0625
disorder = 2.0
F32 = jnp.float32
BF16 = jnp.bfloat16


def remote(src, dst, send, recv, **where):
    return pltpu.make_async_remote_copy(
        src_ref=src, dst_ref=dst, send_sem=send, recv_sem=recv,
        device_id=where, device_id_type=pl.DeviceIdType.MESH,
    )


def wait_bytes(ref, sem):
    pltpu.make_async_copy(ref, ref, sem).wait()


def split(value):
    high = value.astype(BF16)
    return high, (value - high.astype(F32)).astype(BF16)


def arccos(x):
    size = jnp.abs(x)
    large = size > 0.5
    square = jnp.where(large, 0.5 * (1.0 - size), x * x)
    base = jnp.where(large, jnp.sqrt(square), size)
    poly = 4.2163199048e-2 * square + 2.4181311049e-2
    poly = poly * square + 4.5470025998e-2
    poly = poly * square + 7.4953002686e-2
    poly = poly * square + 1.6666752422e-1
    arcsin = base + base * square * poly
    positive = jnp.where(large, 2.0 * arcsin, HALF_PI - arcsin)
    return jnp.where(x < 0.0, math.pi - positive, positive)


def place(s):
    return 4 * (s % 2) + s // 2


def turn_blocks(tiles):
    tiles = list(tiles)
    block = lax.broadcasted_iota(jnp.int32, tiles[0].shape, 1) // 16
    for bit in (1, 2, 4):
        clear = (block & bit) == 0
        for i in range(8):
            if i & bit == 0:
                one, two = tiles[i], tiles[i + bit]
                tiles[i] = jnp.where(clear, one, pltpu.roll(two, 16 * bit, 1))
                tiles[i + bit] = jnp.where(clear, pltpu.roll(one, 128 - 16 * bit, 1), two)
    return tiles


def to_classes(tiles):
    lane = lax.broadcasted_iota(jnp.int32, tiles[0].shape, 1)
    index = 8 * (lane % 16) + lane // 16
    return turn_blocks([jnp.take_along_axis(tile, index, axis=1) for tile in tiles])


def from_classes(tiles):
    lane = lax.broadcasted_iota(jnp.int32, tiles[0].shape, 1)
    index = 16 * (lane % 8) + lane // 8
    return [jnp.take_along_axis(tile, index, axis=1) for tile in turn_blocks(tiles)]


def eliminate(rows, panels):
    sub = lax.broadcasted_iota(jnp.int32, (8, 128), 0)
    done = []

    def spread(value, k):
        return jnp.broadcast_to(value[k:k + 1], (8, 128))

    for p in panels:
        columns = {
            (j, i): jnp.broadcast_to(rows[i][:, 8 * p + j:8 * p + j + 1], (8, 128))
            for i in range(p, 8) for j in range(8)
        }
        pivots = spread(columns[0, p], 0)
        for k in range(8):
            pivot = spread(columns[k, p], k)
            pivots = jnp.where(sub == k, pivot, pivots)
            inverse = 1.0 / pivot
            row = spread(rows[p], k)
            heads = {j: spread(columns[j, p], k) for j in range(k + 1, 8)}
            for i in range(p, 8):
                factor = columns[k, i] * inverse
                if i == p:
                    factor = jnp.where(sub > k, factor, 0.0)
                rows[i] = rows[i] - factor * row
                for j in range(k + 1, 8):
                    columns[j, i] = columns[j, i] - factor * heads[j]
        done.append(pltpu.roll(rows[p], 64, 1) * lax.rsqrt(pivots))
    return jnp.concatenate(done, axis=0)[:, 0:64]


def kernel(
    bounds_ref, x_hbm, pot_hbm, fields, ritz_ref,
    x_ref, pot_ref, coef, start, even, odd, filt, filtered, diag_rows, diag, pot_own, slab, halos, ops_y, ops_z, apply_ops,
    parts, scattered, summed, total, ortho_first, ortho_second,
    in_sem, pot_send, pot_recv, ghost_send, ghost_recv, vec_send, vec_recv, halo_send, halo_recv, small_send, small_recv,
    back_send, back_recv,
):
    s = lax.axis_index("strip")
    v = lax.axis_index("vec")
    y_lo = s // 2 % 2

    barrier = pltpu.get_barrier_semaphore()

    def greet(j, carry):
        for where in ({"vec": lax.rem(v + j, NV)}, {"strip": lax.rem(s + j, NS)}):
            pl.semaphore_signal(barrier, inc=1, device_id=where, device_id_type=pl.DeviceIdType.MESH)
        return carry

    pot_in = pltpu.make_async_copy(pot_hbm, pot_ref, in_sem.at[0])
    x_in = pltpu.make_async_copy(x_hbm, x_ref, in_sem.at[1])
    pot_in.start()
    x_in.start()
    lax.fori_loop(1, NV, greet, 0)

    def splat(i):
        return jnp.full((8, 128), bounds_ref[i], jnp.int32).astype(F32) * grid_unit

    edges = [splat(i) for i in range(4)]
    center = (edges[0] + edges[1]) * 0.5
    spread = (edges[1] - edges[0]) * 0.5
    scale = 2.0 / spread

    pot_in.wait()
    for r in range(ROWS // 8):
        tiles = []
        for t in range(SUB):
            level = pot_ref[8 * r:8 * r + 8, 128 * t:128 * t + 128].astype(F32)
            tiles.append(disorder * (level / (POT_LEVELS - 1) - 0.5))
        for c, field in enumerate(to_classes(tiles)):
            pot_own[pl.ds(64 * r + place(c), 8, stride=8), :] = field
            diag_rows[pl.ds(OWN + 64 * r + place(c), 8, stride=8), :] = (field - center) * scale

    x_in.wait()

    def classes_of(q, carry):
        for r in range(ROWS // 8):
            tiles = [0.5 * x_ref[q, 8 * r:8 * r + 8, 128 * t:128 * t + 128] for t in range(SUB)]
            for c, tile in enumerate(to_classes(tiles)):
                start[q, pl.ds(OWN + 64 * r + place(c), 8, stride=8), :] = tile
        return carry

    classes_of(0, 0)

    pl.semaphore_wait(barrier, NV + NS - 2)

    up = lax.rem(s + NS - 1, NS)
    down = lax.rem(s + 1, NS)
    up2 = lax.rem(s + NS - 2, NS)

    def pot_copies():
        mine = diag_rows.at[pl.ds(OWN, OWN)]
        return (
            remote(mine, diag_rows.at[pl.ds(2 * OWN, OWN)], pot_send.at[0], pot_recv.at[0], strip=up),
            remote(mine, diag_rows.at[pl.ds(0, OWN)], pot_send.at[1], pot_recv.at[1], strip=down),
        )

    def ghost_copies(q):
        mine = start.at[q, pl.ds(OWN, OWN)]
        return (
            remote(mine, start.at[q, pl.ds(2 * OWN, OWN)], ghost_send.at[q, 0], ghost_recv.at[q, 0], strip=up),
            remote(mine, start.at[q, pl.ds(0, OWN)], ghost_send.at[q, 1], ghost_recv.at[q, 1], strip=down),
            remote(
                start.at[q, pl.ds(OWN, SUB)], start.at[q, pl.ds(3 * OWN, SUB)],
                ghost_send.at[q, 2], ghost_recv.at[q, 2], strip=up2,
            ),
        )

    def start_ghosts(q):
        for copy in ghost_copies(q):
            copy.start()

    for copy in pot_copies():
        copy.start()
    start_ghosts(0)
    lax.fori_loop(1, NQ, classes_of, 0)

    theta_lo = arccos((edges[2] - center) / spread)
    theta_hi = arccos((edges[3] - center) / spread)
    coef[0:8] = (theta_lo - theta_hi) / math.pi

    def coefficient(k, carry):
        order = jnp.full((8, 128), k, jnp.int32).astype(F32)
        coef[pl.ds(pl.multiple_of(8 * k, 8), 8)] = (
            2.0 * (jnp.sin(order * theta_lo) - jnp.sin(order * theta_hi)) / (order * math.pi)
        )
        return carry

    lax.fori_loop(1, DEGREE + 1, coefficient, 0)

    def pair_place(row):
        return (16 * row, 0) if row <= 48 else (16 * (96 - row), 1)

    for copy in pot_copies() + ghost_copies(0):
        copy.wait_send()
    start_ghosts(1)

    for copy in pot_copies():
        copy.wait_recv()
    for row in range(1, 3 * ROWS):
        value = diag_rows[8 * row:8 * row + 8]
        for base, half in {pair_place(row), (16 * (96 - row), 1) if row == 48 else pair_place(row)}:
            diag[pl.ds(base + half, 8, stride=2), :] = value

    sub = lax.broadcasted_iota(jnp.int32, (8, 128), 0)
    lane = lax.broadcasted_iota(jnp.int32, (8, 128), 1)
    index_left = jnp.where(sub >= 6, (lane + 127) % 128, lane)
    index_right = jnp.where(sub < 2, (lane + 1) % 128, lane)
    upper = (sub % 2 == 0)[None, None]

    def shift(value, index, by):
        index = jnp.broadcast_to(index[None], value.shape)
        return pltpu.roll(jnp.take_along_axis(value, index, axis=2), by, 1)

    def update(k, low, high):
        now, then = (even, odd) if k % 2 else (odd, even)
        rows = high - low
        top = min(high + 1, PAIRS)
        ext = now[(low - 1) * 16:top * 16].reshape(top - low + 1, 2, 8, 128)
        above = ext[0:rows]
        mid = ext[1:rows + 1]
        if high == PAIRS:
            crossing = ext[rows - 1:rows]
            crossing = jnp.where(upper, pltpu.roll(crossing, 7, 2), pltpu.roll(crossing, 1, 2))
            below = jnp.concatenate([ext[2:rows + 1], crossing], axis=0)
        else:
            below = ext[2:rows + 2]
        left = shift(mid[:, 1], index_left, 2)
        right = shift(mid[:, 0], index_right, 6)
        before = then[low * 16:high * 16].reshape(rows, 2, 8, 128) if k > 1 else None
        local = diag[low * 16:high * 16].reshape(rows, 2, 8, 128)
        halves = []
        for j, beside in enumerate((left + mid[:, 1], mid[:, 0] + right)):
            inside = local[:, j] * mid[:, j]
            if k == 2:
                inside = inside - (before[:, j] + before[:, j])
            elif k > 2:
                inside = inside - before[:, j]
            halves.append(inside - scale * ((above[:, j] + below[:, j]) + beside))
        after = jnp.stack(halves, axis=1)
        then[low * 16:high * 16] = after.reshape(rows * 16, 128)
        if k % 2 == 0 and high == PAIRS:
            first = max(ROWS, low)
            c_now = coef[8 * k - 8:8 * k]
            c_next = coef[8 * k:8 * k + 8]
            term = c_now * mid[first - low:] + c_next * after[first - low:]
            place_in = slice((first - ROWS) * 16, (PAIRS - ROWS) * 16)
            filt[place_in] = filt[place_in] + term.reshape((PAIRS - first) * 16, 128)

    def vec_peer(step):
        return lax.rem(v // 8 + step[0], 2) * 8 + lax.rem(v % 8 + step[1], 8)

    def send_vector(q, count):
        for step in VEC_STEPS:
            peer = vec_peer(step)
            remote(
                filtered.at[q, pl.ds(peer * CHUNKS, count)], slab.at[pl.ds((v * NQ + q) * HALO, count)],
                vec_send.at[q], vec_recv.at[q], vec=peer,
            ).start()

    def one_vector(q, carry):
        for copy in ghost_copies(q):
            copy.wait_recv()
        for row in range(3 * ROWS + 1):
            value = start[q, 8 * row:8 * row + 8]
            base, half = pair_place(row)
            even[pl.ds(base + half, 8, stride=2), :] = value
            if row == 48:
                even[pl.ds(base + 1, 8, stride=2), :] = value
        filt[...] = (
            (2.0 * coef[0:8]) * even[16 * ROWS:16 * PAIRS].reshape(2 * (PAIRS - ROWS), 8, 128)
        ).reshape(16 * (PAIRS - ROWS), 128)
        for k in range(1, DEGREE + 1):
            if k < ROWS - 1:
                update(k, k, ROWS)
                update(k, ROWS, PAIRS)
            else:
                update(k, k, PAIRS)
            if k == DEGREE // 2:
                @pl.when(q < NQ - 2)
                def _():
                    for copy in ghost_copies(q + 1):
                        copy.wait_send()
                    start_ghosts(q + 2)

        for row in range(ROWS + 1):
            base, half = pair_place(ROWS + row)
            filtered[q, 8 * row:8 * row + 8] = filt[pl.ds(base - 16 * ROWS + half, 8, stride=2), :]
        slab[pl.ds((v * NQ + q) * HALO, HALO)] = filtered[q, pl.ds(v * CHUNKS, HALO)]

        @pl.when(q < LAST)
        def _():
            send_vector(q, HALO)

        @pl.when(q == LAST)
        def _():
            send_vector(q, CHUNKS)

        return carry

    lax.fori_loop(0, NQ, one_vector, 0)
    for q in range(NQ):
        wait_bytes(slab.at[pl.ds(0, (NV - 1) * (CHUNKS if q == LAST else HALO))], vec_recv.at[q])

    def take(source, stride, g, n):
        base = 16 * g * stride + n
        return jnp.concatenate(
            [source[pl.ds(base, 8, stride=stride), :], source[pl.ds(base + 8 * stride, 8, stride=stride), :]], axis=0
        )

    def keep(target, g, n, value):
        for part, half in enumerate(split(value)):
            target[64 * part + 16 * g:64 * part + 16 * g + 16, 128 * n:128 * n + 128] = half

    def matrix_part(left):
        prod = lax.dot_general(left[...], ops_y[...], (((1,), (1,)), ((), ())), preferred_element_type=F32)
        return prod[0:64] + prod[64:128]

    def along_strip(stage, i, source, target):
        for a, b, c in STRIP_STEPS:
            peer = lax.rem(s // 4 + a, 4) * 4 + lax.rem(y_lo + b, 2) * 2 + lax.rem(s % 2 + c, 2)
            remote(source(peer), target, small_send.at[i, stage], small_recv.at[i, stage], strip=peer).start()

    def scatter(i, value):
        for c in range(NS):
            parts[i, c] = value[PART * c:PART * c + PART]
        scattered[i, s] = parts[i, s]
        along_strip(0, i, lambda peer: parts.at[i, peer], scattered.at[i, s])

    def exchange(i):
        wait_bytes(scattered.at[i, pl.ds(0, NS - 1)], small_recv.at[i, 0])
        summed[i, v] = jnp.sum(scattered[i], axis=0)
        for step in VEC_STEPS:
            remote(
                summed.at[i, v], summed.at[i, v], small_send.at[i, 1], small_recv.at[i, 1], vec=vec_peer(step)
            ).start()

    def gather(i):
        wait_bytes(summed.at[i, pl.ds(0, NV - 1)], small_recv.at[i, 1])
        total[i, s] = jnp.sum(summed[i], axis=0)
        along_strip(2, i, lambda peer: total.at[i, s], total.at[i, s])

    def finish(i):
        wait_bytes(total.at[i, pl.ds(0, NS - 1)], small_recv.at[i, 2])
        value = jnp.concatenate([total[i, c] for c in range(NS)], axis=0)
        return value + pltpu.roll(value, 64, 1)

    for g in range(NVEC // 16):
        for n in range(CHUNKS):
            keep(ops_y, g, n, take(slab, HALO, g, n))
    scatter(0, matrix_part(ops_y))

    def send_halos(j, carry):
        peer = lax.rem(v + j, NV)
        remote(
            filtered.at[LAST, pl.ds(peer * CHUNKS + CHUNKS, SUB)], halos.at[v], halo_send.at[0], halo_recv.at[0], vec=peer
        ).start()
        return carry

    lax.fori_loop(1, NV, send_halos, 0)
    halos[v] = filtered[LAST, pl.ds(v * CHUNKS + CHUNKS, SUB)]

    for g in range(NVEC // 16):
        for row in range(PIECE):
            tiles = from_classes([take(slab, HALO, g, SUB * row + place(c)) for c in range(SUB)])
            for t, tile in enumerate(tiles):
                keep(apply_ops, g, SUB * row + t, tile)
    exchange(0)

    wait_bytes(halos.at[pl.ds(0, NV - 1)], halo_recv.at[0])
    for peer in range(NV):
        base = (peer * NQ + LAST) * HALO + CHUNKS
        slab[base:base + SUB] = halos[peer]
    pot_slab = pot_own[pl.ds(v * CHUNKS, CHUNKS)] * 0.5
    for g in range(NVEC // 16):
        y = [take(slab, HALO, g, n) for n in range(HALO)]
        for row in range(PIECE):
            for c in range(SUB):
                n = SUB * row + place(c)
                if c < SUB - 1:
                    right = y[SUB * row + place(c + 1)]
                else:
                    right = pltpu.roll(y[SUB * row + place(0)], 127, 1)
                keep(ops_z, g, n, pot_slab[n:n + 1] * y[n] - (right + y[n + SUB]))
    scatter(1, matrix_part(ops_z))
    gather(0)
    exchange(1)

    rows64 = lax.broadcasted_iota(jnp.int32, (64, 128), 0)
    lanes64 = lax.broadcasted_iota(jnp.int32, (64, 128), 1)
    gram = finish(0)
    aug = jnp.where(lanes64 < 64, gram, jnp.where(lanes64 - 64 == rows64, 1.0, 0.0))
    aug_rows = [aug[8 * i:8 * i + 8] for i in range(8)]

    blocks = []
    for half, ortho in enumerate((ortho_first, ortho_second)):
        block = eliminate(aug_rows, range(4 * half, 4 * half + 4))
        blocks.append(block)
        high, low = split(math.sqrt(SITES) * block)
        left = jnp.concatenate(
            [jnp.concatenate([high, high], axis=1), jnp.concatenate([low, low], axis=1)], axis=0
        )
        product = jnp.dot(left, apply_ops[...], preferred_element_type=F32)
        flat = ortho.reshape(NVEC // 2 * CHUNKS, 128)
        for n in range(CHUNKS):
            value = product[0:32, 128 * n:128 * n + 128] + product[32:64, 128 * n:128 * n + 128]
            for g in range(4):
                flat[pl.ds(n + 8 * g * CHUNKS, 8, stride=CHUNKS), :] = value[8 * g:8 * g + 8]

        def send_back(j, carry, half=half, ortho=ortho):
            local = lax.rem(v + j, NV // 2)
            peer = local + half * (NV // 2)

            @pl.when(peer != v)
            def _():
                remote(
                    ortho.at[pl.ds(local * NQ, NQ)], fields.at[:, pl.ds(v * CHUNKS, CHUNKS)],
                    back_send.at[0], back_recv.at[0], vec=peer,
                ).start()

            @pl.when(peer == v)
            def _():
                fields[:, pl.ds(v * CHUNKS, CHUNKS)] = ortho[pl.ds(local * NQ, NQ)]

            return carry

        lax.fori_loop(0, NV // 2, send_back, 0)
    inverse = jnp.concatenate(blocks, axis=0)

    gather(1)
    cross = finish(1)[:, 0:64]
    cross = cross + cross.T
    half = jnp.dot(inverse, cross, precision=lax.Precision.HIGHEST, preferred_element_type=F32)
    ritz_ref[...] = float(ROWS) * lax.dot_general(
        inverse, half, (((1,), (1,)), ((), ())), precision=lax.Precision.HIGHEST, preferred_element_type=F32
    )

    wait_bytes(slab.at[pl.ds(0, (NV - 1) * NQ * CHUNKS)], back_recv.at[0])
    wait_bytes(slab.at[pl.ds(0, (NV - 1) * NQ * CHUNKS)], back_send.at[0])
    for i in range(2):
        for stage in range(3):
            wait_bytes(total.at[i, pl.ds(0, NS - 1)], small_send.at[i, stage])
    wait_bytes(halos.at[pl.ds(0, NV - 1)], halo_send.at[0])
    for q in range(NQ):
        wait_bytes(slab.at[pl.ds(0, (NV - 1) * (CHUNKS if q == LAST else HALO))], vec_send.at[q])
    for copy in ghost_copies(NQ - 1):
        copy.wait_send()


def arrange(fields, ritz, out_ref, ritz_ref):
    for q in range(NQ):
        for r in range(ROWS // 8):
            for t in range(SUB):
                out_ref[q, 8 * r:8 * r + 8, 128 * t:128 * t + 128] = fields[q, pl.ds(64 * r + t, 8, stride=8), :]
    ritz_ref[...] = ritz[...]


def shards(start_vectors, potential, bounds):
    vmem = pl.BlockSpec(memory_space=pltpu.VMEM)
    hbm = pl.BlockSpec(memory_space=pltpu.HBM)
    dma = pltpu.SemaphoreType.DMA
    ritz_shape = jax.ShapeDtypeStruct((NVEC, NVEC), F32)
    fields, ritz = pl.pallas_call(
        kernel,
        out_shape=(pltpu.VMEM((NQ, OWN, 128), F32), pltpu.VMEM((NVEC, NVEC), F32)),
        in_specs=[pl.BlockSpec(memory_space=pltpu.SMEM), hbm, hbm],
        out_specs=(vmem, vmem),
        scratch_shapes=[
            pltpu.VMEM((NQ, ROWS, 1024), F32),
            pltpu.VMEM((ROWS, 1024), jnp.int32),
            pltpu.VMEM((8 * (DEGREE + 1), 128), F32),
            pltpu.VMEM((NQ, FIELD, 128), F32),
            pltpu.VMEM((16 * PAIRS, 128), F32),
            pltpu.VMEM((16 * PAIRS, 128), F32),
            pltpu.VMEM((16 * (PAIRS - ROWS), 128), F32),
            pltpu.VMEM((NQ, OWN + SUB, 128), F32),
            pltpu.VMEM((FIELD, 128), F32),
            pltpu.VMEM((16 * PAIRS, 128), F32),
            pltpu.VMEM((OWN, 128), F32),
            pltpu.VMEM((NVEC * HALO, 128), F32),
            pltpu.VMEM((NV, SUB, 128), F32),
            pltpu.VMEM((128, CHUNKS * 128), BF16),
            pltpu.VMEM((128, CHUNKS * 128), BF16),
            pltpu.VMEM((128, CHUNKS * 128), BF16),
            pltpu.VMEM((2, NS, PART, 128), F32),
            pltpu.VMEM((2, NS, PART, 128), F32),
            pltpu.VMEM((2, NV, PART, 128), F32),
            pltpu.VMEM((2, NS, PART, 128), F32),
            pltpu.VMEM((NVEC // 2, CHUNKS, 128), F32),
            pltpu.VMEM((NVEC // 2, CHUNKS, 128), F32),
            dma((2,)), dma((2,)), dma((2,)), dma((NQ, 3)), dma((NQ, 3)), dma((NQ,)), dma((NQ,)), dma((1,)), dma((1,)),
            dma((2, 3)), dma((2, 3)), dma((1,)), dma((1,)),
        ],
        compiler_params=pltpu.CompilerParams(
            collective_id=0, has_side_effects=True, vmem_limit_bytes=60 << 20
        ),
        name="filter_ritz",
    )(bounds, start_vectors, potential)
    return pl.pallas_call(
        arrange,
        out_shape=(jax.ShapeDtypeStruct((NQ, ROWS, 1024), F32), ritz_shape),
        in_specs=[vmem, vmem],
        out_specs=(vmem, vmem),
        name="arrange",
    )(pltpu.with_memory_space_constraint(fields, pltpu.VMEM), pltpu.with_memory_space_constraint(ritz, pltpu.VMEM))


def solution(mesh):
    in_specs = (P("vec", "strip", None), P("strip", None), P())
    out_specs = (P("vec", "strip", None), P())
    return jax.shard_map(shards, mesh=mesh, in_specs=in_specs, out_specs=out_specs, check_vma=False)
```
